32 devices in a mesh: group: 4 (over x, core), batch: 8 (over z, y).
Axes of the slice: x: 2, y: 2, z: 4, core: 2. Of those that a mesh axis runs over, the one named last changes fastest.
Arguments:
- panel_alleles: int32 [32, 131072], P('group', 'batch'), may hold values 0 or 1
- recomb_rates: float32 [32], P('group'), may hold values from 0.001 to 0.3
- genotypes: int32 [2, 32], P(None, 'group'), may hold values from 0 to 2, as said below
Outputs:
- dosage: float32 [2, 32], P(None, 'group')
- log_likelihood: float32 [2], replicated
The draws below stay inside these ranges and needn't reach their ends.
Inputs may be any that keep to these rules, and one draw needn't show every extreme that they name: `genotypes`: 2 marks a marker at which the target's allele is missing; 0 and 1 are observed alleles.
All inputs are finite; a program needn't handle non-finite values. No bound on the sum of `panel_alleles` on one device may be relied on, other than what follows from the above.
Results may differ from the reference program's by a relative error of at most 0.0003.
Values sent between devices are 32-bit elements; how exact they have to be, the bound alone decides.
No kernel may reach another device: no remote copies, remote signals or barrier semaphores. Data moves between devices by JAX's collectives and lax.ppermute only.
A program may use at most 64 MiB of HBM per device.

```python
import math
import jax
import jax.numpy as jnp
from jax import lax

K = 131072
MD = 8
H = 2
M = 32
N_GROUP = 4


def draw_genotypes(key, part):
    key_allele = jax.random.fold_in(key, 11)
    key_missing = jax.random.fold_in(key, 23)
    allele = jax.random.randint(key_allele, (H, M), 0, 2, dtype=jnp.int32)
    roll = jax.random.randint(key_missing, (H, M), 0, 4 * M, dtype=jnp.int32)
    position = jnp.arange(M, dtype=jnp.int32)[None, :]
    return jnp.where(roll < M + 2 * position, allele, 2).astype(jnp.int32)


def plant(array, own_key, least, top_value):
    place = [jax.random.randint(jax.random.fold_in(own_key, axis), (), 0, length) for axis, length in enumerate(array.shape)]
    widest = array.shape.index(max(array.shape))
    beside = place[:widest] + [(place[widest] + 1) % array.shape[widest]] + place[widest + 1:]
    return array.at[tuple(place)].set(least).at[tuple(beside)].set(top_value)


def block_scale(own_key, shape, shards, low, top_value):
    level = 1.0
    for axis_at, blocks in shards:
        steps = jax.random.uniform(jax.random.fold_in(jax.random.fold_in(own_key, 6), axis_at), (blocks,), jnp.float32, low / len(shards), top_value / len(shards))
        level = level * jnp.repeat(jnp.exp(steps), shape[axis_at] // blocks).reshape((-1,) + (1,) * (len(shape) - 1 - axis_at))
    return level


def setup_inputs(seed: int = 0) -> dict:
    arg_keys = jax.random.split(jax.random.key(seed), 4)
    return {
        "panel_alleles": plant((jax.random.randint(arg_keys[0], (M, K), 0, 2) < 1).astype(jnp.int32), jax.random.fold_in(arg_keys[0], 1), 0, 1),
        "recomb_rates": jnp.clip(jnp.exp(math.log(0.3) - 5.7037825 * jax.random.uniform(arg_keys[1], (M,), jnp.float32) ** block_scale(arg_keys[1], (M,), ((0, 4),), -0.2, 0.2)), 0.001, 0.3),
        "genotypes": draw_genotypes(jax.random.fold_in(arg_keys[3], 71), 0),
    }


MISMATCH = 0.05


def emission(panel_rows, geno_cols):
    observed = geno_cols.T[:, :, None]
    agrees = jnp.where(panel_rows[:, None, :] == observed, 1.0 - MISMATCH, MISMATCH)
    return jnp.where(observed == 2, 1.0, agrees).astype(jnp.float32)


def forward_marker(scaled, emitted, switch):
    unscaled = emitted * ((1.0 - switch) * scaled + switch / K)
    totals = jnp.sum(unscaled, axis=1, keepdims=True)
    return unscaled / totals, totals[:, 0]


def backward_marker(scaled, emitted, switch):
    weighted = emitted * scaled
    spread = (1.0 - switch) * weighted + switch / K * jnp.sum(weighted, axis=1, keepdims=True)
    return spread / jnp.sum(spread, axis=1, keepdims=True)


def reference(panel_alleles, recomb_rates, genotypes):
    panel_blocks = panel_alleles.reshape(N_GROUP, MD, K)
    geno_blocks = genotypes.reshape(H, N_GROUP, MD).transpose(1, 0, 2)
    rate_blocks = recomb_rates.reshape(N_GROUP, MD)
    uniform = jnp.full((H, K), 1.0 / K, jnp.float32)

    def forward_stretch(carried, inputs):
        alphas, log_total = carried
        emitted = emission(inputs[0], inputs[1])

        def marker_step(status, pieces):
            scaled, totals = forward_marker(status[0], pieces[0], pieces[1])
            return (scaled, status[1] + jnp.log(totals)), None

        (alpha_out, log_total), unused = lax.scan(marker_step, (alphas, log_total), (emitted, inputs[2]))
        return (alpha_out, log_total), alphas

    (alpha_last, log_total), alpha_starts = lax.scan(
        forward_stretch, (uniform, jnp.zeros((H,), jnp.float32)), (panel_blocks, geno_blocks, rate_blocks))

    def backward_stretch(betas, inputs):
        emitted = emission(inputs[0], inputs[1])

        def marker_step(scaled, pieces):
            return backward_marker(scaled, pieces[0], pieces[1]), None

        beta_out, unused = lax.scan(marker_step, betas, (emitted, inputs[2]), reverse=True)
        return beta_out, betas

    beta_first, beta_ends = lax.scan(backward_stretch, uniform, (panel_blocks, geno_blocks, rate_blocks), reverse=True)

    def stretch_dosage(inputs):
        alphas, betas, panel_rows, geno_cols, switches = inputs
        emitted = emission(panel_rows, geno_cols)

        def forward_step(scaled, pieces):
            nextrow, totals = forward_marker(scaled, pieces[0], pieces[1])
            return nextrow, nextrow

        def backward_step(scaled, pieces):
            return backward_marker(scaled, pieces[0], pieces[1]), scaled

        unused_f, forward_rows = lax.scan(forward_step, alphas, (emitted, switches))
        unused_b, backward_rows = lax.scan(backward_step, betas, (emitted, switches), reverse=True)
        product = forward_rows * backward_rows
        numerator = jnp.sum(jnp.where(panel_rows[:, None, :] == 1, product, 0.0), axis=2)
        return numerator / jnp.sum(product, axis=2)

    dosage = lax.map(stretch_dosage, (alpha_starts, beta_ends, panel_blocks, geno_blocks, rate_blocks))
    dosage = dosage.transpose(2, 0, 1).reshape(H, N_GROUP * MD)
    return dosage, log_total / (N_GROUP * MD)
```

```python
import functools
import math

import jax
import jax.numpy as jnp
from jax import lax
from jax.experimental import pallas as pl
from jax.experimental.pallas import tpu as pltpu
from jax.sharding import PartitionSpec as P

MISMATCH = 0.05
HIGHEST = lax.Precision.HIGHEST


def haplotypes(panel_rows):
    return panel_rows.shape[1] * lax.axis_size("batch")


def from_behind(x, axis, by):
    peers = lax.axis_size(axis)
    pairs = [(i, i + by) for i in range(peers) if 0 <= i + by < peers]
    return lax.ppermute(x, axis, pairs)


def emission(panel_rows, geno_col):
    observed = geno_col[:, None]
    agrees = jnp.where(panel_rows == observed, 1.0 - MISMATCH, MISMATCH)
    return jnp.where(observed == 2, 1.0, agrees).astype(jnp.float32)


def forward_terms(panel_rows, geno_col, switches):
    emitted = emission(panel_rows, geno_col)
    retain = emitted * (1.0 - switches)[:, None]
    inject = emitted * (switches / haplotypes(panel_rows))[:, None]
    return (retain, inject, None)


def backward_terms(panel_rows, geno_col, switches):
    emitted = emission(panel_rows, geno_col)[::-1]
    flipped = switches[::-1]
    retain = emitted * (1.0 - flipped)[:, None]
    inject = jnp.broadcast_to((flipped / haplotypes(panel_rows))[:, None], emitted.shape)
    return (retain, inject, emitted)


def partial_sums(entering, retain, inject, weight, extent):
    logs = jnp.cumsum(jnp.log(retain), axis=0)
    shifted = jnp.concatenate([jnp.zeros_like(entering)[None], logs[: extent - 1]], axis=0)
    before = jnp.exp(shifted)
    left_side = before if weight is None else weight * before
    leading = jnp.einsum("jk,k->j", left_side, entering, precision=HIGHEST)
    anchor = shifted[0]
    right_side = inject * jnp.exp(anchor[None] - logs)
    nearby = jnp.exp(jnp.minimum(shifted - anchor[None], 0.0))
    nearby = nearby if weight is None else weight * nearby
    columns = [jnp.einsum("jk,tk->jt", nearby, right_side, precision=HIGHEST)]
    coupling = jnp.concatenate(columns, axis=1)
    return (leading, coupling)


def solve_sums(leading, coupling):
    columns = coupling.shape[1]

    def settle(marker, sigmas):
        below = jnp.arange(columns) < marker
        update = leading[marker] + jnp.sum(
            jnp.where(below, coupling[marker] * sigmas[:columns], 0.0)
        )
        return sigmas.at[marker].set(update)

    return lax.fori_loop(0, leading.shape[0], settle, jnp.zeros_like(leading))


def advance(entering, retain, inject, sigmas, keep_states):

    def advance_single(current, pieces):
        current = pieces[0] * current + pieces[1] * pieces[2]
        return (current, current if keep_states else None)

    return lax.scan(advance_single, entering, (retain, inject, sigmas[: retain.shape[0]]))


def place_rows(store, block, active):
    return jnp.where(active, block, store)


def on_device_chain(panel_alleles, recomb_rates, genotypes):
    chain_size = lax.axis_size("group")
    position = lax.axis_index("group")
    markers, width = panel_alleles.shape
    targets = genotypes.shape[0]
    bundles = targets // targets
    uniform = jnp.full((targets, width), 1.0 / haplotypes(panel_alleles), jnp.float32)
    first_row = position == 0
    last_row = position == chain_size - 1

    def local_sums(active, arrivals, geno_rows, maker, extent):

        def local_compute():

            def local_single(pieces):
                retain, inject, weight = maker(panel_alleles, pieces[1], recomb_rates)
                return partial_sums(pieces[0], retain, inject, weight, extent)

            return lax.map(local_single, (arrivals, geno_rows))

        def local_skipped():
            return (
                jnp.zeros((targets, extent), jnp.float32),
                jnp.zeros((targets, extent, markers), jnp.float32),
            )

        return lax.cond(active, local_compute, local_skipped)

    def outgoing(active, arrivals, geno_rows, sigmas, maker, scale_row):

        def outgoing_compute():

            def outgoing_single(pieces):
                retain, inject, weight = maker(panel_alleles, pieces[1], recomb_rates)
                ending, unused = advance(pieces[0], retain, inject, pieces[2], False)
                return ending / pieces[2][scale_row]

            return lax.map(outgoing_single, (arrivals, geno_rows, sigmas))

        def outgoing_skipped():
            return jnp.zeros((targets, width), jnp.float32)

        return lax.cond(active, outgoing_compute, outgoing_skipped)

    def moment_step(moment, carried_state):
        (
            sent_forward,
            sent_backward,
            sent_running,
            store_forward,
            store_backward,
            sigma_forward,
            sigma_backward,
            log_terms,
        ) = carried_state
        got_forward = from_behind(sent_forward, "group", 1)
        got_backward = from_behind(sent_backward, "group", -1)
        entering_forward = jnp.where(first_row, uniform, got_forward)
        entering_backward = jnp.where(last_row, uniform, got_backward)
        index_forward = moment - position
        index_backward = moment - (chain_size - 1 - position)
        active_forward = (index_forward >= 0) & (index_forward < bundles)
        active_backward = (index_backward >= 0) & (index_backward < bundles)
        lead_forward, couple_forward = local_sums(
            active_forward, entering_forward, genotypes, forward_terms, markers + 1
        )
        lead_backward, couple_backward = local_sums(
            active_backward, entering_backward, genotypes, backward_terms, markers
        )
        lead_forward, couple_forward, lead_backward, couple_backward = lax.psum(
            (lead_forward, couple_forward, lead_backward, couple_backward), "batch"
        )
        sigmas_forward = jax.vmap(solve_sums)(lead_forward, couple_forward)
        sigmas_backward = jax.vmap(solve_sums)(lead_backward, couple_backward)
        next_forward = outgoing(
            active_forward, entering_forward, genotypes, sigmas_forward, forward_terms, markers
        )
        next_backward = outgoing(
            active_backward,
            entering_backward,
            genotypes,
            sigmas_backward,
            backward_terms,
            markers - 1,
        )
        guarded = jnp.where(active_forward, sigmas_forward[:, markers], 1.0)
        running = jnp.log(guarded)
        store_forward = place_rows(store_forward, entering_forward, active_forward)
        store_backward = place_rows(store_backward, entering_backward, active_backward)
        sigma_forward = place_rows(sigma_forward, sigmas_forward, active_forward)
        sigma_backward = place_rows(sigma_backward, sigmas_backward, active_backward)
        log_terms = place_rows(log_terms, running, active_forward)
        return (
            next_forward,
            next_backward,
            running,
            store_forward,
            store_backward,
            sigma_forward,
            sigma_backward,
            log_terms,
        )

    initial = (
        jnp.zeros((targets, width), jnp.float32),
        jnp.zeros((targets, width), jnp.float32),
        jnp.zeros((targets,), jnp.float32),
        jnp.zeros((targets, width), jnp.float32),
        jnp.zeros((targets, width), jnp.float32),
        jnp.zeros((targets, markers + 1), jnp.float32),
        jnp.zeros((targets, markers), jnp.float32),
        jnp.zeros((targets,), jnp.float32),
    )
    final_state = lax.fori_loop(0, chain_size + bundles - 1, moment_step, initial)
    store_forward, store_backward, sigma_forward, sigma_backward, log_terms = final_state[3:]
    whole_log = lax.psum(log_terms, "group")
    log_likelihood = whole_log / (markers * chain_size)

    def posterior(pieces):
        entering_ahead, entering_behind, geno_col, sigmas_ahead, sigmas_behind = pieces
        retain, inject, weight = forward_terms(panel_alleles, geno_col, recomb_rates)
        unused_f, forward_states = advance(entering_ahead, retain, inject, sigmas_ahead, True)
        forward_rows = forward_states / sigmas_ahead[1:, None]
        retain, inject, weight = backward_terms(panel_alleles, geno_col, recomb_rates)
        unused_b, backward_states = advance(entering_behind, retain, inject, sigmas_behind, True)
        scaled_back = backward_states[:-1] / sigmas_behind[:-1, None]
        backward_rows = jnp.concatenate([entering_behind[None], scaled_back], axis=0)[::-1]
        product = forward_rows * backward_rows
        numerator = jnp.sum(jnp.where(panel_alleles == 1, product, 0.0), axis=1)
        return (numerator, jnp.sum(product, axis=1))

    numerator, denominator = lax.map(
        posterior, (store_forward, store_backward, genotypes, sigma_forward, sigma_backward)
    )
    numerator, denominator = lax.psum((numerator, denominator), "batch")
    return (numerator / denominator, log_likelihood)


ROWS, LANES = 8, 128
HALF = LANES // 2
GROUPS = 4
MISSING = 2
SCALE = math.sqrt(MISMATCH * (1.0 - MISMATCH))
HALF_STEP = 0.5 * math.log((1.0 - MISMATCH) / MISMATCH)
VMEM = pl.BlockSpec(memory_space=pltpu.VMEM)
SMEM = pl.BlockSpec(memory_space=pltpu.SMEM)
F32, BF16 = jnp.float32, jnp.bfloat16


def iota(shape, axis):
    return lax.broadcasted_iota(jnp.int32, shape, axis)


def pack_kernel(geno_ref, panel_ref, *out_refs):
    place = lax.axis_index("group")
    chunk = panel_ref.shape[1] // GROUPS
    row, lane = iota((ROWS, LANES), 0), iota((ROWS, LANES), 1)
    tile = jnp.zeros((ROWS, LANES), jnp.int32)
    for i in range(ROWS):
        both = jnp.where(lane < HALF, geno_ref[0, i], geno_ref[1, i])
        tile = jnp.where(row == i, both, tile)
    for d in range(GROUPS):
        start = pl.multiple_of((place ^ d) * chunk, LANES)
        out_refs[d][:, :chunk] = panel_ref[:, pl.ds(start, chunk)]
        out_refs[d][:, chunk:] = tile


def window_kernel(step, rate_ref, *refs):
    pieces, (t_ref, em_ref, panel, genos, wide, left) = refs[:GROUPS], refs[GROUPS:]
    place = lax.axis_index("group")
    columns = panel.shape[1]
    markers = ROWS * GROUPS
    for d in range(GROUPS):
        rows = pl.ds(pl.multiple_of((place ^ d) * ROWS, ROWS), ROWS)
        panel[rows, :] = pieces[d][:, :columns]
        genos[rows, :] = pieces[d][:, columns:]

    r, j = iota((4 * markers, 2 * markers), 0), iota((4 * markers, 2 * markers), 1)
    same = r // (2 * markers) == j // markers
    prefix, marker = (r // markers) % 2 == 0, r % markers
    at = j % markers
    sums = jnp.where(prefix, jnp.where(at <= marker, 1.0, 0.0), jnp.where(at < marker, -1.0, 0.0))
    sums = jnp.where(same, sums, 0.0).astype(BF16)

    def fill(c, carry):
        here = pl.ds(pl.multiple_of(c * step, LANES), step)
        signs = []
        for h in range(2):
            for b in range(GROUPS):
                rows = slice(b * ROWS, (b + 1) * ROWS)
                seen = genos[rows, h * HALF : h * HALF + 1]
                agrees = jnp.where(panel[rows, here] == seen, 1.0, -1.0)
                signs.append(jnp.where(seen == MISSING, 0.0, agrees))
        signs = jnp.concatenate(signs, axis=0).astype(BF16)
        power = jnp.dot(sums, signs, preferred_element_type=F32)
        value = jnp.exp(power * HALF_STEP)
        upper = value.astype(BF16).astype(F32)
        lower = value - upper
        blocks = {}
        for h in range(2):
            for kind in range(2):
                for b in range(GROUPS):
                    at = h * 2 * markers + kind * markers + b * ROWS
                    both = jnp.concatenate([upper[at : at + ROWS], lower[at : at + ROWS]], axis=0).astype(BF16)
                    blocks[kind, h, b] = both
                    wide[kind, (h * GROUPS + b) * 2 * ROWS : (h * GROUPS + b + 1) * 2 * ROWS, here] = both
        slot = 0
        for half, h, t, b in LEFT:
            carries = jnp.broadcast_to(panel[t : t + 1, here], (2 * ROWS, step)).astype(F32).astype(BF16)
            left[slot * 2 * ROWS : (slot + 1) * 2 * ROWS, here] = blocks[1 - half, h, b] * carries
            slot += 1
        return carry

    lax.fori_loop(0, columns // step, fill, 0)

    def product(a, b):
        return lax.dot_general(a, b, (((1,), (1,)), ((), ())), preferred_element_type=F32)

    middle = len(LEFT) * ROWS
    sums_t = [product(left[:middle, :], wide[0]), product(left[middle:, :], wide[1])]
    sums_e = [product(wide[1], wide[0]), product(wide[0], wide[1])]
    lane = iota((ROWS, LANES), 1)
    first = lane % (2 * ROWS) < ROWS

    def rows_of(acc, slot):
        return acc[slot * 2 * ROWS : slot * 2 * ROWS + ROWS] + acc[slot * 2 * ROWS + ROWS : (slot + 1) * 2 * ROWS]

    def fold(a, b):
        a = a + pltpu.roll(a, LANES - ROWS, 1)
        b = 0.0 if b is None else b + pltpu.roll(b, ROWS, 1)
        return jnp.where(first, a, b)

    def both_targets(acc, slots):
        return jnp.where(lane < HALF, rows_of(acc, slots[0]), rows_of(acc, slots[1]))

    for t in range(markers):
        half = t // (markers // 2)
        tiles = [both_targets(sums_t[half], [LEFT_AT[half, h, t, b] for h in range(2)]) for b in left_blocks(t)]
        tiles = tiles + [None] * (2 - len(tiles))
        t_ref[t // ROWS, (t % ROWS) * ROWS : (t % ROWS + 1) * ROWS, :] = fold(*tiles)
    for kind in range(2):
        tiles = [both_targets(sums_e[kind], [b, GROUPS + b]) for b in range(GROUPS)]
        for q in range(GROUPS // 2):
            at = (kind * GROUPS // 2 + q) * ROWS
            em_ref[at : at + ROWS, :] = fold(tiles[2 * q], tiles[2 * q + 1])
    row = iota((ROWS, LANES), 0)
    rates = jnp.zeros((ROWS, LANES), F32)
    for i in range(ROWS):
        rates = jnp.where(row == i, rate_ref[i], rates)
    own = pl.ds(pl.multiple_of(place * ROWS, ROWS), ROWS)
    inner = lane % (LANES // GROUPS)
    known = jnp.where(genos[own, :] == MISSING, 0.0, 1.0)
    known0 = jnp.broadcast_to(known[:, 0:1], (ROWS, LANES))
    known1 = jnp.broadcast_to(known[:, HALF : HALF + 1], (ROWS, LANES))
    misc = jnp.where(inner < 2 * ROWS, rates, jnp.where(inner < 3 * ROWS, known0, known1))
    em_ref[GROUPS * ROWS :, :] = jnp.where(lane // (LANES // GROUPS) == place, misc, 0.0)


def left_blocks(t):
    b = t // ROWS
    return list(range(b + 1)) if b < GROUPS // 2 else list(range(GROUPS - 1, b - 1, -1))


LEFT = [
    (half, h, t, b)
    for half in range(2)
    for t in range(half * ROWS * GROUPS // 2, (half + 1) * ROWS * GROUPS // 2)
    for b in left_blocks(t)
    for h in range(2)
]
LEFT_AT = {entry: slot % (len(LEFT) // 2) for slot, entry in enumerate(LEFT)}


def finish_kernel(panel_size, copies, t_ref, em_ref, dose_ref, log_ref):
    place = lax.axis_index("group")
    markers = ROWS * GROUPS
    row, lane = iota((ROWS, LANES), 0), iota((ROWS, LANES), 1)
    target = lane // HALF
    folded = (lane % (2 * ROWS)) // ROWS
    misc = em_ref[GROUPS * ROWS :, :] * (1.0 / copies)
    wide = LANES // GROUPS

    def spread(tile, at):
        return jnp.broadcast_to(tile[:, at : at + 1], (ROWS, LANES))

    rates = [spread(misc, b * wide) for b in range(GROUPS)]
    odds = [rate / (1.0 - rate) for rate in rates]
    inverse = 1.0 / panel_size
    ahead = []
    for b in range(GROUPS):
        following = odds[b + 1][0:1, :] if b + 1 < GROUPS else jnp.ones((1, LANES), F32)
        ahead.append(jnp.concatenate([odds[b][1:, :], following], axis=0) * inverse)
    behind = [odd * inverse for odd in odds]

    def scaled(base, factors):
        tiles = []
        for q in range(GROUPS // 2):
            tile = em_ref[base + q * ROWS : base + (q + 1) * ROWS, :]
            tiles.append(tile * jnp.where(folded == 0, factors[2 * q], factors[2 * q + 1]))
        return tiles

    lead_tiles = scaled(GROUPS // 2 * ROWS, ahead)
    trail_tiles = scaled(0, behind)

    def column(tiles, t, b):
        at = 2 * ROWS * (t // ROWS) + t % ROWS + ROWS * (b % 2)
        tile = tiles[b // 2]
        return jnp.where(target == 0, spread(tile, at), spread(tile, HALF + at))

    lead = [jnp.zeros((ROWS, LANES), F32)] * GROUPS
    trail = [jnp.zeros((ROWS, LANES), F32)] * GROUPS
    starts = [jnp.zeros((ROWS, LANES), F32)] * GROUPS
    ends = [jnp.zeros((ROWS, LANES), F32)] * GROUPS
    v = jnp.ones((ROWS, LANES), F32)
    z = jnp.ones((ROWS, LANES), F32)
    for step in range(markers):
        t, u = step, markers - 1 - step
        bt, bu = t // ROWS, u // ROWS
        starts[bt] = jnp.where(row == t % ROWS, v, starts[bt])
        ends[bu] = jnp.where(row == u % ROWS, z, ends[bu])
        for b in range(bt, GROUPS):
            lead[b] = lead[b] + v * column(lead_tiles, t, b)
        for b in range(bu + 1):
            trail[b] = trail[b] + z * column(trail_tiles, u, b)
        v = jnp.broadcast_to(lead[bt][t % ROWS : t % ROWS + 1, :], (ROWS, LANES))
        z = jnp.broadcast_to(trail[bu][u % ROWS : u % ROWS + 1, :], (ROWS, LANES))
    total = v

    low = place < GROUPS // 2
    inner = lane % HALF
    outer = [jnp.where(low, starts[b], ends[GROUPS - 1 - b]) for b in range(2)]
    outer = jnp.where(folded == 0, outer[0], outer[1])
    across = [jnp.where(low, ends[b], starts[b]) for b in range(GROUPS)]
    picked = across[GROUPS - 1]
    for b in range(GROUPS - 1):
        picked = jnp.where(inner // (2 * ROWS) == b, across[b], picked)
    picked = jnp.where(row == lane % ROWS, picked, 0.0)
    across = jnp.sum(picked, axis=0, keepdims=True)
    weight = outer * across
    block = jnp.where(low, folded, GROUPS - 1 - folded)
    side = jnp.where(low, 1, -1)
    near = block * ROWS + row
    far = ROWS * (inner // (2 * ROWS)) + lane % ROWS
    parts = []
    for i in range(ROWS):
        t = place * ROWS + i
        inside = ((near - t) * side <= 0) & ((far - t) * side >= 0)
        tile = jnp.where(inside, t_ref[i * ROWS : (i + 1) * ROWS, :] * weight, 0.0)
        parts.append(jnp.sum(tile, axis=0, keepdims=True))
    parts = jnp.concatenate(parts, axis=0) * (inverse / total)
    doses, logs = [], []
    counts = jnp.sum(misc, axis=0, keepdims=True)
    stay = [jnp.log(1.0 - rate) for rate in rates]
    stay[0] = jnp.where(row == 0, 0.0, stay[0])
    stay = jnp.sum(sum(stay), axis=0, keepdims=True)
    for h in range(2):
        dose = jnp.sum(jnp.where(target == h, parts, 0.0), axis=1, keepdims=True)
        doses.append(jnp.sum(jnp.where(row == lane, dose, 0.0), axis=0, keepdims=True))
        seen = sum(counts[:, b * wide + (2 + h) * ROWS : b * wide + (2 + h) * ROWS + 1] for b in range(GROUPS))
        whole = jnp.log(total[0:1, h * HALF : h * HALF + 1]) + stay[:, 0:1] + seen * math.log(SCALE)
        logs.append(whole * (1.0 / markers))
    dose_ref[...] = jnp.concatenate(doses, axis=0)[:, :ROWS]
    log_ref[...] = jnp.concatenate(logs, axis=0)


def exchange(x, axis, by):
    peers = lax.axis_size(axis)
    return lax.ppermute(x, axis, [(i, i ^ by) for i in range(peers)])


def on_device_windows(panel_alleles, recomb_rates, genotypes):
    width = panel_alleles.shape[1]
    copies = lax.axis_size("batch")
    chunk = width // GROUPS
    markers = ROWS * GROUPS
    cut = jax.ShapeDtypeStruct((ROWS, chunk + LANES), jnp.int32)
    pieces = pl.pallas_call(
        pack_kernel, out_shape=[cut] * GROUPS, in_specs=[SMEM, VMEM], out_specs=[VMEM] * GROUPS, name="pack"
    )(genotypes, panel_alleles)
    pieces = [pieces[0]] + [exchange(pieces[d], "group", d) for d in range(1, GROUPS)]
    extra = (GROUPS + 1) * ROWS
    sums_t, sums_e = pl.pallas_call(
        functools.partial(window_kernel, min(512, chunk)),
        out_shape=[
            jax.ShapeDtypeStruct((GROUPS, ROWS * ROWS, LANES), F32),
            jax.ShapeDtypeStruct((extra, LANES), F32),
        ],
        in_specs=[SMEM] + [VMEM] * GROUPS,
        out_specs=[VMEM] * 2,
        scratch_shapes=[
            pltpu.VMEM((markers, chunk), jnp.int32),
            pltpu.VMEM((markers, LANES), jnp.int32),
            pltpu.VMEM((2, 4 * markers, chunk), BF16),
            pltpu.VMEM((len(LEFT) * 2 * ROWS, chunk), BF16),
        ],
        compiler_params=pltpu.CompilerParams(vmem_limit_bytes=48 * 1024 * 1024),
        name="windows",
    )(recomb_rates, *pieces)
    place = lax.axis_index("group")
    tall = ROWS * ROWS

    def block(index):
        return lax.dynamic_index_in_dim(sums_t, index, 0, False)

    kept = jnp.concatenate([block(place), sums_e, block(place ^ 2)], axis=0)
    sent = jnp.concatenate([block(place ^ 1), sums_e, block(place ^ 3)], axis=0)
    kept = kept + exchange(sent, "group", 1)
    got = exchange(kept[tall:], "group", 2)
    kept = kept[: tall + extra] + jnp.concatenate([got[extra:], got[:extra]], axis=0)
    by = 1
    while by < copies:
        kept = kept + exchange(kept, "batch", by)
        by *= 2
    dosage, logs = pl.pallas_call(
        functools.partial(finish_kernel, float(width * copies), float(copies)),
        out_shape=[jax.ShapeDtypeStruct((2, ROWS), F32), jax.ShapeDtypeStruct((2, 1), F32)],
        in_specs=[VMEM] * 2,
        out_specs=[VMEM] * 2,
        name="finish",
    )(kept[:tall], kept[tall:])
    return dosage, logs.reshape(2)


def fits_windows(panel_alleles, genotypes, groups, copies):
    markers, width = panel_alleles.shape
    return (
        groups == GROUPS
        and copies & (copies - 1) == 0
        and markers == ROWS
        and genotypes.shape[0] == 2
        and width % (GROUPS * LANES * 4) == 0
    )


def on_device(panel_alleles, recomb_rates, genotypes):
    groups, copies = lax.axis_size("group"), lax.axis_size("batch")
    if fits_windows(panel_alleles, genotypes, groups, copies):
        return on_device_windows(panel_alleles, recomb_rates, genotypes)
    return on_device_chain(panel_alleles, recomb_rates, genotypes)


def solution(mesh):
    placed = (P("group", "batch"), P("group"), P(None, "group"))
    return jax.shard_map(
        on_device, mesh=mesh, in_specs=placed, out_specs=(P(None, "group"), P()), check_vma=False
    )
```

```python
import functools
import math

import jax
import jax.numpy as jnp
from jax import lax
from jax.experimental import pallas as pl
from jax.experimental.pallas import tpu as pltpu
from jax.sharding import PartitionSpec as P

MISMATCH = 0.05
HIGHEST = lax.Precision.HIGHEST


def haplotypes(panel_rows):
    return panel_rows.shape[1] * lax.axis_size("batch")


def from_behind(x, axis, by):
    peers = lax.axis_size(axis)
    pairs = [(i, i + by) for i in range(peers) if 0 <= i + by < peers]
    return lax.ppermute(x, axis, pairs)


def emission(panel_rows, geno_col):
    observed = geno_col[:, None]
    agrees = jnp.where(panel_rows == observed, 1.0 - MISMATCH, MISMATCH)
    return jnp.where(observed == 2, 1.0, agrees).astype(jnp.float32)


def forward_terms(panel_rows, geno_col, switches):
    emitted = emission(panel_rows, geno_col)
    retain = emitted * (1.0 - switches)[:, None]
    inject = emitted * (switches / haplotypes(panel_rows))[:, None]
    return (retain, inject, None)


def backward_terms(panel_rows, geno_col, switches):
    emitted = emission(panel_rows, geno_col)[::-1]
    flipped = switches[::-1]
    retain = emitted * (1.0 - flipped)[:, None]
    inject = jnp.broadcast_to((flipped / haplotypes(panel_rows))[:, None], emitted.shape)
    return (retain, inject, emitted)


def partial_sums(entering, retain, inject, weight, extent):
    logs = jnp.cumsum(jnp.log(retain), axis=0)
    shifted = jnp.concatenate([jnp.zeros_like(entering)[None], logs[: extent - 1]], axis=0)
    before = jnp.exp(shifted)
    left_side = before if weight is None else weight * before
    leading = jnp.einsum("jk,k->j", left_side, entering, precision=HIGHEST)
    anchor = shifted[0]
    right_side = inject * jnp.exp(anchor[None] - logs)
    nearby = jnp.exp(jnp.minimum(shifted - anchor[None], 0.0))
    nearby = nearby if weight is None else weight * nearby
    columns = [jnp.einsum("jk,tk->jt", nearby, right_side, precision=HIGHEST)]
    coupling = jnp.concatenate(columns, axis=1)
    return (leading, coupling)


def solve_sums(leading, coupling):
    columns = coupling.shape[1]

    def settle(marker, sigmas):
        below = jnp.arange(columns) < marker
        update = leading[marker] + jnp.sum(
            jnp.where(below, coupling[marker] * sigmas[:columns], 0.0)
        )
        return sigmas.at[marker].set(update)

    return lax.fori_loop(0, leading.shape[0], settle, jnp.zeros_like(leading))


def advance(entering, retain, inject, sigmas, keep_states):

    def advance_single(current, pieces):
        current = pieces[0] * current + pieces[1] * pieces[2]
        return (current, current if keep_states else None)

    return lax.scan(advance_single, entering, (retain, inject, sigmas[: retain.shape[0]]))


def place_rows(store, block, active):
    return jnp.where(active, block, store)


def on_device_chain(panel_alleles, recomb_rates, genotypes):
    chain_size = lax.axis_size("group")
    position = lax.axis_index("group")
    markers, width = panel_alleles.shape
    targets = genotypes.shape[0]
    bundles = targets // targets
    uniform = jnp.full((targets, width), 1.0 / haplotypes(panel_alleles), jnp.float32)
    first_row = position == 0
    last_row = position == chain_size - 1

    def local_sums(active, arrivals, geno_rows, maker, extent):

        def local_compute():

            def local_single(pieces):
                retain, inject, weight = maker(panel_alleles, pieces[1], recomb_rates)
                return partial_sums(pieces[0], retain, inject, weight, extent)

            return lax.map(local_single, (arrivals, geno_rows))

        def local_skipped():
            return (
                jnp.zeros((targets, extent), jnp.float32),
                jnp.zeros((targets, extent, markers), jnp.float32),
            )

        return lax.cond(active, local_compute, local_skipped)

    def outgoing(active, arrivals, geno_rows, sigmas, maker, scale_row):

        def outgoing_compute():

            def outgoing_single(pieces):
                retain, inject, weight = maker(panel_alleles, pieces[1], recomb_rates)
                ending, unused = advance(pieces[0], retain, inject, pieces[2], False)
                return ending / pieces[2][scale_row]

            return lax.map(outgoing_single, (arrivals, geno_rows, sigmas))

        def outgoing_skipped():
            return jnp.zeros((targets, width), jnp.float32)

        return lax.cond(active, outgoing_compute, outgoing_skipped)

    def moment_step(moment, carried_state):
        (
            sent_forward,
            sent_backward,
            sent_running,
            store_forward,
            store_backward,
            sigma_forward,
            sigma_backward,
            log_terms,
        ) = carried_state
        got_forward = from_behind(sent_forward, "group", 1)
        got_backward = from_behind(sent_backward, "group", -1)
        entering_forward = jnp.where(first_row, uniform, got_forward)
        entering_backward = jnp.where(last_row, uniform, got_backward)
        index_forward = moment - position
        index_backward = moment - (chain_size - 1 - position)
        active_forward = (index_forward >= 0) & (index_forward < bundles)
        active_backward = (index_backward >= 0) & (index_backward < bundles)
        lead_forward, couple_forward = local_sums(
            active_forward, entering_forward, genotypes, forward_terms, markers + 1
        )
        lead_backward, couple_backward = local_sums(
            active_backward, entering_backward, genotypes, backward_terms, markers
        )
        lead_forward, couple_forward, lead_backward, couple_backward = lax.psum(
            (lead_forward, couple_forward, lead_backward, couple_backward), "batch"
        )
        sigmas_forward = jax.vmap(solve_sums)(lead_forward, couple_forward)
        sigmas_backward = jax.vmap(solve_sums)(lead_backward, couple_backward)
        next_forward = outgoing(
            active_forward, entering_forward, genotypes, sigmas_forward, forward_terms, markers
        )
        next_backward = outgoing(
            active_backward,
            entering_backward,
            genotypes,
            sigmas_backward,
            backward_terms,
            markers - 1,
        )
        guarded = jnp.where(active_forward, sigmas_forward[:, markers], 1.0)
        running = jnp.log(guarded)
        store_forward = place_rows(store_forward, entering_forward, active_forward)
        store_backward = place_rows(store_backward, entering_backward, active_backward)
        sigma_forward = place_rows(sigma_forward, sigmas_forward, active_forward)
        sigma_backward = place_rows(sigma_backward, sigmas_backward, active_backward)
        log_terms = place_rows(log_terms, running, active_forward)
        return (
            next_forward,
            next_backward,
            running,
            store_forward,
            store_backward,
            sigma_forward,
            sigma_backward,
            log_terms,
        )

    initial = (
        jnp.zeros((targets, width), jnp.float32),
        jnp.zeros((targets, width), jnp.float32),
        jnp.zeros((targets,), jnp.float32),
        jnp.zeros((targets, width), jnp.float32),
        jnp.zeros((targets, width), jnp.float32),
        jnp.zeros((targets, markers + 1), jnp.float32),
        jnp.zeros((targets, markers), jnp.float32),
        jnp.zeros((targets,), jnp.float32),
    )
    final_state = lax.fori_loop(0, chain_size + bundles - 1, moment_step, initial)
    store_forward, store_backward, sigma_forward, sigma_backward, log_terms = final_state[3:]
    whole_log = lax.psum(log_terms, "group")
    log_likelihood = whole_log / (markers * chain_size)

    def posterior(pieces):
        entering_ahead, entering_behind, geno_col, sigmas_ahead, sigmas_behind = pieces
        retain, inject, weight = forward_terms(panel_alleles, geno_col, recomb_rates)
        unused_f, forward_states = advance(entering_ahead, retain, inject, sigmas_ahead, True)
        forward_rows = forward_states / sigmas_ahead[1:, None]
        retain, inject, weight = backward_terms(panel_alleles, geno_col, recomb_rates)
        unused_b, backward_states = advance(entering_behind, retain, inject, sigmas_behind, True)
        scaled_back = backward_states[:-1] / sigmas_behind[:-1, None]
        backward_rows = jnp.concatenate([entering_behind[None], scaled_back], axis=0)[::-1]
        product = forward_rows * backward_rows
        numerator = jnp.sum(jnp.where(panel_alleles == 1, product, 0.0), axis=1)
        return (numerator, jnp.sum(product, axis=1))

    numerator, denominator = lax.map(
        posterior, (store_forward, store_backward, genotypes, sigma_forward, sigma_backward)
    )
    numerator, denominator = lax.psum((numerator, denominator), "batch")
    return (numerator / denominator, log_likelihood)


ROWS, LANES = 8, 128
HALF = LANES // 2
GROUPS = 4
MISSING = 2
SCALE = math.sqrt(MISMATCH * (1.0 - MISMATCH))
HALF_STEP = 0.5 * math.log((1.0 - MISMATCH) / MISMATCH)
VMEM = pl.BlockSpec(memory_space=pltpu.VMEM)
SMEM = pl.BlockSpec(memory_space=pltpu.SMEM)
F32, BF16 = jnp.float32, jnp.bfloat16


def iota(shape, axis):
    return lax.broadcasted_iota(jnp.int32, shape, axis)


def left_blocks(t):
    b = t // ROWS
    return list(range(b + 1)) if b < GROUPS // 2 else list(range(GROUPS - 1, b - 1, -1))


MARKERS = ROWS * GROUPS
HALF_T = MARKERS // 2
LEFT = [
    [(h, t, b) for t in range(half * HALF_T, (half + 1) * HALF_T) for b in left_blocks(t) for h in range(2)]
    for half in range(2)
]
LEFT_AT = [{entry: slot for slot, entry in enumerate(LEFT[half])} for half in range(2)]
TALL = len(LEFT[0]) // 4 * ROWS
SHORT_TALL = ROWS // 2 * ROWS
EXTRA = (GROUPS // 2 + 1) * ROWS


def window_kernel(step, rate_ref, *refs):
    pieces, geno_refs = refs[:GROUPS], refs[GROUPS : 2 * GROUPS]
    t_ref, em_ref, panel, genos, wide, left = refs[2 * GROUPS :]
    place = lax.axis_index("group")
    columns = panel.shape[1]
    for d in range(GROUPS):
        rows = pl.ds(pl.multiple_of((place ^ d) * ROWS, ROWS), ROWS)
        panel[rows, :] = pieces[d][...]
        genos[rows, :] = geno_refs[d][...]

    r, j = iota((4 * MARKERS, 2 * MARKERS), 0), iota((4 * MARKERS, 2 * MARKERS), 1)
    same = r // (2 * MARKERS) == j // MARKERS
    prefix, marker = (r // MARKERS) % 2 == 0, r % MARKERS
    at = j % MARKERS
    sums = jnp.where(prefix, jnp.where(at <= marker, 1.0, 0.0), jnp.where(at < marker, -1.0, 0.0))
    sums = jnp.where(same, sums, 0.0).astype(BF16)

    for start in range(0, columns, step):
        here = slice(start, start + step)
        signs = []
        for h in range(2):
            for b in range(GROUPS):
                rows = slice(b * ROWS, (b + 1) * ROWS)
                seen = genos[rows, h * HALF : h * HALF + 1]
                agrees = jnp.where(panel[rows, here] == seen, 1.0, -1.0)
                signs.append(jnp.where(seen == MISSING, 0.0, agrees))
        signs = jnp.concatenate(signs, axis=0).astype(BF16)
        power = jnp.dot(sums, signs, preferred_element_type=F32)
        value = jnp.exp(power * HALF_STEP)
        upper = value.astype(BF16).astype(F32)
        lower = value - upper
        blocks = {}
        for h in range(2):
            for kind in range(2):
                for b in range(GROUPS):
                    at = h * 2 * MARKERS + kind * MARKERS + b * ROWS
                    both = jnp.concatenate([upper[at : at + ROWS], lower[at : at + ROWS]], axis=0).astype(BF16)
                    blocks[kind, h, b] = both
                    wide[kind, (h * GROUPS + b) * 2 * ROWS : (h * GROUPS + b + 1) * 2 * ROWS, here] = both
        for half in range(2):
            for slot, (h, t, b) in enumerate(LEFT[half]):
                carries = jnp.broadcast_to(panel[t : t + 1, here], (2 * ROWS, step)).astype(F32).astype(BF16)
                left[half, slot * 2 * ROWS : (slot + 1) * 2 * ROWS, here] = blocks[1 - half, h, b] * carries

    def product(a, b):
        return lax.dot_general(a, b, (((1,), (1,)), ((), ())), preferred_element_type=F32)

    lane = iota((ROWS, LANES), 1)
    first = lane % (2 * ROWS) < ROWS

    def rows_of(acc, slot):
        return acc[slot * 2 * ROWS : slot * 2 * ROWS + ROWS] + acc[slot * 2 * ROWS + ROWS : (slot + 1) * 2 * ROWS]

    def fold(a, b):
        return jnp.where(first, a + pltpu.roll(a, LANES - ROWS, 1), b + pltpu.roll(b, ROWS, 1))

    def both_targets(acc, slots):
        return jnp.where(lane < HALF, rows_of(acc, slots[0]), rows_of(acc, slots[1]))

    for half in range(2):
        sums_t = product(left[half], wide[half])
        tiles = {
            (t, b): both_targets(sums_t, [LEFT_AT[half][h, t, b] for h in range(2)]) for h, t, b in LEFT[half] if h == 0
        }
        short, long = near_markers(half)
        pairs = [((short[2 * q], 0), (short[2 * q + 1], 0)) for q in range(ROWS // 2)]
        pairs += [((t, 0), (t, 1)) for t in long]
        for q, pair in enumerate(pairs):
            a, b = (tiles[t, left_blocks(t)[depth]] for t, depth in pair)
            t_ref[half, q * ROWS : (q + 1) * ROWS, :] = fold(a, b)
    sums_e = product(wide[1], wide[0])
    tiles = [both_targets(sums_e, [b, GROUPS + b]) for b in range(GROUPS)]
    for q in range(GROUPS // 2):
        em_ref[q * ROWS : (q + 1) * ROWS, :] = fold(tiles[2 * q], tiles[2 * q + 1])
    row = iota((ROWS, LANES), 0)
    rates = jnp.zeros((ROWS, LANES), F32)
    for i in range(ROWS):
        rates = jnp.where(row == i, rate_ref[i], rates)
    own = pl.ds(pl.multiple_of(place * ROWS, ROWS), ROWS)
    inner = lane % (LANES // GROUPS)
    known = jnp.where(genos[own, :] == MISSING, 0.0, 1.0)
    known0 = jnp.broadcast_to(known[:, 0:1], (ROWS, LANES))
    known1 = jnp.broadcast_to(known[:, HALF : HALF + 1], (ROWS, LANES))
    misc = jnp.where(inner < 2 * ROWS, rates, jnp.where(inner < 3 * ROWS, known0, known1))
    em_ref[GROUPS // 2 * ROWS :, :] = jnp.where(lane // (LANES // GROUPS) == place, misc, 0.0)


def near_markers(half):
    outer, inner = (0, 1) if half == 0 else (GROUPS - 1, GROUPS - 2)
    return [outer * ROWS + i for i in range(ROWS)], [inner * ROWS + i for i in range(ROWS)]


def finish_kernel(panel_size, copies, sum_ref, dose_ref, log_ref):
    place = lax.axis_index("group")
    row, lane = iota((ROWS, LANES), 0), iota((ROWS, LANES), 1)
    target = lane // HALF
    folded = (lane % (2 * ROWS)) // ROWS
    misc = sum_ref[TALL + GROUPS // 2 * ROWS :, :] * (1.0 / copies)
    wide = LANES // GROUPS

    def spread(tile, at):
        return jnp.broadcast_to(tile[:, at : at + 1], (ROWS, LANES))

    rates = [spread(misc, b * wide) for b in range(GROUPS)]
    odds = [rate / (1.0 - rate) for rate in rates]
    inverse = 1.0 / panel_size
    ahead = []
    for b in range(GROUPS):
        following = odds[b + 1][0:1, :] if b + 1 < GROUPS else jnp.ones((1, LANES), F32)
        ahead.append(jnp.concatenate([odds[b][1:, :], following], axis=0) * inverse)
    behind = [odd * inverse for odd in odds]

    pair = sum_ref[TALL : TALL + GROUPS // 2 * ROWS, :]
    trail_tiles = []
    for q in range(GROUPS // 2):
        factor = jnp.where(folded == 0, behind[2 * q], behind[2 * q + 1])
        trail_tiles.append(pair[q * ROWS : (q + 1) * ROWS] * factor)
    square = jnp.concatenate([pair, jnp.zeros((LANES - pair.shape[0], LANES), F32)], axis=0)
    turned = jnp.transpose(square)

    def turned_tile(h, b, f):
        at = h * HALF + b * 2 * ROWS + f * ROWS
        return turned[at : at + ROWS] * ahead[b]

    lead_tiles = {(h, b, f): turned_tile(h, b, f) for h in range(2) for b in range(GROUPS) for f in range(2)}

    def lead_column(t, b):
        s, at = t // ROWS, (t // ROWS // 2) * ROWS + t % ROWS
        return jnp.where(target == 0, spread(lead_tiles[0, b, s % 2], at), spread(lead_tiles[1, b, s % 2], at))

    def trail_column(t, b):
        at = 2 * ROWS * (t // ROWS) + t % ROWS + ROWS * (b % 2)
        tile = trail_tiles[b // 2]
        return jnp.where(target == 0, spread(tile, at), spread(tile, HALF + at))

    zero = jnp.zeros((ROWS, LANES), F32)
    lead, trail, starts, ends = [zero] * GROUPS, [zero] * GROUPS, [zero] * GROUPS, [zero] * GROUPS
    v = jnp.ones((ROWS, LANES), F32)
    z = jnp.ones((ROWS, LANES), F32)
    for t in range(MARKERS):
        u = MARKERS - 1 - t
        bt, bu = t // ROWS, u // ROWS
        starts[bt] = jnp.where(row == t % ROWS, v, starts[bt])
        ends[bu] = jnp.where(row == u % ROWS, z, ends[bu])
        for b in range(bt, GROUPS):
            lead[b] = lead[b] + v * lead_column(t, b)
        for b in range(bu + 1):
            trail[b] = trail[b] + z * trail_column(u, b)
        v = jnp.broadcast_to(lead[bt][t % ROWS : t % ROWS + 1, :], (ROWS, LANES))
        z = jnp.broadcast_to(trail[bu][u % ROWS : u % ROWS + 1, :], (ROWS, LANES))
    total = v

    low = place < GROUPS // 2
    side = jnp.where(low, 1, -1)
    inner = lane % HALF
    near = [jnp.where(low, starts[b], ends[GROUPS - 1 - b]) for b in range(2)]
    across = [jnp.where(low, ends[b], starts[b]) for b in range(GROUPS)]
    picked = across[GROUPS - 1]
    for b in range(GROUPS - 1):
        picked = jnp.where(inner // (2 * ROWS) == b, across[b], picked)
    picked = jnp.where(row == lane % ROWS, picked, 0.0)
    across = jnp.sum(picked, axis=0, keepdims=True)
    far_end = ROWS * (inner // (2 * ROWS)) + lane % ROWS
    scale = inverse / total[0:1, :]

    def inside(t, near_end):
        return ((near_end - t) * side <= 0) & ((far_end - t) * side >= 0)

    def put(rows_of_t):
        doses = []
        for h in range(2):
            dose = jnp.sum(jnp.where(target == h, rows_of_t * scale, 0.0), axis=1, keepdims=True)
            doses.append(jnp.sum(jnp.where(row == lane, dose, 0.0), axis=0, keepdims=True))
        dose_ref[...] = jnp.concatenate(doses, axis=0)[:, :ROWS]

    outermost = (place == 0) | (place == GROUPS - 1)

    @pl.when(outermost)
    def _():
        weight = near[0] * across
        near_end = place * ROWS + row
        merged = zero
        for q in range(ROWS // 2):
            t = place * ROWS + 2 * q + folded
            tile = jnp.where(inside(t, near_end), sum_ref[q * ROWS : (q + 1) * ROWS, :] * weight, 0.0)
            tile = jnp.sum(tile, axis=0, keepdims=True)
            merged = jnp.where(row // 2 == q, jnp.where(folded == row % 2, tile, 0.0), merged)
        put(merged)

    @pl.when(jnp.logical_not(outermost))
    def _():
        weight = jnp.where(folded == 0, near[0], near[1]) * across
        near_end = jnp.where(low, folded, GROUPS - 1 - folded) * ROWS + row
        merged = zero
        for q in range(ROWS):
            at = SHORT_TALL + q * ROWS
            tile = jnp.where(inside(place * ROWS + q, near_end), sum_ref[at : at + ROWS, :] * weight, 0.0)
            merged = jnp.where(row == q, jnp.sum(tile, axis=0, keepdims=True), merged)
        put(merged)

    counts = jnp.sum(misc, axis=0, keepdims=True)
    stay = [jnp.log(1.0 - rate) for rate in rates]
    stay[0] = jnp.where(row == 0, 0.0, stay[0])
    stay = jnp.sum(sum(stay), axis=0, keepdims=True)
    logs = []
    for h in range(2):
        seen = sum(counts[:, b * wide + (2 + h) * ROWS : b * wide + (2 + h) * ROWS + 1] for b in range(GROUPS))
        whole = jnp.log(total[0:1, h * HALF : h * HALF + 1]) + stay[:, 0:1] + seen * math.log(SCALE)
        logs.append(whole * (1.0 / MARKERS))
    log_ref[...] = jnp.concatenate(logs, axis=1)


def exchange(x, axis, by):
    peers = lax.axis_size(axis)
    return lax.ppermute(x, axis, [(i, i ^ by) for i in range(peers)])


def exchange_crossed(x, by):
    copies = lax.axis_size("batch")
    peers = lax.axis_size("group") * copies
    return lax.ppermute(x, ("group", "batch"), [(i, i ^ (copies + by)) for i in range(peers)])


def on_device_windows(panel_alleles, recomb_rates, genotypes):
    width = panel_alleles.shape[1]
    copies = lax.axis_size("batch")
    chunk = width // GROUPS
    place = lax.axis_index("group")
    own_genos = jnp.broadcast_to(genotypes.T[:, :, None], (ROWS, 2, HALF)).reshape(ROWS, LANES)
    cuts = panel_alleles.reshape(ROWS, GROUPS, chunk)
    cuts = [lax.dynamic_index_in_dim(cuts, place ^ d, 1, False) for d in range(GROUPS)]
    pieces, tags = [cuts[0]], [own_genos]
    for d in range(1, GROUPS):
        got = exchange(jnp.concatenate([cuts[d], own_genos], axis=1), "group", d)
        pieces.append(got[:, :chunk])
        tags.append(got[:, chunk:])
    sums_t, sums_e = pl.pallas_call(
        functools.partial(window_kernel, min(512, chunk)),
        out_shape=[
            jax.ShapeDtypeStruct((2, TALL, LANES), F32),
            jax.ShapeDtypeStruct((EXTRA, LANES), F32),
        ],
        in_specs=[SMEM] + [VMEM] * (2 * GROUPS),
        out_specs=[VMEM] * 2,
        scratch_shapes=[
            pltpu.VMEM((MARKERS, chunk), jnp.int32),
            pltpu.VMEM((MARKERS, LANES), jnp.int32),
            pltpu.VMEM((2, 4 * MARKERS, chunk), BF16),
            pltpu.VMEM((2, len(LEFT[0]) * 2 * ROWS, chunk), BF16),
        ],
        compiler_params=pltpu.CompilerParams(vmem_limit_bytes=40 * 1024 * 1024),
        name="windows",
    )(recomb_rates, *pieces, *tags)

    sent = jnp.concatenate([sums_t[0], sums_e, sums_t[1]], axis=0)
    both = sent + exchange(sent, "group", 1)
    low = place < GROUPS // 2
    upper, lower = both[: TALL + EXTRA], both[TALL:]
    lower = jnp.concatenate([lower[EXTRA:], lower[:EXTRA]], axis=0)
    kept = jnp.where(low, upper, lower) + exchange(jnp.where(low, lower, upper), "group", 3)
    by = 1
    while by < copies:
        kept = kept + exchange_crossed(kept, by)
        by *= 2
    dosage, logs = pl.pallas_call(
        functools.partial(finish_kernel, float(width * copies), float(copies)),
        out_shape=[jax.ShapeDtypeStruct((2, ROWS), F32), jax.ShapeDtypeStruct((1, 2), F32)],
        in_specs=[VMEM],
        out_specs=[VMEM] * 2,
        name="finish",
    )(kept)
    return dosage, logs.reshape(2)


def fits_windows(panel_alleles, genotypes, groups, copies):
    markers, width = panel_alleles.shape
    return (
        groups == GROUPS
        and copies & (copies - 1) == 0
        and markers == ROWS
        and genotypes.shape[0] == 2
        and width % (GROUPS * LANES * 4) == 0
    )


def on_device(panel_alleles, recomb_rates, genotypes):
    groups, copies = lax.axis_size("group"), lax.axis_size("batch")
    if fits_windows(panel_alleles, genotypes, groups, copies):
        return on_device_windows(panel_alleles, recomb_rates, genotypes)
    return on_device_chain(panel_alleles, recomb_rates, genotypes)


def solution(mesh):
    placed = (P("group", "batch"), P("group"), P(None, "group"))
    return jax.shard_map(
        on_device, mesh=mesh, in_specs=placed, out_specs=(P(None, "group"), P()), check_vma=False
    )
```

```python
import functools
import math

import jax
import jax.numpy as jnp
from jax import lax
from jax.experimental import pallas as pl
from jax.experimental.pallas import tpu as pltpu
from jax.sharding import PartitionSpec as P

MISMATCH = 0.05
HIGHEST = lax.Precision.HIGHEST


def haplotypes(panel_rows):
    return panel_rows.shape[1] * lax.axis_size("batch")


def from_behind(x, axis, by):
    peers = lax.axis_size(axis)
    pairs = [(i, i + by) for i in range(peers) if 0 <= i + by < peers]
    return lax.ppermute(x, axis, pairs)


def emission(panel_rows, geno_col):
    observed = geno_col[:, None]
    agrees = jnp.where(panel_rows == observed, 1.0 - MISMATCH, MISMATCH)
    return jnp.where(observed == 2, 1.0, agrees).astype(jnp.float32)


def forward_terms(panel_rows, geno_col, switches):
    emitted = emission(panel_rows, geno_col)
    retain = emitted * (1.0 - switches)[:, None]
    inject = emitted * (switches / haplotypes(panel_rows))[:, None]
    return (retain, inject, None)


def backward_terms(panel_rows, geno_col, switches):
    emitted = emission(panel_rows, geno_col)[::-1]
    flipped = switches[::-1]
    retain = emitted * (1.0 - flipped)[:, None]
    inject = jnp.broadcast_to((flipped / haplotypes(panel_rows))[:, None], emitted.shape)
    return (retain, inject, emitted)


def partial_sums(entering, retain, inject, weight, extent):
    logs = jnp.cumsum(jnp.log(retain), axis=0)
    shifted = jnp.concatenate([jnp.zeros_like(entering)[None], logs[: extent - 1]], axis=0)
    before = jnp.exp(shifted)
    left_side = before if weight is None else weight * before
    leading = jnp.einsum("jk,k->j", left_side, entering, precision=HIGHEST)
    anchor = shifted[0]
    right_side = inject * jnp.exp(anchor[None] - logs)
    nearby = jnp.exp(jnp.minimum(shifted - anchor[None], 0.0))
    nearby = nearby if weight is None else weight * nearby
    columns = [jnp.einsum("jk,tk->jt", nearby, right_side, precision=HIGHEST)]
    coupling = jnp.concatenate(columns, axis=1)
    return (leading, coupling)


def solve_sums(leading, coupling):
    columns = coupling.shape[1]

    def settle(marker, sigmas):
        below = jnp.arange(columns) < marker
        update = leading[marker] + jnp.sum(
            jnp.where(below, coupling[marker] * sigmas[:columns], 0.0)
        )
        return sigmas.at[marker].set(update)

    return lax.fori_loop(0, leading.shape[0], settle, jnp.zeros_like(leading))


def advance(entering, retain, inject, sigmas, keep_states):

    def advance_single(current, pieces):
        current = pieces[0] * current + pieces[1] * pieces[2]
        return (current, current if keep_states else None)

    return lax.scan(advance_single, entering, (retain, inject, sigmas[: retain.shape[0]]))


def place_rows(store, block, active):
    return jnp.where(active, block, store)


def on_device_chain(panel_alleles, recomb_rates, genotypes):
    chain_size = lax.axis_size("group")
    position = lax.axis_index("group")
    markers, width = panel_alleles.shape
    targets = genotypes.shape[0]
    bundles = targets // targets
    uniform = jnp.full((targets, width), 1.0 / haplotypes(panel_alleles), jnp.float32)
    first_row = position == 0
    last_row = position == chain_size - 1

    def local_sums(active, arrivals, geno_rows, maker, extent):

        def local_compute():

            def local_single(pieces):
                retain, inject, weight = maker(panel_alleles, pieces[1], recomb_rates)
                return partial_sums(pieces[0], retain, inject, weight, extent)

            return lax.map(local_single, (arrivals, geno_rows))

        def local_skipped():
            return (
                jnp.zeros((targets, extent), jnp.float32),
                jnp.zeros((targets, extent, markers), jnp.float32),
            )

        return lax.cond(active, local_compute, local_skipped)

    def outgoing(active, arrivals, geno_rows, sigmas, maker, scale_row):

        def outgoing_compute():

            def outgoing_single(pieces):
                retain, inject, weight = maker(panel_alleles, pieces[1], recomb_rates)
                ending, unused = advance(pieces[0], retain, inject, pieces[2], False)
                return ending / pieces[2][scale_row]

            return lax.map(outgoing_single, (arrivals, geno_rows, sigmas))

        def outgoing_skipped():
            return jnp.zeros((targets, width), jnp.float32)

        return lax.cond(active, outgoing_compute, outgoing_skipped)

    def moment_step(moment, carried_state):
        (
            sent_forward,
            sent_backward,
            sent_running,
            store_forward,
            store_backward,
            sigma_forward,
            sigma_backward,
            log_terms,
        ) = carried_state
        got_forward = from_behind(sent_forward, "group", 1)
        got_backward = from_behind(sent_backward, "group", -1)
        entering_forward = jnp.where(first_row, uniform, got_forward)
        entering_backward = jnp.where(last_row, uniform, got_backward)
        index_forward = moment - position
        index_backward = moment - (chain_size - 1 - position)
        active_forward = (index_forward >= 0) & (index_forward < bundles)
        active_backward = (index_backward >= 0) & (index_backward < bundles)
        lead_forward, couple_forward = local_sums(
            active_forward, entering_forward, genotypes, forward_terms, markers + 1
        )
        lead_backward, couple_backward = local_sums(
            active_backward, entering_backward, genotypes, backward_terms, markers
        )
        lead_forward, couple_forward, lead_backward, couple_backward = lax.psum(
            (lead_forward, couple_forward, lead_backward, couple_backward), "batch"
        )
        sigmas_forward = jax.vmap(solve_sums)(lead_forward, couple_forward)
        sigmas_backward = jax.vmap(solve_sums)(lead_backward, couple_backward)
        next_forward = outgoing(
            active_forward, entering_forward, genotypes, sigmas_forward, forward_terms, markers
        )
        next_backward = outgoing(
            active_backward,
            entering_backward,
            genotypes,
            sigmas_backward,
            backward_terms,
            markers - 1,
        )
        guarded = jnp.where(active_forward, sigmas_forward[:, markers], 1.0)
        running = jnp.log(guarded)
        store_forward = place_rows(store_forward, entering_forward, active_forward)
        store_backward = place_rows(store_backward, entering_backward, active_backward)
        sigma_forward = place_rows(sigma_forward, sigmas_forward, active_forward)
        sigma_backward = place_rows(sigma_backward, sigmas_backward, active_backward)
        log_terms = place_rows(log_terms, running, active_forward)
        return (
            next_forward,
            next_backward,
            running,
            store_forward,
            store_backward,
            sigma_forward,
            sigma_backward,
            log_terms,
        )

    initial = (
        jnp.zeros((targets, width), jnp.float32),
        jnp.zeros((targets, width), jnp.float32),
        jnp.zeros((targets,), jnp.float32),
        jnp.zeros((targets, width), jnp.float32),
        jnp.zeros((targets, width), jnp.float32),
        jnp.zeros((targets, markers + 1), jnp.float32),
        jnp.zeros((targets, markers), jnp.float32),
        jnp.zeros((targets,), jnp.float32),
    )
    final_state = lax.fori_loop(0, chain_size + bundles - 1, moment_step, initial)
    store_forward, store_backward, sigma_forward, sigma_backward, log_terms = final_state[3:]
    whole_log = lax.psum(log_terms, "group")
    log_likelihood = whole_log / (markers * chain_size)

    def posterior(pieces):
        entering_ahead, entering_behind, geno_col, sigmas_ahead, sigmas_behind = pieces
        retain, inject, weight = forward_terms(panel_alleles, geno_col, recomb_rates)
        unused_f, forward_states = advance(entering_ahead, retain, inject, sigmas_ahead, True)
        forward_rows = forward_states / sigmas_ahead[1:, None]
        retain, inject, weight = backward_terms(panel_alleles, geno_col, recomb_rates)
        unused_b, backward_states = advance(entering_behind, retain, inject, sigmas_behind, True)
        scaled_back = backward_states[:-1] / sigmas_behind[:-1, None]
        backward_rows = jnp.concatenate([entering_behind[None], scaled_back], axis=0)[::-1]
        product = forward_rows * backward_rows
        numerator = jnp.sum(jnp.where(panel_alleles == 1, product, 0.0), axis=1)
        return (numerator, jnp.sum(product, axis=1))

    numerator, denominator = lax.map(
        posterior, (store_forward, store_backward, genotypes, sigma_forward, sigma_backward)
    )
    numerator, denominator = lax.psum((numerator, denominator), "batch")
    return (numerator / denominator, log_likelihood)


ROWS, LANES = 8, 128
HALF = LANES // 2
GROUPS = 4
PARTS = 2
MISSING = 2
SCALE = math.sqrt(MISMATCH * (1.0 - MISMATCH))
HALF_STEP = 0.5 * math.log((1.0 - MISMATCH) / MISMATCH)
VMEM = pl.BlockSpec(memory_space=pltpu.VMEM)
SMEM = pl.BlockSpec(memory_space=pltpu.SMEM)
F32, BF16 = jnp.float32, jnp.bfloat16


def iota(shape, axis):
    return lax.broadcasted_iota(jnp.int32, shape, axis)


def left_blocks(t):
    b = t // ROWS
    return list(range(b + 1)) if b < GROUPS // 2 else list(range(GROUPS - 1, b - 1, -1))


MARKERS = ROWS * GROUPS
HALF_T = MARKERS // 2
LEFT = [
    [(h, t, b) for t in range(half * HALF_T, (half + 1) * HALF_T) for b in left_blocks(t) for h in range(2)]
    for half in range(2)
]
LEFT_AT = [{entry: slot for slot, entry in enumerate(LEFT[half])} for half in range(2)]
TALL = len(LEFT[0]) // 4 * ROWS
SHORT_TALL = ROWS // 2 * ROWS
PAIRS = GROUPS // 2 * ROWS
EXTRA = PAIRS + ROWS


def pack_kernel(parts, geno_ref, rate_ref, panel_ref, *refs):
    outs, (misc_ref, genos, rates_in, sems) = refs[:-4], refs[-4:]
    place = lax.axis_index("group")
    chunk = panel_ref.shape[1] // GROUPS
    part = chunk // parts
    copies = []
    for n, ref in enumerate(outs):
        d, p = n % GROUPS, n // GROUPS
        start = pl.multiple_of((place ^ d) * chunk + p * part, LANES)
        copies.append(
            pltpu.make_async_copy(panel_ref.at[:, pl.ds(start, part)], ref.at[:, pl.ds(0, part)], sems.at[n])
        )
    small = [
        pltpu.make_async_copy(geno_ref, genos, sems.at[len(outs)]),
        pltpu.make_async_copy(rate_ref, rates_in, sems.at[len(outs) + 1]),
    ]
    for copy in small + copies:
        copy.start()
    for copy in small:
        copy.wait()
    row, lane = iota((ROWS, LANES), 0), iota((ROWS, LANES), 1)
    tile = jnp.zeros((ROWS, LANES), jnp.int32)
    rates = jnp.zeros((ROWS, LANES), F32)
    for i in range(ROWS):
        tile = jnp.where(row == i, jnp.where(lane < HALF, genos[0, i], genos[1, i]), tile)
        rates = jnp.where(row == i, rates_in[i], rates)
    for ref in outs[:GROUPS]:
        ref[:, part:] = tile
    inner = lane % (LANES // GROUPS)
    known = jnp.where(tile == MISSING, 0.0, 1.0)
    known = [jnp.broadcast_to(known[:, h * HALF : h * HALF + 1], (ROWS, LANES)) for h in range(2)]
    misc = jnp.where(inner < 2 * ROWS, rates, jnp.where(inner < 3 * ROWS, known[0], known[1]))
    misc_ref[...] = jnp.where(lane // (LANES // GROUPS) == place, misc, 0.0)
    for copy in copies:
        copy.wait()


def window_kernel(step, *refs):
    pieces, geno_refs = refs[:GROUPS], refs[GROUPS : 2 * GROUPS]
    t_ref, em_ref, panel, genos, wide, left = refs[2 * GROUPS :]
    place = lax.axis_index("group")
    columns = panel.shape[1]
    for d in range(GROUPS):
        rows = pl.ds(pl.multiple_of((place ^ d) * ROWS, ROWS), ROWS)
        panel[rows, :] = pieces[d][...]
        genos[rows, :] = geno_refs[d][...]

    r, j = iota((4 * MARKERS, 2 * MARKERS), 0), iota((4 * MARKERS, 2 * MARKERS), 1)
    same = r // (2 * MARKERS) == j // MARKERS
    prefix, marker = (r // MARKERS) % 2 == 0, r % MARKERS
    at = j % MARKERS
    sums = jnp.where(prefix, jnp.where(at <= marker, 1.0, 0.0), jnp.where(at < marker, -1.0, 0.0))
    sums = jnp.where(same, sums, 0.0).astype(BF16)

    for start in range(0, columns, step):
        here = slice(start, start + step)
        signs = []
        for h in range(2):
            for b in range(GROUPS):
                rows = slice(b * ROWS, (b + 1) * ROWS)
                seen = genos[rows, h * HALF : h * HALF + 1]
                agrees = jnp.where(panel[rows, here] == seen, 1.0, -1.0)
                signs.append(jnp.where(seen == MISSING, 0.0, agrees))
        signs = jnp.concatenate(signs, axis=0).astype(BF16)
        power = jnp.dot(sums, signs, preferred_element_type=F32)
        value = jnp.exp(power * HALF_STEP)
        upper = value.astype(BF16).astype(F32)
        lower = value - upper
        blocks = {}
        for h in range(2):
            for kind in range(2):
                for b in range(GROUPS):
                    at = h * 2 * MARKERS + kind * MARKERS + b * ROWS
                    both = jnp.concatenate([upper[at : at + ROWS], lower[at : at + ROWS]], axis=0).astype(BF16)
                    blocks[kind, h, b] = both
                    wide[kind, (h * GROUPS + b) * 2 * ROWS : (h * GROUPS + b + 1) * 2 * ROWS, here] = both
        for half in range(2):
            for slot, (h, t, b) in enumerate(LEFT[half]):
                carries = jnp.broadcast_to(panel[t : t + 1, here], (2 * ROWS, step)).astype(F32).astype(BF16)
                left[half, slot * 2 * ROWS : (slot + 1) * 2 * ROWS, here] = blocks[1 - half, h, b] * carries

    def product(a, b):
        return lax.dot_general(a, b, (((1,), (1,)), ((), ())), preferred_element_type=F32)

    lane = iota((ROWS, LANES), 1)
    first = lane % (2 * ROWS) < ROWS

    def rows_of(acc, slot):
        return acc[slot * 2 * ROWS : slot * 2 * ROWS + ROWS] + acc[slot * 2 * ROWS + ROWS : (slot + 1) * 2 * ROWS]

    def fold(a, b):
        return jnp.where(first, a + pltpu.roll(a, LANES - ROWS, 1), b + pltpu.roll(b, ROWS, 1))

    def both_targets(acc, slots):
        return jnp.where(lane < HALF, rows_of(acc, slots[0]), rows_of(acc, slots[1]))

    for half in range(2):
        sums_t = product(left[half], wide[half])
        tiles = {
            (t, b): both_targets(sums_t, [LEFT_AT[half][h, t, b] for h in range(2)]) for h, t, b in LEFT[half] if h == 0
        }
        short, long = near_markers(half)
        pairs = [((short[2 * q], 0), (short[2 * q + 1], 0)) for q in range(ROWS // 2)]
        pairs += [((t, 0), (t, 1)) for t in long]
        for q, pair in enumerate(pairs):
            a, b = (tiles[t, left_blocks(t)[depth]] for t, depth in pair)
            t_ref[half, q * ROWS : (q + 1) * ROWS, :] = fold(a, b)
    sums_e = product(wide[1], wide[0])
    tiles = [both_targets(sums_e, [b, GROUPS + b]) for b in range(GROUPS)]
    for q in range(GROUPS // 2):
        em_ref[q * ROWS : (q + 1) * ROWS, :] = fold(tiles[2 * q], tiles[2 * q + 1])


def near_markers(half):
    outer, inner = (0, 1) if half == 0 else (GROUPS - 1, GROUPS - 2)
    return [outer * ROWS + i for i in range(ROWS)], [inner * ROWS + i for i in range(ROWS)]


def finish_kernel(panel_size, copies, sum_ref, dose_ref, log_ref):
    place = lax.axis_index("group")
    row, lane = iota((ROWS, LANES), 0), iota((ROWS, LANES), 1)
    target = lane // HALF
    folded = (lane % (2 * ROWS)) // ROWS
    misc = sum_ref[TALL + GROUPS // 2 * ROWS :, :] * (1.0 / copies)
    wide = LANES // GROUPS

    def spread(tile, at):
        return jnp.broadcast_to(tile[:, at : at + 1], (ROWS, LANES))

    rates = [spread(misc, b * wide) for b in range(GROUPS)]
    odds = [rate / (1.0 - rate) for rate in rates]
    inverse = 1.0 / panel_size
    ahead = []
    for b in range(GROUPS):
        following = odds[b + 1][0:1, :] if b + 1 < GROUPS else jnp.ones((1, LANES), F32)
        ahead.append(jnp.concatenate([odds[b][1:, :], following], axis=0) * inverse)
    behind = [odd * inverse for odd in odds]

    pair = sum_ref[TALL : TALL + GROUPS // 2 * ROWS, :]
    trail_tiles = []
    for q in range(GROUPS // 2):
        factor = jnp.where(folded == 0, behind[2 * q], behind[2 * q + 1])
        trail_tiles.append(pair[q * ROWS : (q + 1) * ROWS] * factor)
    square = jnp.concatenate([pair, jnp.zeros((LANES - pair.shape[0], LANES), F32)], axis=0)
    turned = jnp.transpose(square)

    def turned_tile(h, b, f):
        at = h * HALF + b * 2 * ROWS + f * ROWS
        return turned[at : at + ROWS] * ahead[b]

    lead_tiles = {(h, b, f): turned_tile(h, b, f) for h in range(2) for b in range(GROUPS) for f in range(2)}

    def lead_column(t, b):
        s, at = t // ROWS, (t // ROWS // 2) * ROWS + t % ROWS
        return jnp.where(target == 0, spread(lead_tiles[0, b, s % 2], at), spread(lead_tiles[1, b, s % 2], at))

    def trail_column(t, b):
        at = 2 * ROWS * (t // ROWS) + t % ROWS + ROWS * (b % 2)
        tile = trail_tiles[b // 2]
        return jnp.where(target == 0, spread(tile, at), spread(tile, HALF + at))

    zero = jnp.zeros((ROWS, LANES), F32)
    lead, trail, starts, ends = [zero] * GROUPS, [zero] * GROUPS, [zero] * GROUPS, [zero] * GROUPS
    v = jnp.ones((ROWS, LANES), F32)
    z = jnp.ones((ROWS, LANES), F32)
    for t in range(MARKERS):
        u = MARKERS - 1 - t
        bt, bu = t // ROWS, u // ROWS
        starts[bt] = jnp.where(row == t % ROWS, v, starts[bt])
        ends[bu] = jnp.where(row == u % ROWS, z, ends[bu])
        for b in range(bt, GROUPS):
            lead[b] = lead[b] + v * lead_column(t, b)
        for b in range(bu + 1):
            trail[b] = trail[b] + z * trail_column(u, b)
        v = jnp.broadcast_to(lead[bt][t % ROWS : t % ROWS + 1, :], (ROWS, LANES))
        z = jnp.broadcast_to(trail[bu][u % ROWS : u % ROWS + 1, :], (ROWS, LANES))
    total = v

    low = place < GROUPS // 2
    side = jnp.where(low, 1, -1)
    inner = lane % HALF
    near = [jnp.where(low, starts[b], ends[GROUPS - 1 - b]) for b in range(2)]
    across = [jnp.where(low, ends[b], starts[b]) for b in range(GROUPS)]
    picked = across[GROUPS - 1]
    for b in range(GROUPS - 1):
        picked = jnp.where(inner // (2 * ROWS) == b, across[b], picked)
    picked = jnp.where(row == lane % ROWS, picked, 0.0)
    across = jnp.sum(picked, axis=0, keepdims=True)
    far_end = ROWS * (inner // (2 * ROWS)) + lane % ROWS
    scale = inverse / total[0:1, :]

    def inside(t, near_end):
        return ((near_end - t) * side <= 0) & ((far_end - t) * side >= 0)

    def put(rows_of_t):
        doses = []
        for h in range(2):
            dose = jnp.sum(jnp.where(target == h, rows_of_t * scale, 0.0), axis=1, keepdims=True)
            doses.append(jnp.sum(jnp.where(row == lane, dose, 0.0), axis=0, keepdims=True))
        dose_ref[...] = jnp.concatenate(doses, axis=0)[:, :ROWS]

    outermost = (place == 0) | (place == GROUPS - 1)

    @pl.when(outermost)
    def _():
        weight = near[0] * across
        near_end = place * ROWS + row
        merged = zero
        for q in range(ROWS // 2):
            t = place * ROWS + 2 * q + folded
            tile = jnp.where(inside(t, near_end), sum_ref[q * ROWS : (q + 1) * ROWS, :] * weight, 0.0)
            tile = jnp.sum(tile, axis=0, keepdims=True)
            merged = jnp.where(row // 2 == q, jnp.where(folded == row % 2, tile, 0.0), merged)
        put(merged)

    @pl.when(jnp.logical_not(outermost))
    def _():
        weight = jnp.where(folded == 0, near[0], near[1]) * across
        near_end = jnp.where(low, folded, GROUPS - 1 - folded) * ROWS + row
        merged = zero
        for q in range(ROWS):
            at = SHORT_TALL + q * ROWS
            tile = jnp.where(inside(place * ROWS + q, near_end), sum_ref[at : at + ROWS, :] * weight, 0.0)
            merged = jnp.where(row == q, jnp.sum(tile, axis=0, keepdims=True), merged)
        put(merged)

    counts = jnp.sum(misc, axis=0, keepdims=True)
    stay = [jnp.log(1.0 - rate) for rate in rates]
    stay[0] = jnp.where(row == 0, 0.0, stay[0])
    stay = jnp.sum(sum(stay), axis=0, keepdims=True)
    logs = []
    for h in range(2):
        seen = sum(counts[:, b * wide + (2 + h) * ROWS : b * wide + (2 + h) * ROWS + 1] for b in range(GROUPS))
        whole = jnp.log(total[0:1, h * HALF : h * HALF + 1]) + stay[:, 0:1] + seen * math.log(SCALE)
        logs.append(whole * (1.0 / MARKERS))
    log_ref[...] = jnp.concatenate(logs, axis=1)


def exchange(x, axis, by):
    peers = lax.axis_size(axis)
    return lax.ppermute(x, axis, [(i, i ^ by) for i in range(peers)])


def exchange_crossed(x, by):
    copies = lax.axis_size("batch")
    peers = lax.axis_size("group") * copies
    return lax.ppermute(x, ("group", "batch"), [(i, i ^ (copies + by)) for i in range(peers)])


def on_device_windows(panel_alleles, recomb_rates, genotypes):
    width = panel_alleles.shape[1]
    copies = lax.axis_size("batch")
    chunk = width // GROUPS
    place = lax.axis_index("group")
    part = chunk // PARTS
    tagged = jax.ShapeDtypeStruct((ROWS, part + LANES), jnp.int32)
    plain = jax.ShapeDtypeStruct((ROWS, part), jnp.int32)
    shapes = [tagged if p == 0 else plain for p in range(PARTS) for d in range(GROUPS)]
    *cuts, misc = pl.pallas_call(
        functools.partial(pack_kernel, PARTS),
        out_shape=shapes + [jax.ShapeDtypeStruct((ROWS, LANES), F32)],
        in_specs=[pl.BlockSpec(memory_space=pltpu.HBM)] * 3,
        out_specs=[VMEM] * (len(shapes) + 1),
        scratch_shapes=[
            pltpu.SMEM(genotypes.shape, jnp.int32),
            pltpu.SMEM(recomb_rates.shape, F32),
            pltpu.SemaphoreType.DMA((len(shapes) + 2,)),
        ],
        compiler_params=pltpu.CompilerParams(vmem_limit_bytes=4 * 1024 * 1024),
        name="pack",
    )(*(pltpu.with_memory_space_constraint(x, pltpu.HBM) for x in (genotypes, recomb_rates, panel_alleles)))
    cuts = [cut if n % GROUPS == 0 else exchange(cut, "group", n % GROUPS) for n, cut in enumerate(cuts)]
    tags = [cut[:, part:] for cut in cuts[:GROUPS]]
    sums = []
    for p in range(PARTS):
        pieces = [cut[:, :part] for cut in cuts[p * GROUPS : (p + 1) * GROUPS]]
        sums.append(
            pl.pallas_call(
                functools.partial(window_kernel, min(512, part)),
                out_shape=[
                    jax.ShapeDtypeStruct((2, TALL, LANES), F32),
                    jax.ShapeDtypeStruct((PAIRS, LANES), F32),
                ],
                in_specs=[VMEM] * (2 * GROUPS),
                out_specs=[VMEM] * 2,
                scratch_shapes=[
                    pltpu.VMEM((MARKERS, part), jnp.int32),
                    pltpu.VMEM((MARKERS, LANES), jnp.int32),
                    pltpu.VMEM((2, 4 * MARKERS, part), BF16),
                    pltpu.VMEM((2, len(LEFT[0]) * 2 * ROWS, part), BF16),
                ],
                compiler_params=pltpu.CompilerParams(vmem_limit_bytes=40 * 1024 * 1024),
                cost_estimate=pl.CostEstimate(flops=part * 900000, bytes_accessed=0, transcendentals=0),
                name="windows",
            )(*pieces, *tags)
        )
    sums_t, sums_e = (sum(each) for each in zip(*sums))

    sent = jnp.concatenate([sums_t[0], sums_e, misc, sums_t[1]], axis=0)
    both = sent + exchange(sent, "group", 1)
    low = place < GROUPS // 2
    upper, lower = both[: TALL + EXTRA], both[TALL:]
    lower = jnp.concatenate([lower[EXTRA:], lower[:EXTRA]], axis=0)
    kept = jnp.where(low, upper, lower) + exchange(jnp.where(low, lower, upper), "group", 3)
    by = 1
    while by < copies:
        kept = kept + exchange_crossed(kept, by)
        by *= 2
    dosage, logs = pl.pallas_call(
        functools.partial(finish_kernel, float(width * copies), float(copies)),
        out_shape=[jax.ShapeDtypeStruct((2, ROWS), F32), jax.ShapeDtypeStruct((1, 2), F32)],
        in_specs=[VMEM],
        out_specs=[VMEM] * 2,
        compiler_params=pltpu.CompilerParams(vmem_limit_bytes=4 * 1024 * 1024),
        name="finish",
    )(kept)
    return dosage, logs.reshape(2)


def fits_windows(panel_alleles, genotypes, groups, copies):
    markers, width = panel_alleles.shape
    return (
        groups == GROUPS
        and copies & (copies - 1) == 0
        and markers == ROWS
        and genotypes.shape[0] == 2
        and width % (GROUPS * LANES * 4) == 0
    )


def on_device(panel_alleles, recomb_rates, genotypes):
    groups, copies = lax.axis_size("group"), lax.axis_size("batch")
    if fits_windows(panel_alleles, genotypes, groups, copies):
        return on_device_windows(panel_alleles, recomb_rates, genotypes)
    return on_device_chain(panel_alleles, recomb_rates, genotypes)


def solution(mesh):
    placed = (P("group", "batch"), P("group"), P(None, "group"))
    return jax.shard_map(
        on_device, mesh=mesh, in_specs=placed, out_specs=(P(None, "group"), P()), check_vma=False
    )
```

```python
import functools
import math

import jax
import jax.numpy as jnp
from jax import lax
from jax.experimental import pallas as pl
from jax.experimental.pallas import tpu as pltpu
from jax.sharding import PartitionSpec as P

MISMATCH = 0.05
HIGHEST = lax.Precision.HIGHEST


def haplotypes(panel_rows):
    return panel_rows.shape[1] * lax.axis_size("batch")


def from_behind(x, axis, by):
    peers = lax.axis_size(axis)
    pairs = [(i, i + by) for i in range(peers) if 0 <= i + by < peers]
    return lax.ppermute(x, axis, pairs)


def emission(panel_rows, geno_col):
    observed = geno_col[:, None]
    agrees = jnp.where(panel_rows == observed, 1.0 - MISMATCH, MISMATCH)
    return jnp.where(observed == 2, 1.0, agrees).astype(jnp.float32)


def forward_terms(panel_rows, geno_col, switches):
    emitted = emission(panel_rows, geno_col)
    retain = emitted * (1.0 - switches)[:, None]
    inject = emitted * (switches / haplotypes(panel_rows))[:, None]
    return (retain, inject, None)


def backward_terms(panel_rows, geno_col, switches):
    emitted = emission(panel_rows, geno_col)[::-1]
    flipped = switches[::-1]
    retain = emitted * (1.0 - flipped)[:, None]
    inject = jnp.broadcast_to((flipped / haplotypes(panel_rows))[:, None], emitted.shape)
    return (retain, inject, emitted)


def partial_sums(entering, retain, inject, weight, extent):
    logs = jnp.cumsum(jnp.log(retain), axis=0)
    shifted = jnp.concatenate([jnp.zeros_like(entering)[None], logs[: extent - 1]], axis=0)
    before = jnp.exp(shifted)
    left_side = before if weight is None else weight * before
    leading = jnp.einsum("jk,k->j", left_side, entering, precision=HIGHEST)
    anchor = shifted[0]
    right_side = inject * jnp.exp(anchor[None] - logs)
    nearby = jnp.exp(jnp.minimum(shifted - anchor[None], 0.0))
    nearby = nearby if weight is None else weight * nearby
    columns = [jnp.einsum("jk,tk->jt", nearby, right_side, precision=HIGHEST)]
    coupling = jnp.concatenate(columns, axis=1)
    return (leading, coupling)


def solve_sums(leading, coupling):
    columns = coupling.shape[1]

    def settle(marker, sigmas):
        below = jnp.arange(columns) < marker
        update = leading[marker] + jnp.sum(
            jnp.where(below, coupling[marker] * sigmas[:columns], 0.0)
        )
        return sigmas.at[marker].set(update)

    return lax.fori_loop(0, leading.shape[0], settle, jnp.zeros_like(leading))


def advance(entering, retain, inject, sigmas, keep_states):

    def advance_single(current, pieces):
        current = pieces[0] * current + pieces[1] * pieces[2]
        return (current, current if keep_states else None)

    return lax.scan(advance_single, entering, (retain, inject, sigmas[: retain.shape[0]]))


def place_rows(store, block, active):
    return jnp.where(active, block, store)


def on_device_chain(panel_alleles, recomb_rates, genotypes):
    chain_size = lax.axis_size("group")
    position = lax.axis_index("group")
    markers, width = panel_alleles.shape
    targets = genotypes.shape[0]
    bundles = targets // targets
    uniform = jnp.full((targets, width), 1.0 / haplotypes(panel_alleles), jnp.float32)
    first_row = position == 0
    last_row = position == chain_size - 1

    def local_sums(active, arrivals, geno_rows, maker, extent):

        def local_compute():

            def local_single(pieces):
                retain, inject, weight = maker(panel_alleles, pieces[1], recomb_rates)
                return partial_sums(pieces[0], retain, inject, weight, extent)

            return lax.map(local_single, (arrivals, geno_rows))

        def local_skipped():
            return (
                jnp.zeros((targets, extent), jnp.float32),
                jnp.zeros((targets, extent, markers), jnp.float32),
            )

        return lax.cond(active, local_compute, local_skipped)

    def outgoing(active, arrivals, geno_rows, sigmas, maker, scale_row):

        def outgoing_compute():

            def outgoing_single(pieces):
                retain, inject, weight = maker(panel_alleles, pieces[1], recomb_rates)
                ending, unused = advance(pieces[0], retain, inject, pieces[2], False)
                return ending / pieces[2][scale_row]

            return lax.map(outgoing_single, (arrivals, geno_rows, sigmas))

        def outgoing_skipped():
            return jnp.zeros((targets, width), jnp.float32)

        return lax.cond(active, outgoing_compute, outgoing_skipped)

    def moment_step(moment, carried_state):
        (
            sent_forward,
            sent_backward,
            sent_running,
            store_forward,
            store_backward,
            sigma_forward,
            sigma_backward,
            log_terms,
        ) = carried_state
        got_forward = from_behind(sent_forward, "group", 1)
        got_backward = from_behind(sent_backward, "group", -1)
        entering_forward = jnp.where(first_row, uniform, got_forward)
        entering_backward = jnp.where(last_row, uniform, got_backward)
        index_forward = moment - position
        index_backward = moment - (chain_size - 1 - position)
        active_forward = (index_forward >= 0) & (index_forward < bundles)
        active_backward = (index_backward >= 0) & (index_backward < bundles)
        lead_forward, couple_forward = local_sums(
            active_forward, entering_forward, genotypes, forward_terms, markers + 1
        )
        lead_backward, couple_backward = local_sums(
            active_backward, entering_backward, genotypes, backward_terms, markers
        )
        lead_forward, couple_forward, lead_backward, couple_backward = lax.psum(
            (lead_forward, couple_forward, lead_backward, couple_backward), "batch"
        )
        sigmas_forward = jax.vmap(solve_sums)(lead_forward, couple_forward)
        sigmas_backward = jax.vmap(solve_sums)(lead_backward, couple_backward)
        next_forward = outgoing(
            active_forward, entering_forward, genotypes, sigmas_forward, forward_terms, markers
        )
        next_backward = outgoing(
            active_backward,
            entering_backward,
            genotypes,
            sigmas_backward,
            backward_terms,
            markers - 1,
        )
        guarded = jnp.where(active_forward, sigmas_forward[:, markers], 1.0)
        running = jnp.log(guarded)
        store_forward = place_rows(store_forward, entering_forward, active_forward)
        store_backward = place_rows(store_backward, entering_backward, active_backward)
        sigma_forward = place_rows(sigma_forward, sigmas_forward, active_forward)
        sigma_backward = place_rows(sigma_backward, sigmas_backward, active_backward)
        log_terms = place_rows(log_terms, running, active_forward)
        return (
            next_forward,
            next_backward,
            running,
            store_forward,
            store_backward,
            sigma_forward,
            sigma_backward,
            log_terms,
        )

    initial = (
        jnp.zeros((targets, width), jnp.float32),
        jnp.zeros((targets, width), jnp.float32),
        jnp.zeros((targets,), jnp.float32),
        jnp.zeros((targets, width), jnp.float32),
        jnp.zeros((targets, width), jnp.float32),
        jnp.zeros((targets, markers + 1), jnp.float32),
        jnp.zeros((targets, markers), jnp.float32),
        jnp.zeros((targets,), jnp.float32),
    )
    final_state = lax.fori_loop(0, chain_size + bundles - 1, moment_step, initial)
    store_forward, store_backward, sigma_forward, sigma_backward, log_terms = final_state[3:]
    whole_log = lax.psum(log_terms, "group")
    log_likelihood = whole_log / (markers * chain_size)

    def posterior(pieces):
        entering_ahead, entering_behind, geno_col, sigmas_ahead, sigmas_behind = pieces
        retain, inject, weight = forward_terms(panel_alleles, geno_col, recomb_rates)
        unused_f, forward_states = advance(entering_ahead, retain, inject, sigmas_ahead, True)
        forward_rows = forward_states / sigmas_ahead[1:, None]
        retain, inject, weight = backward_terms(panel_alleles, geno_col, recomb_rates)
        unused_b, backward_states = advance(entering_behind, retain, inject, sigmas_behind, True)
        scaled_back = backward_states[:-1] / sigmas_behind[:-1, None]
        backward_rows = jnp.concatenate([entering_behind[None], scaled_back], axis=0)[::-1]
        product = forward_rows * backward_rows
        numerator = jnp.sum(jnp.where(panel_alleles == 1, product, 0.0), axis=1)
        return (numerator, jnp.sum(product, axis=1))

    numerator, denominator = lax.map(
        posterior, (store_forward, store_backward, genotypes, sigma_forward, sigma_backward)
    )
    numerator, denominator = lax.psum((numerator, denominator), "batch")
    return (numerator / denominator, log_likelihood)


ROWS, LANES = 8, 128
HALF = LANES // 2
GROUPS = 4
PARTS = 2
MISSING = 2
SCALE = math.sqrt(MISMATCH * (1.0 - MISMATCH))
HALF_STEP = 0.5 * math.log((1.0 - MISMATCH) / MISMATCH)
VMEM = pl.BlockSpec(memory_space=pltpu.VMEM)
SMEM = pl.BlockSpec(memory_space=pltpu.SMEM)
F32, BF16 = jnp.float32, jnp.bfloat16


def iota(shape, axis):
    return lax.broadcasted_iota(jnp.int32, shape, axis)


def left_blocks(t):
    b = t // ROWS
    return list(range(b + 1)) if b < GROUPS // 2 else list(range(GROUPS - 1, b - 1, -1))


MARKERS = ROWS * GROUPS
HALF_T = MARKERS // 2
LEFT = [
    [(h, t, b) for t in range(half * HALF_T, (half + 1) * HALF_T) for b in left_blocks(t) for h in range(2)]
    for half in range(2)
]
LEFT_AT = [{entry: slot for slot, entry in enumerate(LEFT[half])} for half in range(2)]
PAIRS = GROUPS // 2 * ROWS
SUBSET = 5 * ROWS
TALL = 2 * SUBSET
TRIANGLES = [(0, 1), (2, 3), (7, -1)]
MISC = ROWS


def pack_kernel(parts, geno_ref, rate_ref, panel_ref, *refs):
    outs, (misc_ref, genos, rates_in, sems) = refs[:-4], refs[-4:]
    place = lax.axis_index("group")
    chunk = panel_ref.shape[1] // GROUPS
    part = chunk // parts
    copies = []
    for n, ref in enumerate(outs):
        d, p = n % GROUPS, n // GROUPS
        start = pl.multiple_of((place ^ d) * chunk + p * part, LANES)
        copies.append(
            pltpu.make_async_copy(panel_ref.at[:, pl.ds(start, part)], ref.at[:, pl.ds(0, part)], sems.at[n])
        )
    small = [
        pltpu.make_async_copy(geno_ref, genos, sems.at[len(outs)]),
        pltpu.make_async_copy(rate_ref, rates_in, sems.at[len(outs) + 1]),
    ]
    for copy in small + copies:
        copy.start()
    for copy in small:
        copy.wait()
    row, lane = iota((ROWS, LANES), 0), iota((ROWS, LANES), 1)
    tile = jnp.zeros((ROWS, LANES), jnp.int32)
    rates = jnp.zeros((ROWS, LANES), F32)
    for i in range(ROWS):
        tile = jnp.where(row == i, jnp.where(lane < HALF, genos[0, i], genos[1, i]), tile)
        rates = jnp.where(row == i, rates_in[i], rates)
    for ref in outs[:GROUPS]:
        ref[:, part:] = tile
    known = jnp.where(tile == MISSING, 0.0, 1.0)
    misc = jnp.where(lane == MISC + place, rates, 0.0)
    misc = jnp.where((lane == MISC + GROUPS + place) | (lane == HALF + MISC + place), known, misc)
    misc_ref[...] = misc
    for copy in copies:
        copy.wait()


def window_kernel(step, *refs):
    pieces, geno_refs = refs[:GROUPS], refs[GROUPS : 2 * GROUPS]
    t_ref, em_ref, panel, genos, wide, left = refs[2 * GROUPS :]
    place = lax.axis_index("group")
    columns = panel.shape[1]
    for d in range(GROUPS):
        rows = pl.ds(pl.multiple_of((place ^ d) * ROWS, ROWS), ROWS)
        panel[rows, :] = pieces[d][...]
        genos[rows, :] = geno_refs[d][...]

    r, j = iota((4 * MARKERS, 2 * MARKERS), 0), iota((4 * MARKERS, 2 * MARKERS), 1)
    same = r // (2 * MARKERS) == j // MARKERS
    prefix, marker = (r // MARKERS) % 2 == 0, r % MARKERS
    at = j % MARKERS
    sums = jnp.where(prefix, jnp.where(at <= marker, 1.0, 0.0), jnp.where(at < marker, -1.0, 0.0))
    sums = jnp.where(same, sums, 0.0).astype(BF16)

    for start in range(0, columns, step):
        here = slice(start, start + step)
        signs = []
        for h in range(2):
            for b in range(GROUPS):
                rows = slice(b * ROWS, (b + 1) * ROWS)
                seen = genos[rows, h * HALF : h * HALF + 1]
                agrees = jnp.where(panel[rows, here] == seen, 1.0, -1.0)
                signs.append(jnp.where(seen == MISSING, 0.0, agrees))
        signs = jnp.concatenate(signs, axis=0).astype(BF16)
        power = jnp.dot(sums, signs, preferred_element_type=F32)
        value = jnp.exp(power * HALF_STEP)
        upper = value.astype(BF16).astype(F32)
        lower = value - upper
        blocks = {}
        for h in range(2):
            for kind in range(2):
                for b in range(GROUPS):
                    at = h * 2 * MARKERS + kind * MARKERS + b * ROWS
                    both = jnp.concatenate([upper[at : at + ROWS], lower[at : at + ROWS]], axis=0).astype(BF16)
                    blocks[kind, h, b] = both
                    wide[kind, (h * GROUPS + b) * 2 * ROWS : (h * GROUPS + b + 1) * 2 * ROWS, here] = both
        for half in range(2):
            for slot, (h, t, b) in enumerate(LEFT[half]):
                carries = jnp.broadcast_to(panel[t : t + 1, here], (2 * ROWS, step)).astype(F32).astype(BF16)
                left[half, slot * 2 * ROWS : (slot + 1) * 2 * ROWS, here] = blocks[1 - half, h, b] * carries

    def product(a, b):
        return lax.dot_general(a, b, (((1,), (1,)), ((), ())), preferred_element_type=F32)

    lane = iota((ROWS, LANES), 1)
    first = lane % (2 * ROWS) < ROWS

    def rows_of(acc, slot):
        return acc[slot * 2 * ROWS : slot * 2 * ROWS + ROWS] + acc[slot * 2 * ROWS + ROWS : (slot + 1) * 2 * ROWS]

    def fold(a, b):
        return jnp.where(first, a + pltpu.roll(a, LANES - ROWS, 1), b + pltpu.roll(b, ROWS, 1))

    def both_targets(acc, slots):
        return jnp.where(lane < HALF, rows_of(acc, slots[0]), rows_of(acc, slots[1]))

    row = iota((ROWS, LANES), 0)
    for half in range(2):
        sums_t = product(left[half], wide[half])

        def tile(block, j, depth):
            t = block * ROWS + (j if half == 0 else ROWS - 1 - j)
            b = left_blocks(t)[depth]
            return both_targets(sums_t, [LEFT_AT[half][h, t, b] for h in range(2)])

        def triangle(block, depth, a):
            if a < 0:
                return jnp.zeros((ROWS, LANES), F32)
            one = tile(block, a, depth)
            if a > 2:
                return one
            other = tile(block, ROWS - 2 - a, depth)
            if half == 0:
                return jnp.where(row <= a, one, pltpu.roll(other, a + 1, 0))
            return jnp.where(row >= ROWS - 1 - a, one, pltpu.roll(other, ROWS - 1 - a, 0))

        blocks = [0, 1] if half == 0 else [GROUPS - 1, GROUPS - 2]
        for subset in range(2):
            rows = [fold(*(triangle(blocks[subset], subset, a) for a in pair)) for pair in TRIANGLES]
            squares = [tile(blocks[1], subset * ROWS // 2 + j, 0) for j in range(ROWS // 2)]
            rows += [fold(squares[0], squares[1]), fold(squares[2], squares[3])]
            for q, value in enumerate(rows):
                at = subset * SUBSET + q * ROWS
                t_ref[half, at : at + ROWS, :] = value
    sums_e = product(wide[1], wide[0])
    tiles = [both_targets(sums_e, [b, GROUPS + b]) for b in range(GROUPS)]
    for q in range(GROUPS // 2):
        em_ref[q * ROWS : (q + 1) * ROWS, :] = fold(tiles[2 * q], tiles[2 * q + 1])


def solve_kernel(panel_size, copies, sum_ref, ends_ref, log_ref):
    row, lane = iota((ROWS, LANES), 0), iota((ROWS, LANES), 1)
    target = lane // HALF
    folded = (lane % (2 * ROWS)) // ROWS
    misc = sum_ref[:ROWS, :] * (1.0 / copies)

    def spread(tile, at):
        return jnp.broadcast_to(tile[:, at : at + 1], (ROWS, LANES))

    rates = [spread(misc, MISC + b) for b in range(GROUPS)]
    odds = [rate / (1.0 - rate) for rate in rates]
    inverse = 1.0 / panel_size
    ahead = []
    for b in range(GROUPS):
        following = odds[b + 1][0:1, :] if b + 1 < GROUPS else jnp.ones((1, LANES), F32)
        ahead.append(jnp.concatenate([odds[b][1:, :], following], axis=0) * inverse)
    behind = [odd * inverse for odd in odds]

    pair = sum_ref[...]
    trail_tiles = []
    for q in range(GROUPS // 2):
        factor = jnp.where(folded == 0, behind[2 * q], behind[2 * q + 1])
        trail_tiles.append(pair[q * ROWS : (q + 1) * ROWS] * factor)
    square = jnp.concatenate([pair, jnp.zeros((LANES - pair.shape[0], LANES), F32)], axis=0)
    turned = jnp.transpose(square)

    def turned_tile(h, b, f):
        at = h * HALF + b * 2 * ROWS + f * ROWS
        return turned[at : at + ROWS] * ahead[b]

    lead_tiles = {(h, b, f): turned_tile(h, b, f) for h in range(2) for b in range(GROUPS) for f in range(2)}

    def lead_column(t, b):
        s, at = t // ROWS, (t // ROWS // 2) * ROWS + t % ROWS
        return jnp.where(target == 0, spread(lead_tiles[0, b, s % 2], at), spread(lead_tiles[1, b, s % 2], at))

    def trail_column(t, b):
        at = 2 * ROWS * (t // ROWS) + t % ROWS + ROWS * (b % 2)
        tile = trail_tiles[b // 2]
        return jnp.where(target == 0, spread(tile, at), spread(tile, HALF + at))

    zero = jnp.zeros((ROWS, LANES), F32)
    lead, trail, starts, ends = [zero] * GROUPS, [zero] * GROUPS, [zero] * GROUPS, [zero] * GROUPS
    v = jnp.ones((ROWS, LANES), F32)
    z = jnp.ones((ROWS, LANES), F32)
    for t in range(MARKERS):
        u = MARKERS - 1 - t
        bt, bu = t // ROWS, u // ROWS
        starts[bt] = jnp.where(row == t % ROWS, v, starts[bt])
        ends[bu] = jnp.where(row == u % ROWS, z, ends[bu])
        for b in range(bt, GROUPS):
            lead[b] = lead[b] + v * lead_column(t, b)
        for b in range(bu + 1):
            trail[b] = trail[b] + z * trail_column(u, b)
        v = jnp.broadcast_to(lead[bt][t % ROWS : t % ROWS + 1, :], (ROWS, LANES))
        z = jnp.broadcast_to(trail[bu][u % ROWS : u % ROWS + 1, :], (ROWS, LANES))
    for b in range(GROUPS):
        ends_ref[b * ROWS : (b + 1) * ROWS, :] = starts[b]
        ends_ref[MARKERS + b * ROWS : MARKERS + (b + 1) * ROWS, :] = ends[b]
    ends_ref[2 * MARKERS :, :] = inverse / v

    stay = [jnp.log(1.0 - rate) for rate in rates]
    stay[0] = jnp.where(row == 0, 0.0, stay[0])
    stay = jnp.sum(sum(stay), axis=0, keepdims=True)
    counts = jnp.sum(misc, axis=0, keepdims=True)
    logs = []
    for h, at in enumerate((MISC + GROUPS, HALF + MISC)):
        seen = sum(counts[:, at + b : at + b + 1] for b in range(GROUPS))
        whole = jnp.log(v[0:1, h * HALF : h * HALF + 1]) + stay[:, 0:1] + seen * math.log(SCALE)
        logs.append(whole * (1.0 / MARKERS))
    log_ref[...] = jnp.concatenate(logs, axis=1)


def contract_kernel(weight_ref, t_ref, dose_ref):
    place = lax.axis_index("group")
    low = place < GROUPS // 2
    inward = (place == 1) | (place == GROUPS - 2)
    row, lane = iota((ROWS, LANES), 0), iota((ROWS, LANES), 1)
    folded = (lane % (2 * ROWS)) // ROWS
    side = jnp.where(low, 1, -1)
    turn = jnp.where(low, 0, ROWS - 1)
    order = turn + side * row

    def weights(is_start, block):
        at = jnp.where(is_start, 0, MARKERS) + block * ROWS
        return weight_ref[pl.ds(pl.multiple_of(at, ROWS), ROWS), :]

    picked = weights(jnp.logical_not(low), GROUPS - 1)
    column = (lane % HALF) // (2 * ROWS)
    for b in range(GROUPS - 1):
        picked = jnp.where(column == b, weights(jnp.logical_not(low), b), picked)
    picked = jnp.where(row == lane % ROWS, picked, 0.0)
    across = jnp.sum(picked, axis=0, keepdims=True) * weight_ref[2 * MARKERS : 2 * MARKERS + 1, :]
    far_end = ROWS * column + lane % ROWS

    def reaches(j):
        t = place * ROWS + turn + side * j
        return (far_end - t) * side >= 0

    near = weights(low, place)
    base = jnp.where(inward, SUBSET, 0)
    total = jnp.zeros((ROWS, LANES), F32)
    for q, (a0, a1) in enumerate(TRIANGLES):
        a = jnp.where(folded == 0, a0, a1)
        own = order <= a
        paired = (a >= 0) & (a < 3)
        moved = []
        for each in (a0, a1):
            if 0 <= each < 3:
                moved.append(jnp.where(low, pltpu.roll(near, each + 1, 0), pltpu.roll(near, ROWS - 1 - each, 0)))
            else:
                moved.append(near)
        weight = jnp.where(own, near, jnp.where(folded == 0, moved[0], moved[1])) * across
        data = t_ref[pl.ds(pl.multiple_of(base + q * ROWS, ROWS), ROWS), :]
        valid = (own | paired) & reaches(jnp.where(own, a, ROWS - 2 - a))
        terms = jnp.where(valid, data * weight, 0.0)
        one = jnp.sum(jnp.where(own, terms, 0.0), axis=0, keepdims=True)
        other = jnp.sum(jnp.where(own, 0.0, terms), axis=0, keepdims=True)
        total = total + jnp.where(row == a, one, 0.0)
        total = total + jnp.where(paired & (row == ROWS - 2 - a), other, 0.0)
    outermost = weights(low, jnp.where(low, 0, GROUPS - 1)) * jnp.where(inward, 1.0, 0.0) * across
    for subset in range(2):
        for q in range(ROWS // 4):
            j = subset * ROWS // 2 + 2 * q + folded
            at = subset * SUBSET + (len(TRIANGLES) + q) * ROWS
            terms = jnp.where(reaches(j), t_ref[at : at + ROWS, :] * outermost, 0.0)
            total = total + jnp.where(row == j, jnp.sum(terms, axis=0, keepdims=True), 0.0)
    doses = []
    for h in range(2):
        dose = jnp.sum(jnp.where(lane // HALF == h, total, 0.0), axis=1, keepdims=True)
        doses.append(jnp.sum(jnp.where(order == lane, dose, 0.0), axis=0, keepdims=True))
    dose_ref[...] = jnp.concatenate(doses, axis=0)[:, :ROWS]


def exchange(x, axis, by):
    peers = lax.axis_size(axis)
    return lax.ppermute(x, axis, [(i, i ^ by) for i in range(peers)])


def exchange_flat(x, by):
    peers = lax.axis_size("group") * lax.axis_size("batch")
    return lax.ppermute(x, ("group", "batch"), [(i, i ^ by) for i in range(peers)])


def is_odd(bits):
    odd = bits
    for shift in (16, 8, 4, 2, 1):
        odd = odd ^ (odd >> shift)
    return odd & 1


def on_device_windows(panel_alleles, recomb_rates, genotypes):
    width = panel_alleles.shape[1]
    copies = lax.axis_size("batch")
    chunk = width // GROUPS
    place = lax.axis_index("group")
    part = chunk // PARTS
    tagged = jax.ShapeDtypeStruct((ROWS, part + LANES), jnp.int32)
    plain = jax.ShapeDtypeStruct((ROWS, part), jnp.int32)
    shapes = [tagged if p == 0 else plain for p in range(PARTS) for d in range(GROUPS)]
    *cuts, misc = pl.pallas_call(
        functools.partial(pack_kernel, PARTS),
        out_shape=shapes + [jax.ShapeDtypeStruct((ROWS, LANES), F32)],
        in_specs=[pl.BlockSpec(memory_space=pltpu.HBM)] * 3,
        out_specs=[VMEM] * (len(shapes) + 1),
        scratch_shapes=[
            pltpu.SMEM(genotypes.shape, jnp.int32),
            pltpu.SMEM(recomb_rates.shape, F32),
            pltpu.SemaphoreType.DMA((len(shapes) + 2,)),
        ],
        compiler_params=pltpu.CompilerParams(vmem_limit_bytes=4 * 1024 * 1024),
        name="pack",
    )(*(pltpu.with_memory_space_constraint(x, pltpu.HBM) for x in (genotypes, recomb_rates, panel_alleles)))
    cuts = [cut if n % GROUPS == 0 else exchange(cut, "group", n % GROUPS) for n, cut in enumerate(cuts)]
    tags = [cut[:, part:] for cut in cuts[:GROUPS]]
    sums = []
    for p in range(PARTS):
        pieces = [cut[:, :part] for cut in cuts[p * GROUPS : (p + 1) * GROUPS]]
        sums.append(
            pl.pallas_call(
                functools.partial(window_kernel, min(512, part)),
                out_shape=[
                    jax.ShapeDtypeStruct((2, TALL, LANES), F32),
                    jax.ShapeDtypeStruct((PAIRS, LANES), F32),
                ],
                in_specs=[VMEM] * (2 * GROUPS),
                out_specs=[VMEM] * 2,
                scratch_shapes=[
                    pltpu.VMEM((MARKERS, part), jnp.int32),
                    pltpu.VMEM((MARKERS, LANES), jnp.int32),
                    pltpu.VMEM((2, 4 * MARKERS, part), BF16),
                    pltpu.VMEM((2, len(LEFT[0]) * 2 * ROWS, part), BF16),
                ],
                compiler_params=pltpu.CompilerParams(vmem_limit_bytes=40 * 1024 * 1024),
                cost_estimate=pl.CostEstimate(flops=part * 900000, bytes_accessed=0, transcendentals=0),
                name="windows",
            )(*pieces, *tags)
        )
    sums_t, sums_e = (sum(each) for each in zip(*sums))

    lane, row = iota(sums_e.shape, 1), iota(sums_e.shape, 0)
    unused = (row < ROWS) & (lane % HALF >= MISC) & (lane % HALF < 2 * ROWS)
    sums_e = jnp.where(unused, jnp.concatenate([misc, jnp.zeros_like(misc)], axis=0), sums_e)
    sent = jnp.concatenate([sums_t.reshape(2 * TALL, LANES), sums_e], axis=0)
    both = sent + exchange(sent, "group", 1)
    half = place // (GROUPS // 2)
    carried = is_odd(place ^ lax.axis_index("batch"))

    def part_of(which):
        start = (2 * which + carried) * SUBSET
        return jnp.concatenate([lax.dynamic_slice_in_dim(both, start, SUBSET), both[2 * TALL :]], axis=0)

    core = copies
    kept = part_of(half) + exchange_flat(part_of(1 - half), 2 * core + core)
    by = 1
    while by < copies:
        kept = kept + exchange_flat(kept, by + core)
        by *= 2
    mine = kept[:SUBSET]
    theirs = exchange(mine, "group", 1)
    weights, logs = pl.pallas_call(
        functools.partial(solve_kernel, float(width * copies), float(copies)),
        out_shape=[
            jax.ShapeDtypeStruct((2 * MARKERS + ROWS, LANES), F32),
            jax.ShapeDtypeStruct((1, 2), F32),
        ],
        in_specs=[VMEM],
        out_specs=[VMEM] * 2,
        compiler_params=pltpu.CompilerParams(vmem_limit_bytes=4 * 1024 * 1024),
        cost_estimate=pl.CostEstimate(flops=1000000, bytes_accessed=0, transcendentals=0),
        name="solve",
    )(kept[SUBSET:])
    whole = jnp.where(carried == 0, jnp.concatenate([mine, theirs], axis=0), jnp.concatenate([theirs, mine], axis=0))
    dosage = pl.pallas_call(
        contract_kernel,
        out_shape=jax.ShapeDtypeStruct((2, ROWS), F32),
        in_specs=[VMEM] * 2,
        out_specs=VMEM,
        compiler_params=pltpu.CompilerParams(vmem_limit_bytes=4 * 1024 * 1024),
        name="contract",
    )(weights, whole)
    return dosage, logs.reshape(2)


def fits_windows(panel_alleles, genotypes, groups, copies):
    markers, width = panel_alleles.shape
    return (
        groups == GROUPS
        and copies & (copies - 1) == 0
        and markers == ROWS
        and genotypes.shape[0] == 2
        and width % (GROUPS * LANES * 4) == 0
    )


def on_device(panel_alleles, recomb_rates, genotypes):
    groups, copies = lax.axis_size("group"), lax.axis_size("batch")
    if fits_windows(panel_alleles, genotypes, groups, copies):
        return on_device_windows(panel_alleles, recomb_rates, genotypes)
    return on_device_chain(panel_alleles, recomb_rates, genotypes)


def solution(mesh):
    placed = (P("group", "batch"), P("group"), P(None, "group"))
    return jax.shard_map(
        on_device, mesh=mesh, in_specs=placed, out_specs=(P(None, "group"), P()), check_vma=False
    )
```

```python
import functools
import math

import jax
import jax.numpy as jnp
from jax import lax
from jax.experimental import pallas as pl
from jax.experimental.pallas import tpu as pltpu
from jax.sharding import PartitionSpec as P

MISMATCH = 0.05
HIGHEST = lax.Precision.HIGHEST


def haplotypes(panel_rows):
    return panel_rows.shape[1] * lax.axis_size("batch")


def from_behind(x, axis, by):
    peers = lax.axis_size(axis)
    pairs = [(i, i + by) for i in range(peers) if 0 <= i + by < peers]
    return lax.ppermute(x, axis, pairs)


def emission(panel_rows, geno_col):
    observed = geno_col[:, None]
    agrees = jnp.where(panel_rows == observed, 1.0 - MISMATCH, MISMATCH)
    return jnp.where(observed == 2, 1.0, agrees).astype(jnp.float32)


def forward_terms(panel_rows, geno_col, switches):
    emitted = emission(panel_rows, geno_col)
    retain = emitted * (1.0 - switches)[:, None]
    inject = emitted * (switches / haplotypes(panel_rows))[:, None]
    return (retain, inject, None)


def backward_terms(panel_rows, geno_col, switches):
    emitted = emission(panel_rows, geno_col)[::-1]
    flipped = switches[::-1]
    retain = emitted * (1.0 - flipped)[:, None]
    inject = jnp.broadcast_to((flipped / haplotypes(panel_rows))[:, None], emitted.shape)
    return (retain, inject, emitted)


def partial_sums(entering, retain, inject, weight, extent):
    logs = jnp.cumsum(jnp.log(retain), axis=0)
    shifted = jnp.concatenate([jnp.zeros_like(entering)[None], logs[: extent - 1]], axis=0)
    before = jnp.exp(shifted)
    left_side = before if weight is None else weight * before
    leading = jnp.einsum("jk,k->j", left_side, entering, precision=HIGHEST)
    anchor = shifted[0]
    right_side = inject * jnp.exp(anchor[None] - logs)
    nearby = jnp.exp(jnp.minimum(shifted - anchor[None], 0.0))
    nearby = nearby if weight is None else weight * nearby
    columns = [jnp.einsum("jk,tk->jt", nearby, right_side, precision=HIGHEST)]
    coupling = jnp.concatenate(columns, axis=1)
    return (leading, coupling)


def solve_sums(leading, coupling):
    columns = coupling.shape[1]

    def settle(marker, sigmas):
        below = jnp.arange(columns) < marker
        update = leading[marker] + jnp.sum(
            jnp.where(below, coupling[marker] * sigmas[:columns], 0.0)
        )
        return sigmas.at[marker].set(update)

    return lax.fori_loop(0, leading.shape[0], settle, jnp.zeros_like(leading))


def advance(entering, retain, inject, sigmas, keep_states):

    def advance_single(current, pieces):
        current = pieces[0] * current + pieces[1] * pieces[2]
        return (current, current if keep_states else None)

    return lax.scan(advance_single, entering, (retain, inject, sigmas[: retain.shape[0]]))


def place_rows(store, block, active):
    return jnp.where(active, block, store)


def on_device_chain(panel_alleles, recomb_rates, genotypes):
    chain_size = lax.axis_size("group")
    position = lax.axis_index("group")
    markers, width = panel_alleles.shape
    targets = genotypes.shape[0]
    bundles = targets // targets
    uniform = jnp.full((targets, width), 1.0 / haplotypes(panel_alleles), jnp.float32)
    first_row = position == 0
    last_row = position == chain_size - 1

    def local_sums(active, arrivals, geno_rows, maker, extent):

        def local_compute():

            def local_single(pieces):
                retain, inject, weight = maker(panel_alleles, pieces[1], recomb_rates)
                return partial_sums(pieces[0], retain, inject, weight, extent)

            return lax.map(local_single, (arrivals, geno_rows))

        def local_skipped():
            return (
                jnp.zeros((targets, extent), jnp.float32),
                jnp.zeros((targets, extent, markers), jnp.float32),
            )

        return lax.cond(active, local_compute, local_skipped)

    def outgoing(active, arrivals, geno_rows, sigmas, maker, scale_row):

        def outgoing_compute():

            def outgoing_single(pieces):
                retain, inject, weight = maker(panel_alleles, pieces[1], recomb_rates)
                ending, unused = advance(pieces[0], retain, inject, pieces[2], False)
                return ending / pieces[2][scale_row]

            return lax.map(outgoing_single, (arrivals, geno_rows, sigmas))

        def outgoing_skipped():
            return jnp.zeros((targets, width), jnp.float32)

        return lax.cond(active, outgoing_compute, outgoing_skipped)

    def moment_step(moment, carried_state):
        (
            sent_forward,
            sent_backward,
            sent_running,
            store_forward,
            store_backward,
            sigma_forward,
            sigma_backward,
            log_terms,
        ) = carried_state
        got_forward = from_behind(sent_forward, "group", 1)
        got_backward = from_behind(sent_backward, "group", -1)
        entering_forward = jnp.where(first_row, uniform, got_forward)
        entering_backward = jnp.where(last_row, uniform, got_backward)
        index_forward = moment - position
        index_backward = moment - (chain_size - 1 - position)
        active_forward = (index_forward >= 0) & (index_forward < bundles)
        active_backward = (index_backward >= 0) & (index_backward < bundles)
        lead_forward, couple_forward = local_sums(
            active_forward, entering_forward, genotypes, forward_terms, markers + 1
        )
        lead_backward, couple_backward = local_sums(
            active_backward, entering_backward, genotypes, backward_terms, markers
        )
        lead_forward, couple_forward, lead_backward, couple_backward = lax.psum(
            (lead_forward, couple_forward, lead_backward, couple_backward), "batch"
        )
        sigmas_forward = jax.vmap(solve_sums)(lead_forward, couple_forward)
        sigmas_backward = jax.vmap(solve_sums)(lead_backward, couple_backward)
        next_forward = outgoing(
            active_forward, entering_forward, genotypes, sigmas_forward, forward_terms, markers
        )
        next_backward = outgoing(
            active_backward,
            entering_backward,
            genotypes,
            sigmas_backward,
            backward_terms,
            markers - 1,
        )
        guarded = jnp.where(active_forward, sigmas_forward[:, markers], 1.0)
        running = jnp.log(guarded)
        store_forward = place_rows(store_forward, entering_forward, active_forward)
        store_backward = place_rows(store_backward, entering_backward, active_backward)
        sigma_forward = place_rows(sigma_forward, sigmas_forward, active_forward)
        sigma_backward = place_rows(sigma_backward, sigmas_backward, active_backward)
        log_terms = place_rows(log_terms, running, active_forward)
        return (
            next_forward,
            next_backward,
            running,
            store_forward,
            store_backward,
            sigma_forward,
            sigma_backward,
            log_terms,
        )

    initial = (
        jnp.zeros((targets, width), jnp.float32),
        jnp.zeros((targets, width), jnp.float32),
        jnp.zeros((targets,), jnp.float32),
        jnp.zeros((targets, width), jnp.float32),
        jnp.zeros((targets, width), jnp.float32),
        jnp.zeros((targets, markers + 1), jnp.float32),
        jnp.zeros((targets, markers), jnp.float32),
        jnp.zeros((targets,), jnp.float32),
    )
    final_state = lax.fori_loop(0, chain_size + bundles - 1, moment_step, initial)
    store_forward, store_backward, sigma_forward, sigma_backward, log_terms = final_state[3:]
    whole_log = lax.psum(log_terms, "group")
    log_likelihood = whole_log / (markers * chain_size)

    def posterior(pieces):
        entering_ahead, entering_behind, geno_col, sigmas_ahead, sigmas_behind = pieces
        retain, inject, weight = forward_terms(panel_alleles, geno_col, recomb_rates)
        unused_f, forward_states = advance(entering_ahead, retain, inject, sigmas_ahead, True)
        forward_rows = forward_states / sigmas_ahead[1:, None]
        retain, inject, weight = backward_terms(panel_alleles, geno_col, recomb_rates)
        unused_b, backward_states = advance(entering_behind, retain, inject, sigmas_behind, True)
        scaled_back = backward_states[:-1] / sigmas_behind[:-1, None]
        backward_rows = jnp.concatenate([entering_behind[None], scaled_back], axis=0)[::-1]
        product = forward_rows * backward_rows
        numerator = jnp.sum(jnp.where(panel_alleles == 1, product, 0.0), axis=1)
        return (numerator, jnp.sum(product, axis=1))

    numerator, denominator = lax.map(
        posterior, (store_forward, store_backward, genotypes, sigma_forward, sigma_backward)
    )
    numerator, denominator = lax.psum((numerator, denominator), "batch")
    return (numerator / denominator, log_likelihood)


ROWS, LANES = 8, 128
HALF = LANES // 2
GROUPS = 4
SHARES = (9, 7)
MISSING = 2
SCALE = math.sqrt(MISMATCH * (1.0 - MISMATCH))
HALF_STEP = 0.5 * math.log((1.0 - MISMATCH) / MISMATCH)
VMEM = pl.BlockSpec(memory_space=pltpu.VMEM)
SMEM = pl.BlockSpec(memory_space=pltpu.SMEM)
F32, BF16 = jnp.float32, jnp.bfloat16


def iota(shape, axis):
    return lax.broadcasted_iota(jnp.int32, shape, axis)


MARKERS = ROWS * GROUPS
HALF_T = MARKERS // 2
PAIRS = GROUPS // 2 * ROWS
SUBSET = 5 * ROWS
TALL = 2 * SUBSET
TRIANGLES = [(0, 1), (2, 3), (7, -1)]
MISC = ROWS
TILES = [
    ("triangle", subset, a, ROWS - 2 - a if a < 3 else -1) for subset in range(2) for pair in TRIANGLES for a in pair if a >= 0
] + [("square", 1, j, -1) for j in range(ROWS)]


def pack_kernel(widths, geno_ref, rate_ref, panel_ref, *refs):
    outs, (misc_ref, genos, rates_in, sems) = refs[:-4], refs[-4:]
    place = lax.axis_index("group")
    chunk = panel_ref.shape[1] // GROUPS
    copies = []
    for n, ref in enumerate(outs):
        d, p = n % GROUPS, n // GROUPS
        part = widths[p]
        start = pl.multiple_of((place ^ d) * chunk + sum(widths[:p]), LANES)
        copies.append(
            pltpu.make_async_copy(panel_ref.at[:, pl.ds(start, part)], ref.at[:, pl.ds(0, part)], sems.at[n])
        )
    small = [
        pltpu.make_async_copy(geno_ref, genos, sems.at[len(outs)]),
        pltpu.make_async_copy(rate_ref, rates_in, sems.at[len(outs) + 1]),
    ]
    for copy in small + copies:
        copy.start()
    for copy in small:
        copy.wait()
    row, lane = iota((ROWS, LANES), 0), iota((ROWS, LANES), 1)
    tile = jnp.zeros((ROWS, LANES), jnp.int32)
    rates = jnp.zeros((ROWS, LANES), F32)
    for i in range(ROWS):
        tile = jnp.where(row == i, jnp.where(lane < HALF, genos[0, i], genos[1, i]), tile)
        rates = jnp.where(row == i, rates_in[i], rates)
    for ref in outs[:GROUPS]:
        ref[:, widths[0] :] = tile
    known = jnp.where(tile == MISSING, 0.0, 1.0)
    misc = jnp.where(lane == MISC + place, rates, 0.0)
    misc = jnp.where((lane == MISC + GROUPS + place) | (lane == HALF + MISC + place), known, misc)
    misc_ref[...] = misc
    for copy in copies:
        copy.wait()


def window_kernel(step, *refs):
    pieces, geno_refs = refs[:GROUPS], refs[GROUPS : 2 * GROUPS]
    t_ref, em_ref, panel, genos, wide, left = refs[2 * GROUPS :]
    place = lax.axis_index("group")
    columns = panel.shape[1]
    for d in range(GROUPS):
        rows = pl.ds(pl.multiple_of((place ^ d) * ROWS, ROWS), ROWS)
        panel[rows, :] = pieces[d][...]
        genos[rows, :] = geno_refs[d][...]

    r, j = iota((4 * MARKERS, 2 * MARKERS), 0), iota((4 * MARKERS, 2 * MARKERS), 1)
    same = r // (2 * MARKERS) == j // MARKERS
    prefix, marker = (r // MARKERS) % 2 == 0, r % MARKERS
    at = j % MARKERS
    sums = jnp.where(prefix, jnp.where(at <= marker, 1.0, 0.0), jnp.where(at < marker, -1.0, 0.0))
    sums = jnp.where(same, sums, 0.0).astype(BF16)

    for start in range(0, columns, step):
        here = slice(start, start + step)
        signs = []
        for h in range(2):
            for b in range(GROUPS):
                rows = slice(b * ROWS, (b + 1) * ROWS)
                seen = genos[rows, h * HALF : h * HALF + 1]
                agrees = jnp.where(panel[rows, here] == seen, 1.0, -1.0)
                signs.append(jnp.where(seen == MISSING, 0.0, agrees))
        signs = jnp.concatenate(signs, axis=0).astype(BF16)
        power = jnp.dot(sums, signs, preferred_element_type=F32)
        value = jnp.exp(power * HALF_STEP)
        upper = value.astype(BF16).astype(F32)
        lower = value - upper
        blocks = {}
        for h in range(2):
            for kind in range(2):
                for b in range(GROUPS):
                    at = h * 2 * MARKERS + kind * MARKERS + b * ROWS
                    both = jnp.concatenate([upper[at : at + ROWS], lower[at : at + ROWS]], axis=0).astype(BF16)
                    blocks[kind, h, b] = both
                    wide[kind, (h * GROUPS + b) * 2 * ROWS : (h * GROUPS + b + 1) * 2 * ROWS, here] = both
        row = iota((ROWS, step), 0)
        for half in range(2):
            for slot, (shape, subset, j, paired) in enumerate(TILES):
                outer = 0 if half == 0 else GROUPS - 1
                own = abs(outer - subset)
                near = own if shape == "triangle" else outer
                first = row <= j if half == 0 else row >= ROWS - 1 - j

                def carries(j):
                    t = own * ROWS + (j if half == 0 else ROWS - 1 - j)
                    return jnp.broadcast_to(panel[t : t + 1, here], (ROWS, step)).astype(F32)

                mask = carries(j) if paired < 0 else jnp.where(first, carries(j), carries(paired))
                mask = jnp.concatenate([mask, mask], axis=0).astype(BF16)
                for h in range(2):
                    base = blocks[1 - half, h, near]
                    if paired >= 0:
                        at = h * 2 * MARKERS + (1 - half) * MARKERS + near * ROWS
                        shift = j + 1 if half == 0 else ROWS - 1 - j
                        both = [x[at : at + ROWS] for x in (upper, lower)]
                        both = [jnp.where(first, x, pltpu.roll(x, shift, 0)) for x in both]
                        base = jnp.concatenate(both, axis=0).astype(BF16)
                    at = (slot * 2 + h) * 2 * ROWS
                    left[half, at : at + 2 * ROWS, here] = base * mask

    def product(a, b):
        return lax.dot_general(a, b, (((1,), (1,)), ((), ())), preferred_element_type=F32)

    lane = iota((ROWS, LANES), 1)
    first = lane % (2 * ROWS) < ROWS

    def rows_of(acc, slot):
        return acc[slot * 2 * ROWS : slot * 2 * ROWS + ROWS] + acc[slot * 2 * ROWS + ROWS : (slot + 1) * 2 * ROWS]

    def fold(a, b):
        return jnp.where(first, a + pltpu.roll(a, LANES - ROWS, 1), b + pltpu.roll(b, ROWS, 1))

    def both_targets(acc, slots):
        return jnp.where(lane < HALF, rows_of(acc, slots[0]), rows_of(acc, slots[1]))

    zero = jnp.zeros((ROWS, LANES), F32)
    for half in range(2):
        sums_t = product(left[half], wide[half])
        tiles = {
            (shape, subset, j): both_targets(sums_t, [2 * slot, 2 * slot + 1])
            for slot, (shape, subset, j, paired) in enumerate(TILES)
        }
        for subset in range(2):
            rows = [[tiles.get(("triangle", subset, j), zero) for j in pair] for pair in TRIANGLES]
            rows += [[tiles["square", 1, subset * ROWS // 2 + 2 * q + f] for f in range(2)] for q in range(ROWS // 4)]
            for q, pair in enumerate(rows):
                at = subset * SUBSET + q * ROWS
                t_ref[half, at : at + ROWS, :] = fold(*pair)
    sums_e = product(wide[1], wide[0])
    tiles = [both_targets(sums_e, [b, GROUPS + b]) for b in range(GROUPS)]
    for q in range(GROUPS // 2):
        em_ref[q * ROWS : (q + 1) * ROWS, :] = fold(tiles[2 * q], tiles[2 * q + 1])


def solve_kernel(panel_size, copies, sum_ref, ends_ref, log_ref):
    row, lane = iota((ROWS, LANES), 0), iota((ROWS, LANES), 1)
    target = lane // HALF
    folded = (lane % (2 * ROWS)) // ROWS
    misc = sum_ref[:ROWS, :] * (1.0 / copies)

    def spread(tile, at):
        return jnp.broadcast_to(tile[:, at : at + 1], (ROWS, LANES))

    rates = [spread(misc, MISC + b) for b in range(GROUPS)]
    odds = [rate / (1.0 - rate) for rate in rates]
    inverse = 1.0 / panel_size
    ahead = []
    for b in range(GROUPS):
        following = odds[b + 1][0:1, :] if b + 1 < GROUPS else jnp.ones((1, LANES), F32)
        ahead.append(jnp.concatenate([odds[b][1:, :], following], axis=0) * inverse)
    behind = [odd * inverse for odd in odds]

    pair = sum_ref[...]
    trail_tiles = []
    for q in range(GROUPS // 2):
        factor = jnp.where(folded == 0, behind[2 * q], behind[2 * q + 1])
        trail_tiles.append(pair[q * ROWS : (q + 1) * ROWS] * factor)
    square = jnp.concatenate([pair, jnp.zeros((LANES - pair.shape[0], LANES), F32)], axis=0)
    turned = jnp.transpose(square)

    def turned_tile(h, b, f):
        at = h * HALF + b * 2 * ROWS + f * ROWS
        return turned[at : at + ROWS] * ahead[b]

    lead_tiles = {(h, b, f): turned_tile(h, b, f) for h in range(2) for b in range(GROUPS) for f in range(2)}

    def lead_column(t, b):
        s, at = t // ROWS, (t // ROWS // 2) * ROWS + t % ROWS
        return jnp.where(target == 0, spread(lead_tiles[0, b, s % 2], at), spread(lead_tiles[1, b, s % 2], at))

    def trail_column(t, b):
        at = 2 * ROWS * (t // ROWS) + t % ROWS + ROWS * (b % 2)
        tile = trail_tiles[b // 2]
        return jnp.where(target == 0, spread(tile, at), spread(tile, HALF + at))

    zero = jnp.zeros((ROWS, LANES), F32)
    lead, trail, starts, ends = [zero] * GROUPS, [zero] * GROUPS, [zero] * GROUPS, [zero] * GROUPS
    v = jnp.ones((ROWS, LANES), F32)
    z = jnp.ones((ROWS, LANES), F32)
    for t in range(MARKERS):
        u = MARKERS - 1 - t
        bt, bu = t // ROWS, u // ROWS
        starts[bt] = jnp.where(row == t % ROWS, v, starts[bt])
        ends[bu] = jnp.where(row == u % ROWS, z, ends[bu])
        for b in range(bt, GROUPS):
            lead[b] = lead[b] + v * lead_column(t, b)
        for b in range(bu + 1):
            trail[b] = trail[b] + z * trail_column(u, b)
        v = jnp.broadcast_to(lead[bt][t % ROWS : t % ROWS + 1, :], (ROWS, LANES))
        z = jnp.broadcast_to(trail[bu][u % ROWS : u % ROWS + 1, :], (ROWS, LANES))
    for b in range(GROUPS):
        ends_ref[b * ROWS : (b + 1) * ROWS, :] = starts[b]
        ends_ref[MARKERS + b * ROWS : MARKERS + (b + 1) * ROWS, :] = ends[b]
    ends_ref[2 * MARKERS :, :] = inverse / v

    stay = [jnp.log(1.0 - rate) for rate in rates]
    stay[0] = jnp.where(row == 0, 0.0, stay[0])
    stay = jnp.sum(sum(stay), axis=0, keepdims=True)
    counts = jnp.sum(misc, axis=0, keepdims=True)
    logs = []
    for h, at in enumerate((MISC + GROUPS, HALF + MISC)):
        seen = sum(counts[:, at + b : at + b + 1] for b in range(GROUPS))
        whole = jnp.log(v[0:1, h * HALF : h * HALF + 1]) + stay[:, 0:1] + seen * math.log(SCALE)
        logs.append(whole * (1.0 / MARKERS))
    log_ref[...] = jnp.concatenate(logs, axis=1)


def contract_kernel(weight_ref, t_ref, dose_ref):
    place = lax.axis_index("group")
    low = place < GROUPS // 2
    inward = (place == 1) | (place == GROUPS - 2)
    row, lane = iota((ROWS, LANES), 0), iota((ROWS, LANES), 1)
    folded = (lane % (2 * ROWS)) // ROWS
    side = jnp.where(low, 1, -1)
    turn = jnp.where(low, 0, ROWS - 1)
    order = turn + side * row

    def weights(is_start, block):
        at = jnp.where(is_start, 0, MARKERS) + block * ROWS
        return weight_ref[pl.ds(pl.multiple_of(at, ROWS), ROWS), :]

    picked = weights(jnp.logical_not(low), GROUPS - 1)
    column = (lane % HALF) // (2 * ROWS)
    for b in range(GROUPS - 1):
        picked = jnp.where(column == b, weights(jnp.logical_not(low), b), picked)
    picked = jnp.where(row == lane % ROWS, picked, 0.0)
    across = jnp.sum(picked, axis=0, keepdims=True) * weight_ref[2 * MARKERS : 2 * MARKERS + 1, :]
    far_end = ROWS * column + lane % ROWS

    def reaches(j):
        t = place * ROWS + turn + side * j
        return (far_end - t) * side >= 0

    near = weights(low, place)
    base = jnp.where(inward, SUBSET, 0)
    total = jnp.zeros((ROWS, LANES), F32)
    for q, (a0, a1) in enumerate(TRIANGLES):
        a = jnp.where(folded == 0, a0, a1)
        own = order <= a
        paired = (a >= 0) & (a < 3)
        moved = []
        for each in (a0, a1):
            if 0 <= each < 3:
                moved.append(jnp.where(low, pltpu.roll(near, each + 1, 0), pltpu.roll(near, ROWS - 1 - each, 0)))
            else:
                moved.append(near)
        weight = jnp.where(own, near, jnp.where(folded == 0, moved[0], moved[1])) * across
        data = t_ref[pl.ds(pl.multiple_of(base + q * ROWS, ROWS), ROWS), :]
        valid = (own | paired) & reaches(jnp.where(own, a, ROWS - 2 - a))
        terms = jnp.where(valid, data * weight, 0.0)
        one = jnp.sum(jnp.where(own, terms, 0.0), axis=0, keepdims=True)
        other = jnp.sum(jnp.where(own, 0.0, terms), axis=0, keepdims=True)
        total = total + jnp.where(row == a, one, 0.0)
        total = total + jnp.where(paired & (row == ROWS - 2 - a), other, 0.0)
    outermost = weights(low, jnp.where(low, 0, GROUPS - 1)) * jnp.where(inward, 1.0, 0.0) * across
    for subset in range(2):
        for q in range(ROWS // 4):
            j = subset * ROWS // 2 + 2 * q + folded
            at = subset * SUBSET + (len(TRIANGLES) + q) * ROWS
            terms = jnp.where(reaches(j), t_ref[at : at + ROWS, :] * outermost, 0.0)
            total = total + jnp.where(row == j, jnp.sum(terms, axis=0, keepdims=True), 0.0)
    doses = []
    for h in range(2):
        dose = jnp.sum(jnp.where(lane // HALF == h, total, 0.0), axis=1, keepdims=True)
        doses.append(jnp.sum(jnp.where(order == lane, dose, 0.0), axis=0, keepdims=True))
    dose_ref[...] = jnp.concatenate(doses, axis=0)[:, :ROWS]


def exchange(x, axis, by):
    peers = lax.axis_size(axis)
    return lax.ppermute(x, axis, [(i, i ^ by) for i in range(peers)])


def exchange_flat(x, by):
    peers = lax.axis_size("group") * lax.axis_size("batch")
    return lax.ppermute(x, ("group", "batch"), [(i, i ^ by) for i in range(peers)])


def is_odd(bits):
    odd = bits
    for shift in (16, 8, 4, 2, 1):
        odd = odd ^ (odd >> shift)
    return odd & 1


def on_device_windows(panel_alleles, recomb_rates, genotypes):
    width = panel_alleles.shape[1]
    copies = lax.axis_size("batch")
    chunk = width // GROUPS
    place = lax.axis_index("group")
    widths = [chunk * share // sum(SHARES) for share in SHARES]
    shapes = [
        jax.ShapeDtypeStruct((ROWS, part + (LANES if p == 0 else 0)), jnp.int32)
        for p, part in enumerate(widths)
        for d in range(GROUPS)
    ]
    *cuts, misc = pl.pallas_call(
        functools.partial(pack_kernel, widths),
        out_shape=shapes + [jax.ShapeDtypeStruct((ROWS, LANES), F32)],
        in_specs=[pl.BlockSpec(memory_space=pltpu.HBM)] * 3,
        out_specs=[VMEM] * (len(shapes) + 1),
        scratch_shapes=[
            pltpu.SMEM(genotypes.shape, jnp.int32),
            pltpu.SMEM(recomb_rates.shape, F32),
            pltpu.SemaphoreType.DMA((len(shapes) + 2,)),
        ],
        compiler_params=pltpu.CompilerParams(vmem_limit_bytes=4 * 1024 * 1024),
        name="pack",
    )(*(pltpu.with_memory_space_constraint(x, pltpu.HBM) for x in (genotypes, recomb_rates, panel_alleles)))
    arrived = None
    for p in range(len(widths)):
        part = cuts[p * GROUPS : (p + 1) * GROUPS]
        if arrived is not None:
            part[1:], arrived = lax.optimization_barrier((part[1:], arrived))
            cuts[(p - 1) * GROUPS + 1] = arrived
        part = [cut if d == 0 else exchange(cut, "group", d) for d, cut in enumerate(part)]
        cuts[p * GROUPS : (p + 1) * GROUPS] = part
        arrived = part[1]
    tags = [cut[:, widths[0] :] for cut in cuts[:GROUPS]]
    sums = []
    for p, part in enumerate(widths):
        pieces = [cut[:, :part] for cut in cuts[p * GROUPS : (p + 1) * GROUPS]]
        sums.append(
            pl.pallas_call(
                functools.partial(window_kernel, min(256, part)),
                out_shape=[
                    jax.ShapeDtypeStruct((2, TALL, LANES), F32),
                    jax.ShapeDtypeStruct((PAIRS, LANES), F32),
                ],
                in_specs=[VMEM] * (2 * GROUPS),
                out_specs=[VMEM] * 2,
                scratch_shapes=[
                    pltpu.VMEM((MARKERS, part), jnp.int32),
                    pltpu.VMEM((MARKERS, LANES), jnp.int32),
                    pltpu.VMEM((2, 4 * MARKERS, part), BF16),
                    pltpu.VMEM((2, len(TILES) * 4 * ROWS, part), BF16),
                ],
                compiler_params=pltpu.CompilerParams(vmem_limit_bytes=40 * 1024 * 1024),
                cost_estimate=pl.CostEstimate(flops=part * 900000, bytes_accessed=0, transcendentals=0),
                name="windows",
            )(*pieces, *tags)
        )
    sums_t, sums_e = (sum(each) for each in zip(*sums))

    lane, row = iota(sums_e.shape, 1), iota(sums_e.shape, 0)
    unused = (row < ROWS) & (lane % HALF >= MISC) & (lane % HALF < 2 * ROWS)
    sums_e = jnp.where(unused, jnp.concatenate([misc, jnp.zeros_like(misc)], axis=0), sums_e)
    sent = jnp.concatenate([sums_t.reshape(2 * TALL, LANES), sums_e], axis=0)
    both = sent + exchange(sent, "group", 1)
    half = place // (GROUPS // 2)
    carried = is_odd(place ^ lax.axis_index("batch"))

    def part_of(which):
        start = (2 * which + carried) * SUBSET
        return jnp.concatenate([lax.dynamic_slice_in_dim(both, start, SUBSET), both[2 * TALL :]], axis=0)

    core = copies
    kept = part_of(half) + exchange_flat(part_of(1 - half), 2 * core + core)
    by = 1
    while by < copies:
        kept = kept + exchange_flat(kept, by + core)
        by *= 2
    mine = kept[:SUBSET]
    theirs = exchange(mine, "group", 1)
    weights, logs = pl.pallas_call(
        functools.partial(solve_kernel, float(width * copies), float(copies)),
        out_shape=[
            jax.ShapeDtypeStruct((2 * MARKERS + ROWS, LANES), F32),
            jax.ShapeDtypeStruct((1, 2), F32),
        ],
        in_specs=[VMEM],
        out_specs=[VMEM] * 2,
        compiler_params=pltpu.CompilerParams(vmem_limit_bytes=4 * 1024 * 1024),
        cost_estimate=pl.CostEstimate(flops=1000000, bytes_accessed=0, transcendentals=0),
        name="solve",
    )(kept[SUBSET:])
    whole = jnp.where(carried == 0, jnp.concatenate([mine, theirs], axis=0), jnp.concatenate([theirs, mine], axis=0))
    dosage = pl.pallas_call(
        contract_kernel,
        out_shape=jax.ShapeDtypeStruct((2, ROWS), F32),
        in_specs=[VMEM] * 2,
        out_specs=VMEM,
        compiler_params=pltpu.CompilerParams(vmem_limit_bytes=4 * 1024 * 1024),
        name="contract",
    )(weights, whole)
    return dosage, logs.reshape(2)


def fits_windows(panel_alleles, genotypes, groups, copies):
    markers, width = panel_alleles.shape
    return (
        groups == GROUPS
        and copies & (copies - 1) == 0
        and markers == ROWS
        and genotypes.shape[0] == 2
        and width % (GROUPS * LANES * 32) == 0
    )


def on_device(panel_alleles, recomb_rates, genotypes):
    groups, copies = lax.axis_size("group"), lax.axis_size("batch")
    if fits_windows(panel_alleles, genotypes, groups, copies):
        return on_device_windows(panel_alleles, recomb_rates, genotypes)
    return on_device_chain(panel_alleles, recomb_rates, genotypes)


def solution(mesh):
    placed = (P("group", "batch"), P("group"), P(None, "group"))
    return jax.shard_map(
        on_device, mesh=mesh, in_specs=placed, out_specs=(P(None, "group"), P()), check_vma=False
    )
```

```python
import functools
import math

import jax
import jax.numpy as jnp
from jax import lax
from jax.experimental import pallas as pl
from jax.experimental.pallas import tpu as pltpu
from jax.sharding import PartitionSpec as P

MISMATCH = 0.05
HIGHEST = lax.Precision.HIGHEST


def haplotypes(panel_rows):
    return panel_rows.shape[1] * lax.axis_size("batch")


def from_behind(x, axis, by):
    peers = lax.axis_size(axis)
    pairs = [(i, i + by) for i in range(peers) if 0 <= i + by < peers]
    return lax.ppermute(x, axis, pairs)


def emission(panel_rows, geno_col):
    observed = geno_col[:, None]
    agrees = jnp.where(panel_rows == observed, 1.0 - MISMATCH, MISMATCH)
    return jnp.where(observed == 2, 1.0, agrees).astype(jnp.float32)


def forward_terms(panel_rows, geno_col, switches):
    emitted = emission(panel_rows, geno_col)
    retain = emitted * (1.0 - switches)[:, None]
    inject = emitted * (switches / haplotypes(panel_rows))[:, None]
    return (retain, inject, None)


def backward_terms(panel_rows, geno_col, switches):
    emitted = emission(panel_rows, geno_col)[::-1]
    flipped = switches[::-1]
    retain = emitted * (1.0 - flipped)[:, None]
    inject = jnp.broadcast_to((flipped / haplotypes(panel_rows))[:, None], emitted.shape)
    return (retain, inject, emitted)


def partial_sums(entering, retain, inject, weight, extent):
    logs = jnp.cumsum(jnp.log(retain), axis=0)
    shifted = jnp.concatenate([jnp.zeros_like(entering)[None], logs[: extent - 1]], axis=0)
    before = jnp.exp(shifted)
    left_side = before if weight is None else weight * before
    leading = jnp.einsum("jk,k->j", left_side, entering, precision=HIGHEST)
    anchor = shifted[0]
    right_side = inject * jnp.exp(anchor[None] - logs)
    nearby = jnp.exp(jnp.minimum(shifted - anchor[None], 0.0))
    nearby = nearby if weight is None else weight * nearby
    columns = [jnp.einsum("jk,tk->jt", nearby, right_side, precision=HIGHEST)]
    coupling = jnp.concatenate(columns, axis=1)
    return (leading, coupling)


def solve_sums(leading, coupling):
    columns = coupling.shape[1]

    def settle(marker, sigmas):
        below = jnp.arange(columns) < marker
        update = leading[marker] + jnp.sum(
            jnp.where(below, coupling[marker] * sigmas[:columns], 0.0)
        )
        return sigmas.at[marker].set(update)

    return lax.fori_loop(0, leading.shape[0], settle, jnp.zeros_like(leading))


def advance(entering, retain, inject, sigmas, keep_states):

    def advance_single(current, pieces):
        current = pieces[0] * current + pieces[1] * pieces[2]
        return (current, current if keep_states else None)

    return lax.scan(advance_single, entering, (retain, inject, sigmas[: retain.shape[0]]))


def place_rows(store, block, active):
    return jnp.where(active, block, store)


def on_device_chain(panel_alleles, recomb_rates, genotypes):
    chain_size = lax.axis_size("group")
    position = lax.axis_index("group")
    markers, width = panel_alleles.shape
    targets = genotypes.shape[0]
    bundles = targets // targets
    uniform = jnp.full((targets, width), 1.0 / haplotypes(panel_alleles), jnp.float32)
    first_row = position == 0
    last_row = position == chain_size - 1

    def local_sums(active, arrivals, geno_rows, maker, extent):

        def local_compute():

            def local_single(pieces):
                retain, inject, weight = maker(panel_alleles, pieces[1], recomb_rates)
                return partial_sums(pieces[0], retain, inject, weight, extent)

            return lax.map(local_single, (arrivals, geno_rows))

        def local_skipped():
            return (
                jnp.zeros((targets, extent), jnp.float32),
                jnp.zeros((targets, extent, markers), jnp.float32),
            )

        return lax.cond(active, local_compute, local_skipped)

    def outgoing(active, arrivals, geno_rows, sigmas, maker, scale_row):

        def outgoing_compute():

            def outgoing_single(pieces):
                retain, inject, weight = maker(panel_alleles, pieces[1], recomb_rates)
                ending, unused = advance(pieces[0], retain, inject, pieces[2], False)
                return ending / pieces[2][scale_row]

            return lax.map(outgoing_single, (arrivals, geno_rows, sigmas))

        def outgoing_skipped():
            return jnp.zeros((targets, width), jnp.float32)

        return lax.cond(active, outgoing_compute, outgoing_skipped)

    def moment_step(moment, carried_state):
        (
            sent_forward,
            sent_backward,
            sent_running,
            store_forward,
            store_backward,
            sigma_forward,
            sigma_backward,
            log_terms,
        ) = carried_state
        got_forward = from_behind(sent_forward, "group", 1)
        got_backward = from_behind(sent_backward, "group", -1)
        entering_forward = jnp.where(first_row, uniform, got_forward)
        entering_backward = jnp.where(last_row, uniform, got_backward)
        index_forward = moment - position
        index_backward = moment - (chain_size - 1 - position)
        active_forward = (index_forward >= 0) & (index_forward < bundles)
        active_backward = (index_backward >= 0) & (index_backward < bundles)
        lead_forward, couple_forward = local_sums(
            active_forward, entering_forward, genotypes, forward_terms, markers + 1
        )
        lead_backward, couple_backward = local_sums(
            active_backward, entering_backward, genotypes, backward_terms, markers
        )
        lead_forward, couple_forward, lead_backward, couple_backward = lax.psum(
            (lead_forward, couple_forward, lead_backward, couple_backward), "batch"
        )
        sigmas_forward = jax.vmap(solve_sums)(lead_forward, couple_forward)
        sigmas_backward = jax.vmap(solve_sums)(lead_backward, couple_backward)
        next_forward = outgoing(
            active_forward, entering_forward, genotypes, sigmas_forward, forward_terms, markers
        )
        next_backward = outgoing(
            active_backward,
            entering_backward,
            genotypes,
            sigmas_backward,
            backward_terms,
            markers - 1,
        )
        guarded = jnp.where(active_forward, sigmas_forward[:, markers], 1.0)
        running = jnp.log(guarded)
        store_forward = place_rows(store_forward, entering_forward, active_forward)
        store_backward = place_rows(store_backward, entering_backward, active_backward)
        sigma_forward = place_rows(sigma_forward, sigmas_forward, active_forward)
        sigma_backward = place_rows(sigma_backward, sigmas_backward, active_backward)
        log_terms = place_rows(log_terms, running, active_forward)
        return (
            next_forward,
            next_backward,
            running,
            store_forward,
            store_backward,
            sigma_forward,
            sigma_backward,
            log_terms,
        )

    initial = (
        jnp.zeros((targets, width), jnp.float32),
        jnp.zeros((targets, width), jnp.float32),
        jnp.zeros((targets,), jnp.float32),
        jnp.zeros((targets, width), jnp.float32),
        jnp.zeros((targets, width), jnp.float32),
        jnp.zeros((targets, markers + 1), jnp.float32),
        jnp.zeros((targets, markers), jnp.float32),
        jnp.zeros((targets,), jnp.float32),
    )
    final_state = lax.fori_loop(0, chain_size + bundles - 1, moment_step, initial)
    store_forward, store_backward, sigma_forward, sigma_backward, log_terms = final_state[3:]
    whole_log = lax.psum(log_terms, "group")
    log_likelihood = whole_log / (markers * chain_size)

    def posterior(pieces):
        entering_ahead, entering_behind, geno_col, sigmas_ahead, sigmas_behind = pieces
        retain, inject, weight = forward_terms(panel_alleles, geno_col, recomb_rates)
        unused_f, forward_states = advance(entering_ahead, retain, inject, sigmas_ahead, True)
        forward_rows = forward_states / sigmas_ahead[1:, None]
        retain, inject, weight = backward_terms(panel_alleles, geno_col, recomb_rates)
        unused_b, backward_states = advance(entering_behind, retain, inject, sigmas_behind, True)
        scaled_back = backward_states[:-1] / sigmas_behind[:-1, None]
        backward_rows = jnp.concatenate([entering_behind[None], scaled_back], axis=0)[::-1]
        product = forward_rows * backward_rows
        numerator = jnp.sum(jnp.where(panel_alleles == 1, product, 0.0), axis=1)
        return (numerator, jnp.sum(product, axis=1))

    numerator, denominator = lax.map(
        posterior, (store_forward, store_backward, genotypes, sigma_forward, sigma_backward)
    )
    numerator, denominator = lax.psum((numerator, denominator), "batch")
    return (numerator / denominator, log_likelihood)


ROWS, LANES = 8, 128
HALF = LANES // 2
GROUPS = 4
SHARES = (9, 7)
MISSING = 2
SCALE = math.sqrt(MISMATCH * (1.0 - MISMATCH))
HALF_STEP = 0.5 * math.log((1.0 - MISMATCH) / MISMATCH)
VMEM = pl.BlockSpec(memory_space=pltpu.VMEM)
SMEM = pl.BlockSpec(memory_space=pltpu.SMEM)
F32, BF16 = jnp.float32, jnp.bfloat16


def iota(shape, axis):
    return lax.broadcasted_iota(jnp.int32, shape, axis)


MARKERS = ROWS * GROUPS
HALF_T = MARKERS // 2
SUBSET = 5 * ROWS
TALL = 2 * SUBSET
TRIANGLE, SQUARE = 0, 1
SETS = [
    [(TRIANGLE, 0, 0), (TRIANGLE, 0, 1), (TRIANGLE, 0, 3)]
    + [(TRIANGLE, 1, a) for a in (0, 1, 2, 7)]
    + [(SQUARE, 1, j) for j in (0, 1)],
    [(TRIANGLE, 0, 2), (TRIANGLE, 0, 7), (TRIANGLE, 1, 3)] + [(SQUARE, 1, j) for j in range(2, ROWS)],
]
TILES = SETS[0] + SETS[1]
TUCKED = [(1, 1), (1, 2), (1, 3), (2, 2), (2, 3), (3, 3)]
FIRST_TUCKED = 3
SPARE = 2


def paired_with(shape, a):
    return ROWS - 2 - a if shape == TRIANGLE and a < 3 else -1


def pack_kernel(widths, geno_ref, rate_ref, panel_ref, *refs):
    outs, (misc_ref, genos, rates_in, sems) = refs[:-4], refs[-4:]
    place = lax.axis_index("group")
    chunk = panel_ref.shape[1] // GROUPS
    copies = []
    for n, ref in enumerate(outs):
        d, p = n % GROUPS, n // GROUPS
        part = widths[p]
        start = pl.multiple_of((place ^ d) * chunk + sum(widths[:p]), LANES)
        copies.append(
            pltpu.make_async_copy(panel_ref.at[:, pl.ds(start, part)], ref.at[:, pl.ds(0, part)], sems.at[n])
        )
    small = [
        pltpu.make_async_copy(geno_ref, genos, sems.at[len(outs)]),
        pltpu.make_async_copy(rate_ref, rates_in, sems.at[len(outs) + 1]),
    ]
    for copy in small + copies:
        copy.start()
    for copy in small:
        copy.wait()
    row, lane = iota((ROWS, LANES), 0), iota((ROWS, LANES), 1)
    tile = jnp.zeros((ROWS, LANES), jnp.int32)
    misc = jnp.zeros((ROWS, LANES), F32)
    for i in range(ROWS):
        tile = jnp.where(row == i, jnp.where(lane < HALF, genos[0, i], genos[1, i]), tile)
        misc = jnp.where(lane == i, rates_in[i], misc)
        for h in range(2):
            known = jnp.where(genos[h, i] == MISSING, 0.0, 1.0)
            misc = jnp.where(lane == 2 * ROWS * (h + 1) + i, known, misc)
    for ref in outs[:GROUPS]:
        ref[:, widths[0] :] = tile
    misc_ref[...] = jnp.where((row == GROUPS + place) | (row == GROUPS - 1 - place), misc, 0.0)
    for copy in copies:
        copy.wait()


def window_kernel(step, *refs):
    pieces, geno_refs = refs[:GROUPS], refs[GROUPS : 2 * GROUPS]
    t_ref, panel, genos, wide, left = refs[2 * GROUPS :]
    place = lax.axis_index("group")
    columns = panel.shape[1]
    for d in range(GROUPS):
        rows = pl.ds(pl.multiple_of((place ^ d) * ROWS, ROWS), ROWS)
        panel[rows, :] = pieces[d][...]
        genos[rows, :] = geno_refs[d][...]

    r, j = iota((4 * MARKERS, 2 * MARKERS), 0), iota((4 * MARKERS, 2 * MARKERS), 1)
    same = r // (2 * MARKERS) == j // MARKERS
    prefix, marker = (r // MARKERS) % 2 == 0, r % MARKERS
    at = j % MARKERS
    sums = jnp.where(prefix, jnp.where(at <= marker, 1.0, 0.0), jnp.where(at < marker, -1.0, 0.0))
    sums = jnp.where(same, sums, 0.0).astype(BF16)

    for start in range(0, columns, step):
        here = slice(start, start + step)
        signs = []
        for h in range(2):
            for b in range(GROUPS):
                rows = slice(b * ROWS, (b + 1) * ROWS)
                seen = genos[rows, h * HALF : h * HALF + 1]
                agrees = jnp.where(panel[rows, here] == seen, 1.0, -1.0)
                signs.append(jnp.where(seen == MISSING, 0.0, agrees))
        signs = jnp.concatenate(signs, axis=0).astype(BF16)
        power = jnp.dot(sums, signs, preferred_element_type=F32)
        value = jnp.exp(power * HALF_STEP)
        upper = value.astype(BF16).astype(F32)
        lower = value - upper
        blocks = {}
        for h in range(2):
            for kind in range(2):
                for b in range(GROUPS):
                    at = h * 2 * MARKERS + kind * MARKERS + b * ROWS
                    both = jnp.concatenate([upper[at : at + ROWS], lower[at : at + ROWS]], axis=0).astype(BF16)
                    blocks[kind, h, b] = both
                    wide[kind, (h * GROUPS + b) * 2 * ROWS : (h * GROUPS + b + 1) * 2 * ROWS, here] = both
        row = iota((ROWS, step), 0)
        for half in range(2):
            for slot, (shape, block, j) in enumerate(TILES):
                paired = paired_with(shape, j)
                outer = 0 if half == 0 else GROUPS - 1
                own = abs(outer - block)
                near = own if shape == TRIANGLE else outer
                first = row <= j if half == 0 else row >= ROWS - 1 - j

                def carries(j):
                    t = own * ROWS + (j if half == 0 else ROWS - 1 - j)
                    return jnp.broadcast_to(panel[t : t + 1, here], (ROWS, step)).astype(F32)

                mask = carries(j) if paired < 0 else jnp.where(first, carries(j), carries(paired))
                mask = jnp.concatenate([mask, mask], axis=0).astype(BF16)
                for h in range(2):
                    base = blocks[1 - half, h, near]
                    if paired >= 0:
                        at = h * 2 * MARKERS + (1 - half) * MARKERS + near * ROWS
                        shift = j + 1 if half == 0 else ROWS - 1 - j
                        both = [x[at : at + ROWS] for x in (upper, lower)]
                        both = [jnp.where(first, x, pltpu.roll(x, shift, 0)) for x in both]
                        base = jnp.concatenate(both, axis=0).astype(BF16)
                    at = (slot * 2 + h) * 2 * ROWS
                    left[half, at : at + 2 * ROWS, here] = base * mask

    def product(a, b):
        return lax.dot_general(a, b, (((1,), (1,)), ((), ())), preferred_element_type=F32)

    lane = iota((ROWS, LANES), 1)
    first = lane % (2 * ROWS) < ROWS

    def rows_of(acc, slot):
        return acc[slot * 2 * ROWS : slot * 2 * ROWS + ROWS] + acc[slot * 2 * ROWS + ROWS : (slot + 1) * 2 * ROWS]

    def fold(a, b):
        return jnp.where(first, a + pltpu.roll(a, LANES - ROWS, 1), b + pltpu.roll(b, ROWS, 1))

    def both_targets(acc, slots):
        return jnp.where(lane < HALF, rows_of(acc, slots[0]), rows_of(acc, slots[1]))

    def unfold(tile, column, to_column, odd):
        shift = 2 * ROWS * (to_column - column) + ROWS * odd
        tile = tile + pltpu.roll(tile, LANES - ROWS, 1)
        return tile if shift == 0 else pltpu.roll(tile, shift % LANES, 1)

    sums_e = product(wide[1], wide[0])
    plain = [both_targets(sums_e, [b, GROUPS + b]) for b in range(GROUPS)]
    column = (lane % HALF) // (2 * ROWS)
    for half in range(2):
        outer = 0 if half == 0 else GROUPS - 1
        sums_t = product(left[half], wide[half])
        tucked = {}
        for n, (b, to) in enumerate(TUCKED):
            slot = FIRST_TUCKED + n
            moved = unfold(plain[b], to, outer, slot % 2)
            here = (column == outer) & (first if slot % 2 == 0 else jnp.logical_not(first))
            tucked.setdefault(slot // 2, []).append((here, moved))
        for subset in range(2):
            base = subset * len(SETS[0])
            tiles = [both_targets(sums_t, [2 * n, 2 * n + 1]) for n in range(base, base + len(SETS[subset]))] + [plain[0]]
            for q in range(SUBSET // ROWS):
                value = fold(tiles[2 * q], tiles[2 * q + 1])
                for here, moved in tucked.get(q, []):
                    value = jnp.where(here, moved, value)
                at = subset * SUBSET + q * ROWS
                t_ref[half, at : at + ROWS, :] = value


def solve_kernel(panel_size, copies, sum_ref, ends_ref, log_ref):
    low = lax.axis_index("group") < GROUPS // 2
    row, lane = iota((ROWS, LANES), 0), iota((ROWS, LANES), 1)
    target = lane // HALF
    folded = (lane % (2 * ROWS)) // ROWS
    column_of = (lane % HALF) // (2 * ROWS)
    misc = sum_ref[SPARE // 2 * ROWS : (SPARE // 2 + 1) * ROWS, :]

    def spread(tile, at):
        return jnp.broadcast_to(tile[:, at : at + 1], (ROWS, LANES))

    def drawn(slot, to, odd):
        tile = sum_ref[slot // 2 * ROWS : (slot // 2 + 1) * ROWS, :]
        shifts = [2 * ROWS * (to - outer) + ROWS * (odd - slot % 2) for outer in (0, GROUPS - 1)]
        return jnp.where(low, *(pltpu.roll(tile, shift % LANES, 1) if shift else tile for shift in shifts))

    last = sum_ref[SUBSET - ROWS :, :]
    pair = [jnp.where(folded == 0, pltpu.roll(last, LANES - ROWS, 1), 0.0), jnp.zeros((ROWS, LANES), F32)]
    for n, (b, to) in enumerate(TUCKED):
        here = (column_of == to) & (folded == b % 2)
        pair[b // 2] = jnp.where(here, drawn(FIRST_TUCKED + n, to, b % 2), pair[b // 2])
    square = jnp.concatenate(pair + [misc, jnp.zeros((LANES - 3 * ROWS, LANES), F32)], axis=0)
    turned = jnp.transpose(square)

    listed = turned[:ROWS] * (1.0 / copies)
    spare = GROUPS * ROWS // 2
    rates = [jnp.where(low, spread(listed, spare + GROUPS + b), spread(listed, spare + GROUPS - 1 - b)) for b in range(GROUPS)]
    odds = [rate / (1.0 - rate) for rate in rates]
    inverse = 1.0 / panel_size
    ahead = []
    for b in range(GROUPS):
        following = odds[b + 1][0:1, :] if b + 1 < GROUPS else jnp.ones((1, LANES), F32)
        ahead.append(jnp.concatenate([odds[b][1:, :], following], axis=0) * inverse)
    behind = [odd * inverse for odd in odds]

    trail_tiles = []
    for q in range(GROUPS // 2):
        factor = jnp.where(folded == 0, behind[2 * q], behind[2 * q + 1])
        trail_tiles.append(pair[q] * factor)

    def turned_tile(h, b, f):
        at = h * HALF + b * 2 * ROWS + f * ROWS
        return turned[at : at + ROWS] * ahead[b]

    lead_tiles = {(h, b, f): turned_tile(h, b, f) for h in range(2) for b in range(GROUPS) for f in range(2)}

    def lead_column(t, b):
        s, at = t // ROWS, (t // ROWS // 2) * ROWS + t % ROWS
        return jnp.where(target == 0, spread(lead_tiles[0, b, s % 2], at), spread(lead_tiles[1, b, s % 2], at))

    def trail_column(t, b):
        at = 2 * ROWS * (t // ROWS) + t % ROWS + ROWS * (b % 2)
        tile = trail_tiles[b // 2]
        return jnp.where(target == 0, spread(tile, at), spread(tile, HALF + at))

    zero = jnp.zeros((ROWS, LANES), F32)
    lead, trail, starts, ends = [zero] * GROUPS, [zero] * GROUPS, [zero] * GROUPS, [zero] * GROUPS
    v = jnp.ones((ROWS, LANES), F32)
    z = jnp.ones((ROWS, LANES), F32)
    for t in range(MARKERS):
        u = MARKERS - 1 - t
        bt, bu = t // ROWS, u // ROWS
        starts[bt] = jnp.where(row == t % ROWS, v, starts[bt])
        ends[bu] = jnp.where(row == u % ROWS, z, ends[bu])
        for b in range(bt, GROUPS):
            lead[b] = lead[b] + v * lead_column(t, b)
        for b in range(bu + 1):
            trail[b] = trail[b] + z * trail_column(u, b)
        v = jnp.broadcast_to(lead[bt][t % ROWS : t % ROWS + 1, :], (ROWS, LANES))
        z = jnp.broadcast_to(trail[bu][u % ROWS : u % ROWS + 1, :], (ROWS, LANES))
    for b in range(GROUPS):
        ends_ref[b * ROWS : (b + 1) * ROWS, :] = starts[b]
        ends_ref[MARKERS + b * ROWS : MARKERS + (b + 1) * ROWS, :] = ends[b]
    ends_ref[2 * MARKERS :, :] = inverse / v

    stay = [jnp.log(1.0 - rate) for rate in rates]
    stay[0] = jnp.where(row == 0, 0.0, stay[0])
    stay = jnp.sum(sum(stay), axis=0, keepdims=True)
    marked = jnp.where(low, row, ROWS - 1 - row) >= GROUPS
    logs = []
    for h in range(2):
        cell = marked & (lane >= 2 * ROWS * (h + 1)) & (lane < 2 * ROWS * (h + 1) + ROWS)
        seen = jnp.sum(jnp.where(cell, misc, 0.0), axis=0, keepdims=True)
        seen = jnp.sum(seen, axis=1, keepdims=True) * (1.0 / copies)
        whole = jnp.log(v[0:1, h * HALF : h * HALF + 1]) + stay[:, 0:1] + seen * math.log(SCALE)
        logs.append(whole * (1.0 / MARKERS))
    log_ref[...] = jnp.concatenate(logs, axis=1)


def contract_kernel(weight_ref, t_ref, dose_ref):
    place = lax.axis_index("group")
    low = place < GROUPS // 2
    inward = (place == 1) | (place == GROUPS - 2)
    row, lane = iota((ROWS, LANES), 0), iota((ROWS, LANES), 1)
    folded = (lane % (2 * ROWS)) // ROWS
    side = jnp.where(low, 1, -1)
    turn = jnp.where(low, 0, ROWS - 1)
    order = turn + side * row

    def weights(is_start, block):
        at = jnp.where(is_start, 0, MARKERS) + block * ROWS
        return weight_ref[pl.ds(pl.multiple_of(at, ROWS), ROWS), :]

    picked = weights(jnp.logical_not(low), GROUPS - 1)
    column = (lane % HALF) // (2 * ROWS)
    for b in range(GROUPS - 1):
        picked = jnp.where(column == b, weights(jnp.logical_not(low), b), picked)
    picked = jnp.where(row == lane % ROWS, picked, 0.0)
    across = jnp.sum(picked, axis=0, keepdims=True) * weight_ref[2 * MARKERS : 2 * MARKERS + 1, :]
    far_end = ROWS * column + lane % ROWS

    def reaches(j):
        t = place * ROWS + turn + side * j
        return (far_end - t) * side >= 0

    near = weights(low, place)
    outermost = weights(low, jnp.where(low, 0, GROUPS - 1))
    inner = jnp.where(inward, 1.0, 0.0)
    total = jnp.zeros((ROWS, LANES), F32)

    def select(pair):
        return pair[0] if pair[0] is pair[1] else jnp.where(folded == 0, *pair)

    for subset in range(2):
        slots = SETS[subset] + [None]
        for q in range(SUBSET // ROWS):
            firsts, seconds, shared, moved = [], [], [], []
            for entry in slots[2 * q : 2 * q + 2]:
                if entry is None:
                    firsts.append(-1)
                    seconds.append(-1)
                    shared.append(near)
                    moved.append(near)
                    continue
                shape, block, j = entry
                paired = paired_with(shape, j)
                used = inner if block else 1.0 - inner
                weight = (near if shape == TRIANGLE else outermost) * used
                firsts.append(j)
                seconds.append(paired)
                shared.append(weight)
                if paired < 0:
                    moved.append(weight)
                else:
                    moved.append(jnp.where(low, pltpu.roll(weight, j + 1, 0), pltpu.roll(weight, ROWS - 1 - j, 0)))
            is_square = [entry is not None and entry[0] == SQUARE for entry in slots[2 * q : 2 * q + 2]]
            ends = [ROWS - 1 if square else j for square, j in zip(is_square, firsts)]
            a, second, end = (jnp.where(folded == 0, *pair) for pair in (firsts, seconds, ends))
            own = order <= end
            marker = jnp.where(own, a, second)
            weight = jnp.where(own, select(shared), select(moved)) * across
            at = subset * SUBSET + q * ROWS
            terms = jnp.where((marker >= 0) & reaches(marker), t_ref[at : at + ROWS, :] * weight, 0.0)
            one = jnp.sum(jnp.where(own, terms, 0.0), axis=0, keepdims=True)
            total = total + jnp.where(row == a, one, 0.0)
            if max(seconds) >= 0:
                other = jnp.sum(jnp.where(own, 0.0, terms), axis=0, keepdims=True)
                total = total + jnp.where(row == second, other, 0.0)
    doses = []
    for h in range(2):
        dose = jnp.sum(jnp.where(lane // HALF == h, total, 0.0), axis=1, keepdims=True)
        doses.append(jnp.sum(jnp.where(order == lane, dose, 0.0), axis=0, keepdims=True))
    dose_ref[...] = jnp.concatenate(doses, axis=0)[:, :ROWS]


def exchange(x, axis, by):
    peers = lax.axis_size(axis)
    return lax.ppermute(x, axis, [(i, i ^ by) for i in range(peers)])


def exchange_flat(x, by):
    peers = lax.axis_size("group") * lax.axis_size("batch")
    return lax.ppermute(x, ("group", "batch"), [(i, i ^ by) for i in range(peers)])


def is_odd(bits):
    odd = bits
    for shift in (16, 8, 4, 2, 1):
        odd = odd ^ (odd >> shift)
    return odd & 1


def on_device_windows(panel_alleles, recomb_rates, genotypes):
    width = panel_alleles.shape[1]
    copies = lax.axis_size("batch")
    chunk = width // GROUPS
    place = lax.axis_index("group")
    widths = [chunk * share // sum(SHARES) for share in SHARES]
    shapes = [
        jax.ShapeDtypeStruct((ROWS, part + (LANES if p == 0 else 0)), jnp.int32)
        for p, part in enumerate(widths)
        for d in range(GROUPS)
    ]
    *cuts, misc = pl.pallas_call(
        functools.partial(pack_kernel, widths),
        out_shape=shapes + [jax.ShapeDtypeStruct((ROWS, LANES), F32)],
        in_specs=[pl.BlockSpec(memory_space=pltpu.HBM)] * 3,
        out_specs=[VMEM] * (len(shapes) + 1),
        scratch_shapes=[
            pltpu.SMEM(genotypes.shape, jnp.int32),
            pltpu.SMEM(recomb_rates.shape, F32),
            pltpu.SemaphoreType.DMA((len(shapes) + 2,)),
        ],
        compiler_params=pltpu.CompilerParams(vmem_limit_bytes=4 * 1024 * 1024),
        name="pack",
    )(*(pltpu.with_memory_space_constraint(x, pltpu.HBM) for x in (genotypes, recomb_rates, panel_alleles)))
    arrived = None
    for p in range(len(widths)):
        part = cuts[p * GROUPS : (p + 1) * GROUPS]
        if arrived is not None:
            part[1:], arrived = lax.optimization_barrier((part[1:], arrived))
            cuts[(p - 1) * GROUPS + 1] = arrived
        part = [cut if d == 0 else exchange(cut, "group", d) for d, cut in enumerate(part)]
        cuts[p * GROUPS : (p + 1) * GROUPS] = part
        arrived = part[1]
    tags = [cut[:, widths[0] :] for cut in cuts[:GROUPS]]
    sums = []
    for p, part in enumerate(widths):
        pieces = [cut[:, :part] for cut in cuts[p * GROUPS : (p + 1) * GROUPS]]
        sums.append(
            pl.pallas_call(
                functools.partial(window_kernel, min(256, part)),
                out_shape=jax.ShapeDtypeStruct((2, TALL, LANES), F32),
                in_specs=[VMEM] * (2 * GROUPS),
                out_specs=VMEM,
                scratch_shapes=[
                    pltpu.VMEM((MARKERS, part), jnp.int32),
                    pltpu.VMEM((MARKERS, LANES), jnp.int32),
                    pltpu.VMEM((2, 4 * MARKERS, part), BF16),
                    pltpu.VMEM((2, len(TILES) * 4 * ROWS, part), BF16),
                ],
                compiler_params=pltpu.CompilerParams(vmem_limit_bytes=40 * 1024 * 1024),
                cost_estimate=pl.CostEstimate(flops=part * 900000, bytes_accessed=0, transcendentals=0),
                name="windows",
            )(*pieces, *tags)
        )
    sums = sum(sums)
    shape = (2, 2, SUBSET, LANES)
    rows, lane = iota(shape, 2) - SPARE // 2 * ROWS, iota(shape, 3)
    rows = jnp.where(iota(shape, 0) == 0, rows, ROWS - 1 - rows)
    spare = (rows >= GROUPS) & (rows < ROWS) & (lane % (2 * ROWS) < ROWS)
    misc = jnp.pad(misc, ((SPARE // 2 * ROWS, SUBSET - (SPARE // 2 + 1) * ROWS), (0, 0)))
    sent = jnp.where(spare, misc, sums.reshape(shape)).reshape(2 * TALL, LANES)
    both = sent + exchange(sent, "group", 1)
    half = place // (GROUPS // 2)
    carried = is_odd(place ^ lax.axis_index("batch"))

    def part_of(which):
        start = (2 * which + carried) * SUBSET
        return lax.dynamic_slice_in_dim(both, start, SUBSET)

    core = copies
    kept = part_of(half) + exchange_flat(part_of(1 - half), 2 * core + core)
    by = 1
    while by < copies:
        kept = kept + exchange_flat(kept, by + core)
        by *= 2
    theirs = exchange(kept, "group", 1)
    weights, logs = pl.pallas_call(
        functools.partial(solve_kernel, float(width * copies), float(copies)),
        out_shape=[
            jax.ShapeDtypeStruct((2 * MARKERS + ROWS, LANES), F32),
            jax.ShapeDtypeStruct((1, 2), F32),
        ],
        in_specs=[VMEM],
        out_specs=[VMEM] * 2,
        compiler_params=pltpu.CompilerParams(vmem_limit_bytes=4 * 1024 * 1024),
        cost_estimate=pl.CostEstimate(flops=1000000, bytes_accessed=0, transcendentals=0),
        name="solve",
    )(kept)
    whole = jnp.where(carried == 0, jnp.concatenate([kept, theirs], axis=0), jnp.concatenate([theirs, kept], axis=0))
    dosage = pl.pallas_call(
        contract_kernel,
        out_shape=jax.ShapeDtypeStruct((2, ROWS), F32),
        in_specs=[VMEM] * 2,
        out_specs=VMEM,
        compiler_params=pltpu.CompilerParams(vmem_limit_bytes=4 * 1024 * 1024),
        name="contract",
    )(weights, whole)
    return dosage, logs.reshape(2)


def fits_windows(panel_alleles, genotypes, groups, copies):
    markers, width = panel_alleles.shape
    return (
        groups == GROUPS
        and copies & (copies - 1) == 0
        and markers == ROWS
        and genotypes.shape[0] == 2
        and width % (GROUPS * LANES * 32) == 0
    )


def on_device(panel_alleles, recomb_rates, genotypes):
    groups, copies = lax.axis_size("group"), lax.axis_size("batch")
    if fits_windows(panel_alleles, genotypes, groups, copies):
        return on_device_windows(panel_alleles, recomb_rates, genotypes)
    return on_device_chain(panel_alleles, recomb_rates, genotypes)


def solution(mesh):
    placed = (P("group", "batch"), P("group"), P(None, "group"))
    return jax.shard_map(
        on_device, mesh=mesh, in_specs=placed, out_specs=(P(None, "group"), P()), check_vma=False
    )
```

```python
import functools
import math

import jax
import jax.numpy as jnp
from jax import lax
from jax.experimental import pallas as pl
from jax.experimental.pallas import tpu as pltpu
from jax.sharding import PartitionSpec as P

MISMATCH = 0.05
HIGHEST = lax.Precision.HIGHEST


def haplotypes(panel_rows):
    return panel_rows.shape[1] * lax.axis_size("batch")


def from_behind(x, axis, by):
    peers = lax.axis_size(axis)
    pairs = [(i, i + by) for i in range(peers) if 0 <= i + by < peers]
    return lax.ppermute(x, axis, pairs)


def emission(panel_rows, geno_col):
    observed = geno_col[:, None]
    agrees = jnp.where(panel_rows == observed, 1.0 - MISMATCH, MISMATCH)
    return jnp.where(observed == 2, 1.0, agrees).astype(jnp.float32)


def forward_terms(panel_rows, geno_col, switches):
    emitted = emission(panel_rows, geno_col)
    retain = emitted * (1.0 - switches)[:, None]
    inject = emitted * (switches / haplotypes(panel_rows))[:, None]
    return (retain, inject, None)


def backward_terms(panel_rows, geno_col, switches):
    emitted = emission(panel_rows, geno_col)[::-1]
    flipped = switches[::-1]
    retain = emitted * (1.0 - flipped)[:, None]
    inject = jnp.broadcast_to((flipped / haplotypes(panel_rows))[:, None], emitted.shape)
    return (retain, inject, emitted)


def partial_sums(entering, retain, inject, weight, extent):
    logs = jnp.cumsum(jnp.log(retain), axis=0)
    shifted = jnp.concatenate([jnp.zeros_like(entering)[None], logs[: extent - 1]], axis=0)
    before = jnp.exp(shifted)
    left_side = before if weight is None else weight * before
    leading = jnp.einsum("jk,k->j", left_side, entering, precision=HIGHEST)
    anchor = shifted[0]
    right_side = inject * jnp.exp(anchor[None] - logs)
    nearby = jnp.exp(jnp.minimum(shifted - anchor[None], 0.0))
    nearby = nearby if weight is None else weight * nearby
    columns = [jnp.einsum("jk,tk->jt", nearby, right_side, precision=HIGHEST)]
    coupling = jnp.concatenate(columns, axis=1)
    return (leading, coupling)


def solve_sums(leading, coupling):
    columns = coupling.shape[1]

    def settle(marker, sigmas):
        below = jnp.arange(columns) < marker
        update = leading[marker] + jnp.sum(
            jnp.where(below, coupling[marker] * sigmas[:columns], 0.0)
        )
        return sigmas.at[marker].set(update)

    return lax.fori_loop(0, leading.shape[0], settle, jnp.zeros_like(leading))


def advance(entering, retain, inject, sigmas, keep_states):

    def advance_single(current, pieces):
        current = pieces[0] * current + pieces[1] * pieces[2]
        return (current, current if keep_states else None)

    return lax.scan(advance_single, entering, (retain, inject, sigmas[: retain.shape[0]]))


def place_rows(store, block, active):
    return jnp.where(active, block, store)


def on_device_chain(panel_alleles, recomb_rates, genotypes):
    chain_size = lax.axis_size("group")
    position = lax.axis_index("group")
    markers, width = panel_alleles.shape
    targets = genotypes.shape[0]
    bundles = targets // targets
    uniform = jnp.full((targets, width), 1.0 / haplotypes(panel_alleles), jnp.float32)
    first_row = position == 0
    last_row = position == chain_size - 1

    def local_sums(active, arrivals, geno_rows, maker, extent):

        def local_compute():

            def local_single(pieces):
                retain, inject, weight = maker(panel_alleles, pieces[1], recomb_rates)
                return partial_sums(pieces[0], retain, inject, weight, extent)

            return lax.map(local_single, (arrivals, geno_rows))

        def local_skipped():
            return (
                jnp.zeros((targets, extent), jnp.float32),
                jnp.zeros((targets, extent, markers), jnp.float32),
            )

        return lax.cond(active, local_compute, local_skipped)

    def outgoing(active, arrivals, geno_rows, sigmas, maker, scale_row):

        def outgoing_compute():

            def outgoing_single(pieces):
                retain, inject, weight = maker(panel_alleles, pieces[1], recomb_rates)
                ending, unused = advance(pieces[0], retain, inject, pieces[2], False)
                return ending / pieces[2][scale_row]

            return lax.map(outgoing_single, (arrivals, geno_rows, sigmas))

        def outgoing_skipped():
            return jnp.zeros((targets, width), jnp.float32)

        return lax.cond(active, outgoing_compute, outgoing_skipped)

    def moment_step(moment, carried_state):
        (
            sent_forward,
            sent_backward,
            sent_running,
            store_forward,
            store_backward,
            sigma_forward,
            sigma_backward,
            log_terms,
        ) = carried_state
        got_forward = from_behind(sent_forward, "group", 1)
        got_backward = from_behind(sent_backward, "group", -1)
        entering_forward = jnp.where(first_row, uniform, got_forward)
        entering_backward = jnp.where(last_row, uniform, got_backward)
        index_forward = moment - position
        index_backward = moment - (chain_size - 1 - position)
        active_forward = (index_forward >= 0) & (index_forward < bundles)
        active_backward = (index_backward >= 0) & (index_backward < bundles)
        lead_forward, couple_forward = local_sums(
            active_forward, entering_forward, genotypes, forward_terms, markers + 1
        )
        lead_backward, couple_backward = local_sums(
            active_backward, entering_backward, genotypes, backward_terms, markers
        )
        lead_forward, couple_forward, lead_backward, couple_backward = lax.psum(
            (lead_forward, couple_forward, lead_backward, couple_backward), "batch"
        )
        sigmas_forward = jax.vmap(solve_sums)(lead_forward, couple_forward)
        sigmas_backward = jax.vmap(solve_sums)(lead_backward, couple_backward)
        next_forward = outgoing(
            active_forward, entering_forward, genotypes, sigmas_forward, forward_terms, markers
        )
        next_backward = outgoing(
            active_backward,
            entering_backward,
            genotypes,
            sigmas_backward,
            backward_terms,
            markers - 1,
        )
        guarded = jnp.where(active_forward, sigmas_forward[:, markers], 1.0)
        running = jnp.log(guarded)
        store_forward = place_rows(store_forward, entering_forward, active_forward)
        store_backward = place_rows(store_backward, entering_backward, active_backward)
        sigma_forward = place_rows(sigma_forward, sigmas_forward, active_forward)
        sigma_backward = place_rows(sigma_backward, sigmas_backward, active_backward)
        log_terms = place_rows(log_terms, running, active_forward)
        return (
            next_forward,
            next_backward,
            running,
            store_forward,
            store_backward,
            sigma_forward,
            sigma_backward,
            log_terms,
        )

    initial = (
        jnp.zeros((targets, width), jnp.float32),
        jnp.zeros((targets, width), jnp.float32),
        jnp.zeros((targets,), jnp.float32),
        jnp.zeros((targets, width), jnp.float32),
        jnp.zeros((targets, width), jnp.float32),
        jnp.zeros((targets, markers + 1), jnp.float32),
        jnp.zeros((targets, markers), jnp.float32),
        jnp.zeros((targets,), jnp.float32),
    )
    final_state = lax.fori_loop(0, chain_size + bundles - 1, moment_step, initial)
    store_forward, store_backward, sigma_forward, sigma_backward, log_terms = final_state[3:]
    whole_log = lax.psum(log_terms, "group")
    log_likelihood = whole_log / (markers * chain_size)

    def posterior(pieces):
        entering_ahead, entering_behind, geno_col, sigmas_ahead, sigmas_behind = pieces
        retain, inject, weight = forward_terms(panel_alleles, geno_col, recomb_rates)
        unused_f, forward_states = advance(entering_ahead, retain, inject, sigmas_ahead, True)
        forward_rows = forward_states / sigmas_ahead[1:, None]
        retain, inject, weight = backward_terms(panel_alleles, geno_col, recomb_rates)
        unused_b, backward_states = advance(entering_behind, retain, inject, sigmas_behind, True)
        scaled_back = backward_states[:-1] / sigmas_behind[:-1, None]
        backward_rows = jnp.concatenate([entering_behind[None], scaled_back], axis=0)[::-1]
        product = forward_rows * backward_rows
        numerator = jnp.sum(jnp.where(panel_alleles == 1, product, 0.0), axis=1)
        return (numerator, jnp.sum(product, axis=1))

    numerator, denominator = lax.map(
        posterior, (store_forward, store_backward, genotypes, sigma_forward, sigma_backward)
    )
    numerator, denominator = lax.psum((numerator, denominator), "batch")
    return (numerator / denominator, log_likelihood)


ROWS, LANES = 8, 128
HALF = LANES // 2
GROUPS = 4
SHARES = (9, 7)
MISSING = 2
SCALE = math.sqrt(MISMATCH * (1.0 - MISMATCH))
HALF_STEP = 0.5 * math.log((1.0 - MISMATCH) / MISMATCH)
VMEM = pl.BlockSpec(memory_space=pltpu.VMEM)
SMEM = pl.BlockSpec(memory_space=pltpu.SMEM)
F32, BF16 = jnp.float32, jnp.bfloat16


def iota(shape, axis):
    return lax.broadcasted_iota(jnp.int32, shape, axis)


MARKERS = ROWS * GROUPS
HALF_T = MARKERS // 2
SUBSET = 5 * ROWS
TALL = 2 * SUBSET
TRIANGLE, SQUARE = 0, 1
SETS = [
    [(TRIANGLE, 0, 0), (TRIANGLE, 0, 1), (TRIANGLE, 0, 3)]
    + [(TRIANGLE, 1, a) for a in (0, 1, 2, 7)]
    + [(SQUARE, 1, j) for j in (0, 1)],
    [(TRIANGLE, 0, 2), (TRIANGLE, 0, 7), (TRIANGLE, 1, 3)] + [(SQUARE, 1, j) for j in range(2, ROWS)],
]
TILES = SETS[0] + SETS[1]
TUCKED = [(1, 1), (1, 2), (1, 3), (2, 2), (2, 3), (3, 3)]
FIRST_TUCKED = 3
SPARE = 2


def paired_with(shape, a):
    return ROWS - 2 - a if shape == TRIANGLE and a < 3 else -1


def pack_kernel(widths, geno_ref, rate_ref, panel_ref, *refs):
    outs, (misc_ref, genos, rates_in, sems) = refs[:-4], refs[-4:]
    place = lax.axis_index("group")
    chunk = panel_ref.shape[1] // GROUPS
    copies = []
    for n, ref in enumerate(outs):
        d, p = n % GROUPS, n // GROUPS
        part = widths[p]
        start = pl.multiple_of((place ^ d) * chunk + sum(widths[:p]), LANES)
        copies.append(
            pltpu.make_async_copy(panel_ref.at[:, pl.ds(start, part)], ref.at[:, pl.ds(0, part)], sems.at[n])
        )
    small = [
        pltpu.make_async_copy(geno_ref, genos, sems.at[len(outs)]),
        pltpu.make_async_copy(rate_ref, rates_in, sems.at[len(outs) + 1]),
    ]
    for copy in small + copies:
        copy.start()
    for copy in small:
        copy.wait()
    row, lane = iota((ROWS, LANES), 0), iota((ROWS, LANES), 1)
    tile = jnp.zeros((ROWS, LANES), jnp.int32)
    misc = jnp.zeros((ROWS, LANES), F32)
    for i in range(ROWS):
        tile = jnp.where(row == i, jnp.where(lane < HALF, genos[0, i], genos[1, i]), tile)
        misc = jnp.where(lane == i, rates_in[i], misc)
        for h in range(2):
            known = jnp.where(genos[h, i] == MISSING, 0.0, 1.0)
            misc = jnp.where(lane == 2 * ROWS * (h + 1) + i, known, misc)
    for ref in outs[:GROUPS]:
        ref[:, widths[0] :] = tile
    misc_ref[...] = jnp.where((row == GROUPS + place) | (row == GROUPS - 1 - place), misc, 0.0)
    for copy in copies:
        copy.wait()


def window_kernel(step, has_misc, *refs):
    pieces, geno_refs = refs[:GROUPS], refs[GROUPS : 2 * GROUPS]
    misc_ref, t_ref, panel, genos, wide, left = refs[2 * GROUPS :]
    place = lax.axis_index("group")
    columns = panel.shape[1]
    for d in range(GROUPS):
        rows = pl.ds(pl.multiple_of((place ^ d) * ROWS, ROWS), ROWS)
        panel[rows, :] = pieces[d][...]
        genos[rows, :] = geno_refs[d][...]

    r, j = iota((4 * MARKERS, 2 * MARKERS), 0), iota((4 * MARKERS, 2 * MARKERS), 1)
    same = r // (2 * MARKERS) == j // MARKERS
    prefix, marker = (r // MARKERS) % 2 == 0, r % MARKERS
    at = j % MARKERS
    sums = jnp.where(prefix, jnp.where(at <= marker, 1.0, 0.0), jnp.where(at < marker, -1.0, 0.0))
    sums = jnp.where(same, sums, 0.0).astype(BF16)

    for start in range(0, columns, step):
        here = slice(start, start + step)
        signs = []
        for h in range(2):
            for b in range(GROUPS):
                rows = slice(b * ROWS, (b + 1) * ROWS)
                seen = genos[rows, h * HALF : h * HALF + 1]
                agrees = jnp.where(panel[rows, here] == seen, 1.0, -1.0)
                signs.append(jnp.where(seen == MISSING, 0.0, agrees))
        signs = jnp.concatenate(signs, axis=0).astype(BF16)
        power = jnp.dot(sums, signs, preferred_element_type=F32)
        value = jnp.exp(power * HALF_STEP)
        upper = value.astype(BF16).astype(F32)
        lower = value - upper
        blocks = {}
        for h in range(2):
            for kind in range(2):
                for b in range(GROUPS):
                    at = h * 2 * MARKERS + kind * MARKERS + b * ROWS
                    both = jnp.concatenate([upper[at : at + ROWS], lower[at : at + ROWS]], axis=0).astype(BF16)
                    blocks[kind, h, b] = both
                    wide[kind, (h * GROUPS + b) * 2 * ROWS : (h * GROUPS + b + 1) * 2 * ROWS, here] = both
        row = iota((ROWS, step), 0)
        for half in range(2):
            for slot, (shape, block, j) in enumerate(TILES):
                paired = paired_with(shape, j)
                outer = 0 if half == 0 else GROUPS - 1
                own = abs(outer - block)
                near = own if shape == TRIANGLE else outer
                first = row <= j if half == 0 else row >= ROWS - 1 - j

                def carries(j):
                    t = own * ROWS + (j if half == 0 else ROWS - 1 - j)
                    return jnp.broadcast_to(panel[t : t + 1, here], (ROWS, step)).astype(F32)

                mask = carries(j) if paired < 0 else jnp.where(first, carries(j), carries(paired))
                mask = jnp.concatenate([mask, mask], axis=0).astype(BF16)
                for h in range(2):
                    base = blocks[1 - half, h, near]
                    if paired >= 0:
                        at = h * 2 * MARKERS + (1 - half) * MARKERS + near * ROWS
                        shift = j + 1 if half == 0 else ROWS - 1 - j
                        both = [x[at : at + ROWS] for x in (upper, lower)]
                        both = [jnp.where(first, x, pltpu.roll(x, shift, 0)) for x in both]
                        base = jnp.concatenate(both, axis=0).astype(BF16)
                    at = (slot * 2 + h) * 2 * ROWS
                    left[half, at : at + 2 * ROWS, here] = base * mask

    def product(a, b):
        return lax.dot_general(a, b, (((1,), (1,)), ((), ())), preferred_element_type=F32)

    lane = iota((ROWS, LANES), 1)
    first = lane % (2 * ROWS) < ROWS

    def rows_of(acc, slot):
        return acc[slot * 2 * ROWS : slot * 2 * ROWS + ROWS] + acc[slot * 2 * ROWS + ROWS : (slot + 1) * 2 * ROWS]

    def fold(a, b):
        return jnp.where(first, a + pltpu.roll(a, LANES - ROWS, 1), b + pltpu.roll(b, ROWS, 1))

    def both_targets(acc, slots):
        return jnp.where(lane < HALF, rows_of(acc, slots[0]), rows_of(acc, slots[1]))

    def unfold(tile, column, to_column, odd):
        shift = 2 * ROWS * (to_column - column) + ROWS * odd
        tile = tile + pltpu.roll(tile, LANES - ROWS, 1)
        return tile if shift == 0 else pltpu.roll(tile, shift % LANES, 1)

    row = iota((ROWS, LANES), 0)
    misc = misc_ref[...] if has_misc else jnp.zeros((ROWS, LANES), F32)
    sums_e = product(wide[1], wide[0])
    plain = [both_targets(sums_e, [b, GROUPS + b]) for b in range(GROUPS)]
    column = (lane % HALF) // (2 * ROWS)
    for half in range(2):
        outer = 0 if half == 0 else GROUPS - 1
        sums_t = product(left[half], wide[half])
        tucked = {}
        for n, (b, to) in enumerate(TUCKED):
            slot = FIRST_TUCKED + n
            moved = unfold(plain[b], to, outer, slot % 2)
            here = (column == outer) & (first if slot % 2 == 0 else jnp.logical_not(first))
            tucked.setdefault(slot // 2, []).append((here, moved))
        for subset in range(2):
            base = subset * len(SETS[0])
            tiles = [both_targets(sums_t, [2 * n, 2 * n + 1]) for n in range(base, base + len(SETS[subset]))] + [plain[0]]
            for q in range(SUBSET // ROWS):
                value = fold(tiles[2 * q], tiles[2 * q + 1])
                for here, moved in tucked.get(q, []):
                    value = jnp.where(here, moved, value)
                if q == SPARE // 2:
                    spare = row >= GROUPS if half == 0 else row < GROUPS
                    value = jnp.where(spare & first, misc, value)
                at = subset * SUBSET + q * ROWS
                t_ref[half, at : at + ROWS, :] = value


def solve_kernel(panel_size, copies, sum_ref, ends_ref):
    low = lax.axis_index("group") < GROUPS // 2
    row, lane = iota((ROWS, LANES), 0), iota((ROWS, LANES), 1)
    target = lane // HALF
    folded = (lane % (2 * ROWS)) // ROWS
    column_of = (lane % HALF) // (2 * ROWS)
    misc = sum_ref[SPARE // 2 * ROWS : (SPARE // 2 + 1) * ROWS, :]

    def spread(tile, at):
        return jnp.broadcast_to(tile[:, at : at + 1], (ROWS, LANES))

    def drawn(slot, to, odd):
        tile = sum_ref[slot // 2 * ROWS : (slot // 2 + 1) * ROWS, :]
        shifts = [2 * ROWS * (to - outer) + ROWS * (odd - slot % 2) for outer in (0, GROUPS - 1)]
        return jnp.where(low, *(pltpu.roll(tile, shift % LANES, 1) if shift else tile for shift in shifts))

    last = sum_ref[SUBSET - ROWS :, :]
    pair = [jnp.where(folded == 0, pltpu.roll(last, LANES - ROWS, 1), 0.0), jnp.zeros((ROWS, LANES), F32)]
    for n, (b, to) in enumerate(TUCKED):
        here = (column_of == to) & (folded == b % 2)
        pair[b // 2] = jnp.where(here, drawn(FIRST_TUCKED + n, to, b % 2), pair[b // 2])
    square = jnp.concatenate(pair + [misc, jnp.zeros((LANES - 3 * ROWS, LANES), F32)], axis=0)
    turned = jnp.transpose(square)

    listed = turned[:ROWS] * (1.0 / copies)
    spare = GROUPS * ROWS // 2
    rates = [jnp.where(low, spread(listed, spare + GROUPS + b), spread(listed, spare + GROUPS - 1 - b)) for b in range(GROUPS)]
    odds = [rate / (1.0 - rate) for rate in rates]
    inverse = 1.0 / panel_size
    ahead = []
    for b in range(GROUPS):
        following = odds[b + 1][0:1, :] if b + 1 < GROUPS else jnp.ones((1, LANES), F32)
        ahead.append(jnp.concatenate([odds[b][1:, :], following], axis=0) * inverse)
    behind = [odd * inverse for odd in odds]

    trail_tiles = []
    for q in range(GROUPS // 2):
        factor = jnp.where(folded == 0, behind[2 * q], behind[2 * q + 1])
        trail_tiles.append(pair[q] * factor)

    def turned_tile(h, b, f):
        at = h * HALF + b * 2 * ROWS + f * ROWS
        return turned[at : at + ROWS] * ahead[b]

    lead_tiles = {(h, b, f): turned_tile(h, b, f) for h in range(2) for b in range(GROUPS) for f in range(2)}

    def lead_column(t, b):
        s, at = t // ROWS, (t // ROWS // 2) * ROWS + t % ROWS
        return jnp.where(target == 0, spread(lead_tiles[0, b, s % 2], at), spread(lead_tiles[1, b, s % 2], at))

    def trail_column(t, b):
        at = 2 * ROWS * (t // ROWS) + t % ROWS + ROWS * (b % 2)
        tile = trail_tiles[b // 2]
        return jnp.where(target == 0, spread(tile, at), spread(tile, HALF + at))

    zero = jnp.zeros((ROWS, LANES), F32)
    lead, trail, starts, ends = [zero] * GROUPS, [zero] * GROUPS, [zero] * GROUPS, [zero] * GROUPS
    v = jnp.ones((ROWS, LANES), F32)
    z = jnp.ones((ROWS, LANES), F32)
    for t in range(MARKERS):
        u = MARKERS - 1 - t
        bt, bu = t // ROWS, u // ROWS
        starts[bt] = jnp.where(row == t % ROWS, v, starts[bt])
        ends[bu] = jnp.where(row == u % ROWS, z, ends[bu])
        for b in range(bt, GROUPS):
            lead[b] = lead[b] + v * lead_column(t, b)
        for b in range(bu + 1):
            trail[b] = trail[b] + z * trail_column(u, b)
        v = jnp.broadcast_to(lead[bt][t % ROWS : t % ROWS + 1, :], (ROWS, LANES))
        z = jnp.broadcast_to(trail[bu][u % ROWS : u % ROWS + 1, :], (ROWS, LANES))
    for b in range(GROUPS):
        ends_ref[b * ROWS : (b + 1) * ROWS, :] = starts[b]
        ends_ref[MARKERS + b * ROWS : MARKERS + (b + 1) * ROWS, :] = ends[b]

    stay = [jnp.log(1.0 - rate) for rate in rates]
    stay[0] = jnp.where(row == 0, 0.0, stay[0])
    stay = jnp.sum(sum(stay), axis=0, keepdims=True)
    marked = jnp.where(low, row, ROWS - 1 - row) >= GROUPS
    logs = []
    for h in range(2):
        cell = marked & (lane >= 2 * ROWS * (h + 1)) & (lane < 2 * ROWS * (h + 1) + ROWS)
        seen = jnp.sum(jnp.where(cell, misc, 0.0), axis=0, keepdims=True)
        seen = jnp.sum(seen, axis=1, keepdims=True) * (1.0 / copies)
        whole = jnp.log(v[0:1, h * HALF : h * HALF + 1]) + stay[:, 0:1] + seen * math.log(SCALE)
        logs.append(whole * (1.0 / MARKERS))
    ends_ref[2 * MARKERS :, :] = jnp.where(row == 0, inverse / v, jnp.where(target == 0, *logs))


def contract_kernel(weight_ref, t_ref, dose_ref, log_ref):
    place = lax.axis_index("group")
    low = place < GROUPS // 2
    inward = (place == 1) | (place == GROUPS - 2)
    row, lane = iota((ROWS, LANES), 0), iota((ROWS, LANES), 1)
    folded = (lane % (2 * ROWS)) // ROWS
    side = jnp.where(low, 1, -1)
    turn = jnp.where(low, 0, ROWS - 1)
    order = turn + side * row

    def weights(is_start, block):
        at = jnp.where(is_start, 0, MARKERS) + block * ROWS
        return weight_ref[pl.ds(pl.multiple_of(at, ROWS), ROWS), :]

    picked = weights(jnp.logical_not(low), GROUPS - 1)
    column = (lane % HALF) // (2 * ROWS)
    for b in range(GROUPS - 1):
        picked = jnp.where(column == b, weights(jnp.logical_not(low), b), picked)
    picked = jnp.where(row == lane % ROWS, picked, 0.0)
    across = jnp.sum(picked, axis=0, keepdims=True) * weight_ref[2 * MARKERS : 2 * MARKERS + 1, :]
    far_end = ROWS * column + lane % ROWS

    def reaches(j):
        t = place * ROWS + turn + side * j
        return (far_end - t) * side >= 0

    near = weights(low, place)
    outermost = weights(low, jnp.where(low, 0, GROUPS - 1))
    inner = jnp.where(inward, 1.0, 0.0)
    total = jnp.zeros((ROWS, LANES), F32)

    def select(pair):
        return pair[0] if pair[0] is pair[1] else jnp.where(folded == 0, *pair)

    for subset in range(2):
        slots = SETS[subset] + [None]
        for q in range(SUBSET // ROWS):
            firsts, seconds, shared, moved = [], [], [], []
            for entry in slots[2 * q : 2 * q + 2]:
                if entry is None:
                    firsts.append(-1)
                    seconds.append(-1)
                    shared.append(near)
                    moved.append(near)
                    continue
                shape, block, j = entry
                paired = paired_with(shape, j)
                used = inner if block else 1.0 - inner
                weight = (near if shape == TRIANGLE else outermost) * used
                firsts.append(j)
                seconds.append(paired)
                shared.append(weight)
                if paired < 0:
                    moved.append(weight)
                else:
                    moved.append(jnp.where(low, pltpu.roll(weight, j + 1, 0), pltpu.roll(weight, ROWS - 1 - j, 0)))
            is_square = [entry is not None and entry[0] == SQUARE for entry in slots[2 * q : 2 * q + 2]]
            ends = [ROWS - 1 if square else j for square, j in zip(is_square, firsts)]
            a, second, end = (jnp.where(folded == 0, *pair) for pair in (firsts, seconds, ends))
            own = order <= end
            marker = jnp.where(own, a, second)
            weight = jnp.where(own, select(shared), select(moved)) * across
            at = subset * SUBSET + q * ROWS
            terms = jnp.where((marker >= 0) & reaches(marker), t_ref[at : at + ROWS, :] * weight, 0.0)
            one = jnp.sum(jnp.where(own, terms, 0.0), axis=0, keepdims=True)
            total = total + jnp.where(row == a, one, 0.0)
            if max(seconds) >= 0:
                other = jnp.sum(jnp.where(own, 0.0, terms), axis=0, keepdims=True)
                total = total + jnp.where(row == second, other, 0.0)
    doses = []
    for h in range(2):
        dose = jnp.sum(jnp.where(lane // HALF == h, total, 0.0), axis=1, keepdims=True)
        doses.append(jnp.sum(jnp.where(order == lane, dose, 0.0), axis=0, keepdims=True))
    dose_ref[...] = jnp.concatenate(doses, axis=0)[:, :ROWS]
    logs = weight_ref[2 * MARKERS + 1 : 2 * MARKERS + 2, :]
    log_ref[...] = jnp.concatenate([logs[:, :1], logs[:, HALF : HALF + 1]], axis=1)


def exchange(x, axis, by):
    peers = lax.axis_size(axis)
    return lax.ppermute(x, axis, [(i, i ^ by) for i in range(peers)])


def exchange_flat(x, by):
    peers = lax.axis_size("group") * lax.axis_size("batch")
    return lax.ppermute(x, ("group", "batch"), [(i, i ^ by) for i in range(peers)])


def is_odd(bits):
    odd = bits
    for shift in (16, 8, 4, 2, 1):
        odd = odd ^ (odd >> shift)
    return odd & 1


def on_device_windows(panel_alleles, recomb_rates, genotypes):
    width = panel_alleles.shape[1]
    copies = lax.axis_size("batch")
    chunk = width // GROUPS
    place = lax.axis_index("group")
    widths = [chunk * share // sum(SHARES) for share in SHARES]
    shapes = [
        jax.ShapeDtypeStruct((ROWS, part + (LANES if p == 0 else 0)), jnp.int32)
        for p, part in enumerate(widths)
        for d in range(GROUPS)
    ]
    *cuts, misc = pl.pallas_call(
        functools.partial(pack_kernel, widths),
        out_shape=shapes + [jax.ShapeDtypeStruct((ROWS, LANES), F32)],
        in_specs=[pl.BlockSpec(memory_space=pltpu.HBM)] * 3,
        out_specs=[VMEM] * (len(shapes) + 1),
        scratch_shapes=[
            pltpu.SMEM(genotypes.shape, jnp.int32),
            pltpu.SMEM(recomb_rates.shape, F32),
            pltpu.SemaphoreType.DMA((len(shapes) + 2,)),
        ],
        compiler_params=pltpu.CompilerParams(vmem_limit_bytes=4 * 1024 * 1024),
        name="pack",
    )(*(pltpu.with_memory_space_constraint(x, pltpu.HBM) for x in (genotypes, recomb_rates, panel_alleles)))
    arrived = None
    for p in range(len(widths)):
        part = cuts[p * GROUPS : (p + 1) * GROUPS]
        if arrived is not None:
            part[1:], arrived = lax.optimization_barrier((part[1:], arrived))
            cuts[(p - 1) * GROUPS + 1] = arrived
        part = [cut if d == 0 else exchange(cut, "group", d) for d, cut in enumerate(part)]
        cuts[p * GROUPS : (p + 1) * GROUPS] = part
        arrived = part[1]
    tags = [cut[:, widths[0] :] for cut in cuts[:GROUPS]]
    sums = []
    for p, part in enumerate(widths):
        pieces = [cut[:, :part] for cut in cuts[p * GROUPS : (p + 1) * GROUPS]]
        sums.append(
            pl.pallas_call(
                functools.partial(window_kernel, min(256, part), p == 0),
                out_shape=jax.ShapeDtypeStruct((2, TALL, LANES), F32),
                in_specs=[VMEM] * (2 * GROUPS + 1),
                out_specs=VMEM,
                scratch_shapes=[
                    pltpu.VMEM((MARKERS, part), jnp.int32),
                    pltpu.VMEM((MARKERS, LANES), jnp.int32),
                    pltpu.VMEM((2, 4 * MARKERS, part), BF16),
                    pltpu.VMEM((2, len(TILES) * 4 * ROWS, part), BF16),
                ],
                compiler_params=pltpu.CompilerParams(vmem_limit_bytes=40 * 1024 * 1024),
                cost_estimate=pl.CostEstimate(flops=part * 900000, bytes_accessed=0, transcendentals=0),
                name="windows",
            )(*pieces, *tags, misc)
        )
    sums = sum(sums)
    sent = sums.reshape(2 * TALL, LANES)
    both = sent + exchange(sent, "group", 1)
    half = place // (GROUPS // 2)
    carried = is_odd(place ^ lax.axis_index("batch"))

    def part_of(which):
        start = (2 * which + carried) * SUBSET
        return lax.dynamic_slice_in_dim(both, start, SUBSET)

    core = copies
    kept = part_of(half) + exchange_flat(part_of(1 - half), 2 * core + core)
    by = 1
    while by < copies:
        kept = kept + exchange_flat(kept, by + core)
        by *= 2
    theirs = exchange(kept, "group", 1)
    weights = pl.pallas_call(
        functools.partial(solve_kernel, float(width * copies), float(copies)),
        out_shape=jax.ShapeDtypeStruct((2 * MARKERS + ROWS, LANES), F32),
        in_specs=[VMEM],
        out_specs=VMEM,
        compiler_params=pltpu.CompilerParams(vmem_limit_bytes=4 * 1024 * 1024),
        cost_estimate=pl.CostEstimate(flops=1000000, bytes_accessed=0, transcendentals=0),
        name="solve",
    )(kept)
    whole = jnp.where(carried == 0, jnp.concatenate([kept, theirs], axis=0), jnp.concatenate([theirs, kept], axis=0))
    dosage, logs = pl.pallas_call(
        contract_kernel,
        out_shape=[jax.ShapeDtypeStruct((2, ROWS), F32), jax.ShapeDtypeStruct((1, 2), F32)],
        in_specs=[VMEM] * 2,
        out_specs=[VMEM] * 2,
        compiler_params=pltpu.CompilerParams(vmem_limit_bytes=4 * 1024 * 1024),
        name="contract",
    )(weights, whole)
    return dosage, logs.reshape(2)


def fits_windows(panel_alleles, genotypes, groups, copies):
    markers, width = panel_alleles.shape
    return (
        groups == GROUPS
        and copies & (copies - 1) == 0
        and markers == ROWS
        and genotypes.shape[0] == 2
        and width % (GROUPS * LANES * 32) == 0
    )


def on_device(panel_alleles, recomb_rates, genotypes):
    groups, copies = lax.axis_size("group"), lax.axis_size("batch")
    if fits_windows(panel_alleles, genotypes, groups, copies):
        return on_device_windows(panel_alleles, recomb_rates, genotypes)
    return on_device_chain(panel_alleles, recomb_rates, genotypes)


def solution(mesh):
    placed = (P("group", "batch"), P("group"), P(None, "group"))
    return jax.shard_map(
        on_device, mesh=mesh, in_specs=placed, out_specs=(P(None, "group"), P()), check_vma=False
    )
```

```python
import functools
import math

import jax
import jax.numpy as jnp
from jax import lax
from jax.experimental import pallas as pl
from jax.experimental.pallas import tpu as pltpu
from jax.sharding import PartitionSpec as P

MISMATCH = 0.05
HIGHEST = lax.Precision.HIGHEST


def haplotypes(panel_rows):
    return panel_rows.shape[1] * lax.axis_size("batch")


def from_behind(x, axis, by):
    peers = lax.axis_size(axis)
    pairs = [(i, i + by) for i in range(peers) if 0 <= i + by < peers]
    return lax.ppermute(x, axis, pairs)


def emission(panel_rows, geno_col):
    observed = geno_col[:, None]
    agrees = jnp.where(panel_rows == observed, 1.0 - MISMATCH, MISMATCH)
    return jnp.where(observed == 2, 1.0, agrees).astype(jnp.float32)


def forward_terms(panel_rows, geno_col, switches):
    emitted = emission(panel_rows, geno_col)
    retain = emitted * (1.0 - switches)[:, None]
    inject = emitted * (switches / haplotypes(panel_rows))[:, None]
    return (retain, inject, None)


def backward_terms(panel_rows, geno_col, switches):
    emitted = emission(panel_rows, geno_col)[::-1]
    flipped = switches[::-1]
    retain = emitted * (1.0 - flipped)[:, None]
    inject = jnp.broadcast_to((flipped / haplotypes(panel_rows))[:, None], emitted.shape)
    return (retain, inject, emitted)


def partial_sums(entering, retain, inject, weight, extent):
    logs = jnp.cumsum(jnp.log(retain), axis=0)
    shifted = jnp.concatenate([jnp.zeros_like(entering)[None], logs[: extent - 1]], axis=0)
    before = jnp.exp(shifted)
    left_side = before if weight is None else weight * before
    leading = jnp.einsum("jk,k->j", left_side, entering, precision=HIGHEST)
    anchor = shifted[0]
    right_side = inject * jnp.exp(anchor[None] - logs)
    nearby = jnp.exp(jnp.minimum(shifted - anchor[None], 0.0))
    nearby = nearby if weight is None else weight * nearby
    columns = [jnp.einsum("jk,tk->jt", nearby, right_side, precision=HIGHEST)]
    coupling = jnp.concatenate(columns, axis=1)
    return (leading, coupling)


def solve_sums(leading, coupling):
    columns = coupling.shape[1]

    def settle(marker, sigmas):
        below = jnp.arange(columns) < marker
        update = leading[marker] + jnp.sum(
            jnp.where(below, coupling[marker] * sigmas[:columns], 0.0)
        )
        return sigmas.at[marker].set(update)

    return lax.fori_loop(0, leading.shape[0], settle, jnp.zeros_like(leading))


def advance(entering, retain, inject, sigmas, keep_states):

    def advance_single(current, pieces):
        current = pieces[0] * current + pieces[1] * pieces[2]
        return (current, current if keep_states else None)

    return lax.scan(advance_single, entering, (retain, inject, sigmas[: retain.shape[0]]))


def place_rows(store, block, active):
    return jnp.where(active, block, store)


def on_device_chain(panel_alleles, recomb_rates, genotypes):
    chain_size = lax.axis_size("group")
    position = lax.axis_index("group")
    markers, width = panel_alleles.shape
    targets = genotypes.shape[0]
    bundles = targets // targets
    uniform = jnp.full((targets, width), 1.0 / haplotypes(panel_alleles), jnp.float32)
    first_row = position == 0
    last_row = position == chain_size - 1

    def local_sums(active, arrivals, geno_rows, maker, extent):

        def local_compute():

            def local_single(pieces):
                retain, inject, weight = maker(panel_alleles, pieces[1], recomb_rates)
                return partial_sums(pieces[0], retain, inject, weight, extent)

            return lax.map(local_single, (arrivals, geno_rows))

        def local_skipped():
            return (
                jnp.zeros((targets, extent), jnp.float32),
                jnp.zeros((targets, extent, markers), jnp.float32),
            )

        return lax.cond(active, local_compute, local_skipped)

    def outgoing(active, arrivals, geno_rows, sigmas, maker, scale_row):

        def outgoing_compute():

            def outgoing_single(pieces):
                retain, inject, weight = maker(panel_alleles, pieces[1], recomb_rates)
                ending, unused = advance(pieces[0], retain, inject, pieces[2], False)
                return ending / pieces[2][scale_row]

            return lax.map(outgoing_single, (arrivals, geno_rows, sigmas))

        def outgoing_skipped():
            return jnp.zeros((targets, width), jnp.float32)

        return lax.cond(active, outgoing_compute, outgoing_skipped)

    def moment_step(moment, carried_state):
        (
            sent_forward,
            sent_backward,
            sent_running,
            store_forward,
            store_backward,
            sigma_forward,
            sigma_backward,
            log_terms,
        ) = carried_state
        got_forward = from_behind(sent_forward, "group", 1)
        got_backward = from_behind(sent_backward, "group", -1)
        entering_forward = jnp.where(first_row, uniform, got_forward)
        entering_backward = jnp.where(last_row, uniform, got_backward)
        index_forward = moment - position
        index_backward = moment - (chain_size - 1 - position)
        active_forward = (index_forward >= 0) & (index_forward < bundles)
        active_backward = (index_backward >= 0) & (index_backward < bundles)
        lead_forward, couple_forward = local_sums(
            active_forward, entering_forward, genotypes, forward_terms, markers + 1
        )
        lead_backward, couple_backward = local_sums(
            active_backward, entering_backward, genotypes, backward_terms, markers
        )
        lead_forward, couple_forward, lead_backward, couple_backward = lax.psum(
            (lead_forward, couple_forward, lead_backward, couple_backward), "batch"
        )
        sigmas_forward = jax.vmap(solve_sums)(lead_forward, couple_forward)
        sigmas_backward = jax.vmap(solve_sums)(lead_backward, couple_backward)
        next_forward = outgoing(
            active_forward, entering_forward, genotypes, sigmas_forward, forward_terms, markers
        )
        next_backward = outgoing(
            active_backward,
            entering_backward,
            genotypes,
            sigmas_backward,
            backward_terms,
            markers - 1,
        )
        guarded = jnp.where(active_forward, sigmas_forward[:, markers], 1.0)
        running = jnp.log(guarded)
        store_forward = place_rows(store_forward, entering_forward, active_forward)
        store_backward = place_rows(store_backward, entering_backward, active_backward)
        sigma_forward = place_rows(sigma_forward, sigmas_forward, active_forward)
        sigma_backward = place_rows(sigma_backward, sigmas_backward, active_backward)
        log_terms = place_rows(log_terms, running, active_forward)
        return (
            next_forward,
            next_backward,
            running,
            store_forward,
            store_backward,
            sigma_forward,
            sigma_backward,
            log_terms,
        )

    initial = (
        jnp.zeros((targets, width), jnp.float32),
        jnp.zeros((targets, width), jnp.float32),
        jnp.zeros((targets,), jnp.float32),
        jnp.zeros((targets, width), jnp.float32),
        jnp.zeros((targets, width), jnp.float32),
        jnp.zeros((targets, markers + 1), jnp.float32),
        jnp.zeros((targets, markers), jnp.float32),
        jnp.zeros((targets,), jnp.float32),
    )
    final_state = lax.fori_loop(0, chain_size + bundles - 1, moment_step, initial)
    store_forward, store_backward, sigma_forward, sigma_backward, log_terms = final_state[3:]
    whole_log = lax.psum(log_terms, "group")
    log_likelihood = whole_log / (markers * chain_size)

    def posterior(pieces):
        entering_ahead, entering_behind, geno_col, sigmas_ahead, sigmas_behind = pieces
        retain, inject, weight = forward_terms(panel_alleles, geno_col, recomb_rates)
        unused_f, forward_states = advance(entering_ahead, retain, inject, sigmas_ahead, True)
        forward_rows = forward_states / sigmas_ahead[1:, None]
        retain, inject, weight = backward_terms(panel_alleles, geno_col, recomb_rates)
        unused_b, backward_states = advance(entering_behind, retain, inject, sigmas_behind, True)
        scaled_back = backward_states[:-1] / sigmas_behind[:-1, None]
        backward_rows = jnp.concatenate([entering_behind[None], scaled_back], axis=0)[::-1]
        product = forward_rows * backward_rows
        numerator = jnp.sum(jnp.where(panel_alleles == 1, product, 0.0), axis=1)
        return (numerator, jnp.sum(product, axis=1))

    numerator, denominator = lax.map(
        posterior, (store_forward, store_backward, genotypes, sigma_forward, sigma_backward)
    )
    numerator, denominator = lax.psum((numerator, denominator), "batch")
    return (numerator / denominator, log_likelihood)


ROWS, LANES = 8, 128
HALF = LANES // 2
GROUPS = 4
SHARES = (9, 7)
STEP = 2 * LANES
MISSING = 2
SCALE = math.sqrt(MISMATCH * (1.0 - MISMATCH))
HALF_STEP = 0.5 * math.log((1.0 - MISMATCH) / MISMATCH)
VMEM = pl.BlockSpec(memory_space=pltpu.VMEM)
F32, BF16 = jnp.float32, jnp.bfloat16


def iota(shape, axis):
    return lax.broadcasted_iota(jnp.int32, shape, axis)


MARKERS = ROWS * GROUPS
SUBSET = 5 * ROWS
TALL = 2 * SUBSET
TRIANGLE, SQUARE = 0, 1
SETS = [
    [(TRIANGLE, 0, 0), (TRIANGLE, 0, 1), (TRIANGLE, 0, 3)]
    + [(TRIANGLE, 1, a) for a in (0, 1, 2, 7)]
    + [(SQUARE, 1, j) for j in (0, 1)],
    [(TRIANGLE, 0, 2), (TRIANGLE, 0, 7), (TRIANGLE, 1, 3)] + [(SQUARE, 1, j) for j in range(2, ROWS)],
]
TILES = SETS[0] + SETS[1]
TUCKED = [(1, 1), (1, 2), (1, 3), (2, 2), (2, 3), (3, 3)]
FIRST_TUCKED = 3
SPARE = 2


def paired_with(shape, a):
    return ROWS - 2 - a if shape == TRIANGLE and a < 3 else -1


def pack_kernel(widths, geno_ref, rate_ref, panel_ref, *refs):
    outs, (misc_ref, genos, rates_in, sems) = refs[:-4], refs[-4:]
    place = lax.axis_index("group")
    chunk = panel_ref.shape[1] // GROUPS
    copies = []
    for n, ref in enumerate(outs):
        d, p = n % GROUPS, n // GROUPS
        part = widths[p]
        start = pl.multiple_of((place ^ d) * chunk + sum(widths[:p]), LANES)
        copies.append(
            pltpu.make_async_copy(panel_ref.at[:, pl.ds(start, part)], ref.at[:, pl.ds(0, part)], sems.at[n])
        )
    small = [
        pltpu.make_async_copy(geno_ref, genos, sems.at[len(outs)]),
        pltpu.make_async_copy(rate_ref, rates_in, sems.at[len(outs) + 1]),
    ]
    for copy in small + copies:
        copy.start()
    for copy in small:
        copy.wait()
    row, lane = iota((ROWS, LANES), 0), iota((ROWS, LANES), 1)
    tile = jnp.zeros((ROWS, LANES), jnp.int32)
    misc = jnp.zeros((ROWS, LANES), F32)
    for i in range(ROWS):
        tile = jnp.where(row == i, jnp.where(lane < HALF, genos[0, i], genos[1, i]), tile)
        misc = jnp.where(lane == i, rates_in[i], misc)
        for h in range(2):
            known = jnp.where(genos[h, i] == MISSING, 0.0, 1.0)
            misc = jnp.where(lane == 2 * ROWS * (h + 1) + i, known, misc)
    for ref in outs[:GROUPS]:
        ref[:, widths[0] :] = tile
    misc_ref[...] = jnp.where((row == GROUPS + place) | (row == GROUPS - 1 - place), misc, 0.0)
    for copy in copies:
        copy.wait()


def window_kernel(step, has_misc, *refs):
    pieces, geno_refs = refs[:GROUPS], refs[GROUPS : 2 * GROUPS]
    misc_ref, t_ref, panel, genos, wide, left = refs[2 * GROUPS :]
    place = lax.axis_index("group")
    columns = panel.shape[1]
    for d in range(GROUPS):
        rows = pl.ds(pl.multiple_of((place ^ d) * ROWS, ROWS), ROWS)
        panel[rows, :] = pieces[d][...]
        genos[rows, :] = geno_refs[d][...]

    r, j = iota((4 * MARKERS, 2 * MARKERS), 0), iota((4 * MARKERS, 2 * MARKERS), 1)
    same = r // (2 * MARKERS) == j // MARKERS
    prefix, marker = (r // MARKERS) % 2 == 0, r % MARKERS
    at = j % MARKERS
    sums = jnp.where(prefix, jnp.where(at <= marker, 1.0, 0.0), jnp.where(at < marker, -1.0, 0.0))
    sums = jnp.where(same, sums, 0.0).astype(BF16)

    for start in range(0, columns, step):
        here = slice(start, start + step)
        signs = []
        for h in range(2):
            for b in range(GROUPS):
                rows = slice(b * ROWS, (b + 1) * ROWS)
                seen = genos[rows, h * HALF : h * HALF + 1]
                agrees = jnp.where(panel[rows, here] == seen, 1.0, -1.0)
                signs.append(jnp.where(seen == MISSING, 0.0, agrees))
        signs = jnp.concatenate(signs, axis=0).astype(BF16)
        power = jnp.dot(sums, signs, preferred_element_type=F32)
        value = jnp.exp(power * HALF_STEP)
        upper = value.astype(BF16).astype(F32)
        lower = value - upper
        blocks = {}
        for h in range(2):
            for kind in range(2):
                for b in range(GROUPS):
                    at = h * 2 * MARKERS + kind * MARKERS + b * ROWS
                    both = jnp.concatenate([upper[at : at + ROWS], lower[at : at + ROWS]], axis=0).astype(BF16)
                    blocks[kind, h, b] = both
                    wide[kind, (h * GROUPS + b) * 2 * ROWS : (h * GROUPS + b + 1) * 2 * ROWS, here] = both
        row = iota((ROWS, step), 0)
        for half in range(2):
            for slot, (shape, block, j) in enumerate(TILES):
                paired = paired_with(shape, j)
                outer = 0 if half == 0 else GROUPS - 1
                own = abs(outer - block)
                near = own if shape == TRIANGLE else outer
                first = row <= j if half == 0 else row >= ROWS - 1 - j

                def carries(j):
                    t = own * ROWS + (j if half == 0 else ROWS - 1 - j)
                    return jnp.broadcast_to(panel[t : t + 1, here], (ROWS, step)).astype(F32)

                mask = carries(j) if paired < 0 else jnp.where(first, carries(j), carries(paired))
                mask = jnp.concatenate([mask, mask], axis=0).astype(BF16)
                for h in range(2):
                    base = blocks[1 - half, h, near]
                    if paired >= 0:
                        at = h * 2 * MARKERS + (1 - half) * MARKERS + near * ROWS
                        shift = j + 1 if half == 0 else ROWS - 1 - j
                        both = [x[at : at + ROWS] for x in (upper, lower)]
                        both = [jnp.where(first, x, pltpu.roll(x, shift, 0)) for x in both]
                        base = jnp.concatenate(both, axis=0).astype(BF16)
                    at = (slot * 2 + h) * 2 * ROWS
                    left[half, at : at + 2 * ROWS, here] = base * mask

    def product(a, b):
        return lax.dot_general(a, b, (((1,), (1,)), ((), ())), preferred_element_type=F32)

    lane = iota((ROWS, LANES), 1)
    first = lane % (2 * ROWS) < ROWS

    def rows_of(acc, slot):
        return acc[slot * 2 * ROWS : slot * 2 * ROWS + ROWS] + acc[slot * 2 * ROWS + ROWS : (slot + 1) * 2 * ROWS]

    def fold(a, b):
        return jnp.where(first, a + pltpu.roll(a, LANES - ROWS, 1), b + pltpu.roll(b, ROWS, 1))

    def both_targets(acc, slots):
        return jnp.where(lane < HALF, rows_of(acc, slots[0]), rows_of(acc, slots[1]))

    def unfold(tile, column, to_column, odd):
        shift = 2 * ROWS * (to_column - column) + ROWS * odd
        tile = tile + pltpu.roll(tile, LANES - ROWS, 1)
        return tile if shift == 0 else pltpu.roll(tile, shift % LANES, 1)

    row = iota((ROWS, LANES), 0)
    misc = misc_ref[...] if has_misc else jnp.zeros((ROWS, LANES), F32)
    sums_e = product(wide[1], wide[0])
    plain = [both_targets(sums_e, [b, GROUPS + b]) for b in range(GROUPS)]
    column = (lane % HALF) // (2 * ROWS)
    for half in range(2):
        outer = 0 if half == 0 else GROUPS - 1
        sums_t = product(left[half], wide[half])
        tucked = {}
        for n, (b, to) in enumerate(TUCKED):
            slot = FIRST_TUCKED + n
            moved = unfold(plain[b], to, outer, slot % 2)
            here = (column == outer) & (first if slot % 2 == 0 else jnp.logical_not(first))
            tucked.setdefault(slot // 2, []).append((here, moved))
        for subset in range(2):
            base = subset * len(SETS[0])
            tiles = [both_targets(sums_t, [2 * n, 2 * n + 1]) for n in range(base, base + len(SETS[subset]))] + [plain[0]]
            for q in range(SUBSET // ROWS):
                value = fold(tiles[2 * q], tiles[2 * q + 1])
                for here, moved in tucked.get(q, []):
                    value = jnp.where(here, moved, value)
                if q == SPARE // 2:
                    spare = row >= GROUPS if half == 0 else row < GROUPS
                    value = jnp.where(spare & first, misc, value)
                at = subset * SUBSET + q * ROWS
                t_ref[half, at : at + ROWS, :] = value


def solve_kernel(panel_size, copies, sum_ref, ends_ref):
    low = lax.axis_index("group") < GROUPS // 2
    row, lane = iota((ROWS, LANES), 0), iota((ROWS, LANES), 1)
    target = lane // HALF
    folded = (lane % (2 * ROWS)) // ROWS
    column_of = (lane % HALF) // (2 * ROWS)
    misc = sum_ref[SPARE // 2 * ROWS : (SPARE // 2 + 1) * ROWS, :]

    def spread(tile, at):
        return jnp.broadcast_to(tile[:, at : at + 1], (ROWS, LANES))

    def drawn(slot, to, odd):
        tile = sum_ref[slot // 2 * ROWS : (slot // 2 + 1) * ROWS, :]
        shifts = [2 * ROWS * (to - outer) + ROWS * (odd - slot % 2) for outer in (0, GROUPS - 1)]
        return jnp.where(low, *(pltpu.roll(tile, shift % LANES, 1) if shift else tile for shift in shifts))

    last = sum_ref[SUBSET - ROWS :, :]
    pair = [jnp.where(folded == 0, pltpu.roll(last, LANES - ROWS, 1), 0.0), jnp.zeros((ROWS, LANES), F32)]
    for n, (b, to) in enumerate(TUCKED):
        here = (column_of == to) & (folded == b % 2)
        pair[b // 2] = jnp.where(here, drawn(FIRST_TUCKED + n, to, b % 2), pair[b // 2])
    square = jnp.concatenate(pair + [misc, jnp.zeros((LANES - 3 * ROWS, LANES), F32)], axis=0)
    turned = jnp.transpose(square)

    listed = turned[:ROWS] * (1.0 / copies)
    spare = GROUPS * ROWS // 2
    rates = [jnp.where(low, spread(listed, spare + GROUPS + b), spread(listed, spare + GROUPS - 1 - b)) for b in range(GROUPS)]
    odds = [rate / (1.0 - rate) for rate in rates]
    inverse = 1.0 / panel_size
    ahead = []
    for b in range(GROUPS):
        following = odds[b + 1][0:1, :] if b + 1 < GROUPS else jnp.ones((1, LANES), F32)
        ahead.append(jnp.concatenate([odds[b][1:, :], following], axis=0) * inverse)
    behind = [odd * inverse for odd in odds]

    trail_tiles = []
    for q in range(GROUPS // 2):
        factor = jnp.where(folded == 0, behind[2 * q], behind[2 * q + 1])
        trail_tiles.append(pair[q] * factor)

    def turned_tile(h, b, f):
        at = h * HALF + b * 2 * ROWS + f * ROWS
        return turned[at : at + ROWS] * ahead[b]

    lead_tiles = {(h, b, f): turned_tile(h, b, f) for h in range(2) for b in range(GROUPS) for f in range(2)}

    def lead_column(t, b):
        s, at = t // ROWS, (t // ROWS // 2) * ROWS + t % ROWS
        return jnp.where(target == 0, spread(lead_tiles[0, b, s % 2], at), spread(lead_tiles[1, b, s % 2], at))

    def trail_column(t, b):
        at = 2 * ROWS * (t // ROWS) + t % ROWS + ROWS * (b % 2)
        tile = trail_tiles[b // 2]
        return jnp.where(target == 0, spread(tile, at), spread(tile, HALF + at))

    zero = jnp.zeros((ROWS, LANES), F32)
    lead, trail, starts, ends = [zero] * GROUPS, [zero] * GROUPS, [zero] * GROUPS, [zero] * GROUPS
    v = jnp.ones((ROWS, LANES), F32)
    z = jnp.ones((ROWS, LANES), F32)
    for t in range(MARKERS):
        u = MARKERS - 1 - t
        bt, bu = t // ROWS, u // ROWS
        starts[bt] = jnp.where(row == t % ROWS, v, starts[bt])
        ends[bu] = jnp.where(row == u % ROWS, z, ends[bu])
        for b in range(bt, GROUPS):
            lead[b] = lead[b] + v * lead_column(t, b)
        for b in range(bu + 1):
            trail[b] = trail[b] + z * trail_column(u, b)
        v = jnp.broadcast_to(lead[bt][t % ROWS : t % ROWS + 1, :], (ROWS, LANES))
        z = jnp.broadcast_to(trail[bu][u % ROWS : u % ROWS + 1, :], (ROWS, LANES))
    for b in range(GROUPS):
        ends_ref[b * ROWS : (b + 1) * ROWS, :] = starts[b]
        ends_ref[MARKERS + b * ROWS : MARKERS + (b + 1) * ROWS, :] = ends[b]

    stay = [jnp.log(1.0 - rate) for rate in rates]
    stay[0] = jnp.where(row == 0, 0.0, stay[0])
    stay = jnp.sum(sum(stay), axis=0, keepdims=True)
    marked = jnp.where(low, row, ROWS - 1 - row) >= GROUPS
    logs = []
    for h in range(2):
        cell = marked & (lane >= 2 * ROWS * (h + 1)) & (lane < 2 * ROWS * (h + 1) + ROWS)
        seen = jnp.sum(jnp.where(cell, misc, 0.0), axis=0, keepdims=True)
        seen = jnp.sum(seen, axis=1, keepdims=True) * (1.0 / copies)
        whole = jnp.log(v[0:1, h * HALF : h * HALF + 1]) + stay[:, 0:1] + seen * math.log(SCALE)
        logs.append(whole * (1.0 / MARKERS))
    ends_ref[2 * MARKERS :, :] = jnp.where(row == 0, inverse / v, jnp.where(target == 0, *logs))


def contract_kernel(weight_ref, t_ref, dose_ref, log_ref):
    place = lax.axis_index("group")
    low = place < GROUPS // 2
    inward = (place == 1) | (place == GROUPS - 2)
    row, lane = iota((ROWS, LANES), 0), iota((ROWS, LANES), 1)
    folded = (lane % (2 * ROWS)) // ROWS
    side = jnp.where(low, 1, -1)
    turn = jnp.where(low, 0, ROWS - 1)
    order = turn + side * row

    def weights(is_start, block):
        at = jnp.where(is_start, 0, MARKERS) + block * ROWS
        return weight_ref[pl.ds(pl.multiple_of(at, ROWS), ROWS), :]

    picked = weights(jnp.logical_not(low), GROUPS - 1)
    column = (lane % HALF) // (2 * ROWS)
    for b in range(GROUPS - 1):
        picked = jnp.where(column == b, weights(jnp.logical_not(low), b), picked)
    picked = jnp.where(row == lane % ROWS, picked, 0.0)
    across = jnp.sum(picked, axis=0, keepdims=True) * weight_ref[2 * MARKERS : 2 * MARKERS + 1, :]
    far_end = ROWS * column + lane % ROWS

    def reaches(j):
        t = place * ROWS + turn + side * j
        return (far_end - t) * side >= 0

    near = weights(low, place)
    outermost = weights(low, jnp.where(low, 0, GROUPS - 1))
    inner = jnp.where(inward, 1.0, 0.0)
    total = jnp.zeros((ROWS, LANES), F32)

    def select(pair):
        return pair[0] if pair[0] is pair[1] else jnp.where(folded == 0, *pair)

    for subset in range(2):
        slots = SETS[subset] + [None]
        for q in range(SUBSET // ROWS):
            firsts, seconds, shared, moved = [], [], [], []
            for entry in slots[2 * q : 2 * q + 2]:
                if entry is None:
                    firsts.append(-1)
                    seconds.append(-1)
                    shared.append(near)
                    moved.append(near)
                    continue
                shape, block, j = entry
                paired = paired_with(shape, j)
                used = inner if block else 1.0 - inner
                weight = (near if shape == TRIANGLE else outermost) * used
                firsts.append(j)
                seconds.append(paired)
                shared.append(weight)
                if paired < 0:
                    moved.append(weight)
                else:
                    moved.append(jnp.where(low, pltpu.roll(weight, j + 1, 0), pltpu.roll(weight, ROWS - 1 - j, 0)))
            is_square = [entry is not None and entry[0] == SQUARE for entry in slots[2 * q : 2 * q + 2]]
            ends = [ROWS - 1 if square else j for square, j in zip(is_square, firsts)]
            a, second, end = (jnp.where(folded == 0, *pair) for pair in (firsts, seconds, ends))
            own = order <= end
            marker = jnp.where(own, a, second)
            weight = jnp.where(own, select(shared), select(moved)) * across
            at = subset * SUBSET + q * ROWS
            terms = jnp.where((marker >= 0) & reaches(marker), t_ref[at : at + ROWS, :] * weight, 0.0)
            one = jnp.sum(jnp.where(own, terms, 0.0), axis=0, keepdims=True)
            total = total + jnp.where(row == a, one, 0.0)
            if max(seconds) >= 0:
                other = jnp.sum(jnp.where(own, 0.0, terms), axis=0, keepdims=True)
                total = total + jnp.where(row == second, other, 0.0)
    doses = []
    for h in range(2):
        dose = jnp.sum(jnp.where(lane // HALF == h, total, 0.0), axis=1, keepdims=True)
        doses.append(jnp.sum(jnp.where(order == lane, dose, 0.0), axis=0, keepdims=True))
    dose_ref[...] = jnp.concatenate(doses, axis=0)[:, :ROWS]
    logs = weight_ref[2 * MARKERS + 1 : 2 * MARKERS + 2, :]
    log_ref[...] = jnp.concatenate([logs[:, :1], logs[:, HALF : HALF + 1]], axis=1)


def exchange(x, axis, by):
    peers = lax.axis_size(axis)
    return lax.ppermute(x, axis, [(i, i ^ by) for i in range(peers)])


def exchange_flat(x, by):
    peers = lax.axis_size("group") * lax.axis_size("batch")
    return lax.ppermute(x, ("group", "batch"), [(i, i ^ by) for i in range(peers)])


def is_odd(bits):
    odd = bits
    for shift in (16, 8, 4, 2, 1):
        odd = odd ^ (odd >> shift)
    return odd & 1


def on_device_windows(panel_alleles, recomb_rates, genotypes):
    width = panel_alleles.shape[1]
    copies = lax.axis_size("batch")
    chunk = width // GROUPS
    place = lax.axis_index("group")
    widths = [chunk * share // sum(SHARES) for share in SHARES]
    shapes = [
        jax.ShapeDtypeStruct((ROWS, part + (LANES if p == 0 else 0)), jnp.int32)
        for p, part in enumerate(widths)
        for d in range(GROUPS)
    ]
    *cuts, misc = pl.pallas_call(
        functools.partial(pack_kernel, widths),
        out_shape=shapes + [jax.ShapeDtypeStruct((ROWS, LANES), F32)],
        in_specs=[pl.BlockSpec(memory_space=pltpu.HBM)] * 3,
        out_specs=[VMEM] * (len(shapes) + 1),
        scratch_shapes=[
            pltpu.SMEM(genotypes.shape, jnp.int32),
            pltpu.SMEM(recomb_rates.shape, F32),
            pltpu.SemaphoreType.DMA((len(shapes) + 2,)),
        ],
        compiler_params=pltpu.CompilerParams(vmem_limit_bytes=4 * 1024 * 1024),
        name="pack",
    )(*(pltpu.with_memory_space_constraint(x, pltpu.HBM) for x in (genotypes, recomb_rates, panel_alleles)))
    arrived = None
    for p in range(len(widths)):
        part = cuts[p * GROUPS : (p + 1) * GROUPS]
        if arrived is not None:
            part[1:], arrived = lax.optimization_barrier((part[1:], arrived))
            cuts[(p - 1) * GROUPS + 1] = arrived
        part = [cut if d == 0 else exchange(cut, "group", d) for d, cut in enumerate(part)]
        cuts[p * GROUPS : (p + 1) * GROUPS] = part
        arrived = part[1]
    tags = [cut[:, widths[0] :] for cut in cuts[:GROUPS]]
    sums = []
    for p, part in enumerate(widths):
        pieces = [cut[:, :part] for cut in cuts[p * GROUPS : (p + 1) * GROUPS]]
        sums.append(
            pl.pallas_call(
                functools.partial(window_kernel, STEP, p == 0),
                out_shape=jax.ShapeDtypeStruct((2, TALL, LANES), F32),
                in_specs=[VMEM] * (2 * GROUPS + 1),
                out_specs=VMEM,
                scratch_shapes=[
                    pltpu.VMEM((MARKERS, part), jnp.int32),
                    pltpu.VMEM((MARKERS, LANES), jnp.int32),
                    pltpu.VMEM((2, 4 * MARKERS, part), BF16),
                    pltpu.VMEM((2, len(TILES) * 4 * ROWS, part), BF16),
                ],
                compiler_params=pltpu.CompilerParams(vmem_limit_bytes=40 * 1024 * 1024),
                cost_estimate=pl.CostEstimate(flops=part * 900000, bytes_accessed=0, transcendentals=0),
                name="windows",
            )(*pieces, *tags, misc)
        )
    sums = sum(sums)
    sums = sums.reshape(2, 2, SUBSET, LANES)
    half = place // (GROUPS // 2)
    carried = is_odd(place ^ lax.axis_index("batch"))

    def pick(array, index, axis):
        return lax.dynamic_index_in_dim(array, index, axis, False)

    both = pick(sums, carried, 1) + exchange(pick(sums, 1 - carried, 1), "group", 1)
    core = copies
    kept = pick(both, half, 0) + exchange_flat(pick(both, 1 - half, 0), 2 * core + core)
    by = 1
    while by < copies:
        kept = kept + exchange_flat(kept, by + core)
        by *= 2
    theirs = exchange(kept, "group", 1)
    weights = pl.pallas_call(
        functools.partial(solve_kernel, float(width * copies), float(copies)),
        out_shape=jax.ShapeDtypeStruct((2 * MARKERS + ROWS, LANES), F32),
        in_specs=[VMEM],
        out_specs=VMEM,
        compiler_params=pltpu.CompilerParams(vmem_limit_bytes=4 * 1024 * 1024),
        cost_estimate=pl.CostEstimate(flops=1000000, bytes_accessed=0, transcendentals=0),
        name="solve",
    )(kept)
    whole = jnp.where(carried == 0, jnp.concatenate([kept, theirs], axis=0), jnp.concatenate([theirs, kept], axis=0))
    dosage, logs = pl.pallas_call(
        contract_kernel,
        out_shape=[jax.ShapeDtypeStruct((2, ROWS), F32), jax.ShapeDtypeStruct((1, 2), F32)],
        in_specs=[VMEM] * 2,
        out_specs=[VMEM] * 2,
        compiler_params=pltpu.CompilerParams(vmem_limit_bytes=4 * 1024 * 1024),
        name="contract",
    )(weights, whole)
    return dosage, logs.reshape(2)


def fits_windows(panel_alleles, genotypes, groups, copies):
    markers, width = panel_alleles.shape
    return (
        groups == GROUPS
        and copies & (copies - 1) == 0
        and markers == ROWS
        and genotypes.shape[0] == 2
        and width % (GROUPS * sum(SHARES) * STEP) == 0
    )


def on_device(panel_alleles, recomb_rates, genotypes):
    groups, copies = lax.axis_size("group"), lax.axis_size("batch")
    if fits_windows(panel_alleles, genotypes, groups, copies):
        return on_device_windows(panel_alleles, recomb_rates, genotypes)
    return on_device_chain(panel_alleles, recomb_rates, genotypes)


def solution(mesh):
    placed = (P("group", "batch"), P("group"), P(None, "group"))
    return jax.shard_map(
        on_device, mesh=mesh, in_specs=placed, out_specs=(P(None, "group"), P()), check_vma=False
    )
```

```python
import functools
import math

import jax
import jax.numpy as jnp
from jax import lax
from jax.experimental import pallas as pl
from jax.experimental.pallas import tpu as pltpu
from jax.sharding import PartitionSpec as P

MISMATCH = 0.05
HIGHEST = lax.Precision.HIGHEST


def haplotypes(panel_rows):
    return panel_rows.shape[1] * lax.axis_size("batch")


def from_behind(x, axis, by):
    peers = lax.axis_size(axis)
    pairs = [(i, i + by) for i in range(peers) if 0 <= i + by < peers]
    return lax.ppermute(x, axis, pairs)


def emission(panel_rows, geno_col):
    observed = geno_col[:, None]
    agrees = jnp.where(panel_rows == observed, 1.0 - MISMATCH, MISMATCH)
    return jnp.where(observed == 2, 1.0, agrees).astype(jnp.float32)


def forward_terms(panel_rows, geno_col, switches):
    emitted = emission(panel_rows, geno_col)
    retain = emitted * (1.0 - switches)[:, None]
    inject = emitted * (switches / haplotypes(panel_rows))[:, None]
    return (retain, inject, None)


def backward_terms(panel_rows, geno_col, switches):
    emitted = emission(panel_rows, geno_col)[::-1]
    flipped = switches[::-1]
    retain = emitted * (1.0 - flipped)[:, None]
    inject = jnp.broadcast_to((flipped / haplotypes(panel_rows))[:, None], emitted.shape)
    return (retain, inject, emitted)


def partial_sums(entering, retain, inject, weight, extent):
    logs = jnp.cumsum(jnp.log(retain), axis=0)
    shifted = jnp.concatenate([jnp.zeros_like(entering)[None], logs[: extent - 1]], axis=0)
    before = jnp.exp(shifted)
    left_side = before if weight is None else weight * before
    leading = jnp.einsum("jk,k->j", left_side, entering, precision=HIGHEST)
    anchor = shifted[0]
    right_side = inject * jnp.exp(anchor[None] - logs)
    nearby = jnp.exp(jnp.minimum(shifted - anchor[None], 0.0))
    nearby = nearby if weight is None else weight * nearby
    columns = [jnp.einsum("jk,tk->jt", nearby, right_side, precision=HIGHEST)]
    coupling = jnp.concatenate(columns, axis=1)
    return (leading, coupling)


def solve_sums(leading, coupling):
    columns = coupling.shape[1]

    def settle(marker, sigmas):
        below = jnp.arange(columns) < marker
        update = leading[marker] + jnp.sum(
            jnp.where(below, coupling[marker] * sigmas[:columns], 0.0)
        )
        return sigmas.at[marker].set(update)

    return lax.fori_loop(0, leading.shape[0], settle, jnp.zeros_like(leading))


def advance(entering, retain, inject, sigmas, keep_states):

    def advance_single(current, pieces):
        current = pieces[0] * current + pieces[1] * pieces[2]
        return (current, current if keep_states else None)

    return lax.scan(advance_single, entering, (retain, inject, sigmas[: retain.shape[0]]))


def place_rows(store, block, active):
    return jnp.where(active, block, store)


def on_device_chain(panel_alleles, recomb_rates, genotypes):
    chain_size = lax.axis_size("group")
    position = lax.axis_index("group")
    markers, width = panel_alleles.shape
    targets = genotypes.shape[0]
    bundles = targets // targets
    uniform = jnp.full((targets, width), 1.0 / haplotypes(panel_alleles), jnp.float32)
    first_row = position == 0
    last_row = position == chain_size - 1

    def local_sums(active, arrivals, geno_rows, maker, extent):

        def local_compute():

            def local_single(pieces):
                retain, inject, weight = maker(panel_alleles, pieces[1], recomb_rates)
                return partial_sums(pieces[0], retain, inject, weight, extent)

            return lax.map(local_single, (arrivals, geno_rows))

        def local_skipped():
            return (
                jnp.zeros((targets, extent), jnp.float32),
                jnp.zeros((targets, extent, markers), jnp.float32),
            )

        return lax.cond(active, local_compute, local_skipped)

    def outgoing(active, arrivals, geno_rows, sigmas, maker, scale_row):

        def outgoing_compute():

            def outgoing_single(pieces):
                retain, inject, weight = maker(panel_alleles, pieces[1], recomb_rates)
                ending, unused = advance(pieces[0], retain, inject, pieces[2], False)
                return ending / pieces[2][scale_row]

            return lax.map(outgoing_single, (arrivals, geno_rows, sigmas))

        def outgoing_skipped():
            return jnp.zeros((targets, width), jnp.float32)

        return lax.cond(active, outgoing_compute, outgoing_skipped)

    def moment_step(moment, carried_state):
        (
            sent_forward,
            sent_backward,
            sent_running,
            store_forward,
            store_backward,
            sigma_forward,
            sigma_backward,
            log_terms,
        ) = carried_state
        got_forward = from_behind(sent_forward, "group", 1)
        got_backward = from_behind(sent_backward, "group", -1)
        entering_forward = jnp.where(first_row, uniform, got_forward)
        entering_backward = jnp.where(last_row, uniform, got_backward)
        index_forward = moment - position
        index_backward = moment - (chain_size - 1 - position)
        active_forward = (index_forward >= 0) & (index_forward < bundles)
        active_backward = (index_backward >= 0) & (index_backward < bundles)
        lead_forward, couple_forward = local_sums(
            active_forward, entering_forward, genotypes, forward_terms, markers + 1
        )
        lead_backward, couple_backward = local_sums(
            active_backward, entering_backward, genotypes, backward_terms, markers
        )
        lead_forward, couple_forward, lead_backward, couple_backward = lax.psum(
            (lead_forward, couple_forward, lead_backward, couple_backward), "batch"
        )
        sigmas_forward = jax.vmap(solve_sums)(lead_forward, couple_forward)
        sigmas_backward = jax.vmap(solve_sums)(lead_backward, couple_backward)
        next_forward = outgoing(
            active_forward, entering_forward, genotypes, sigmas_forward, forward_terms, markers
        )
        next_backward = outgoing(
            active_backward,
            entering_backward,
            genotypes,
            sigmas_backward,
            backward_terms,
            markers - 1,
        )
        guarded = jnp.where(active_forward, sigmas_forward[:, markers], 1.0)
        running = jnp.log(guarded)
        store_forward = place_rows(store_forward, entering_forward, active_forward)
        store_backward = place_rows(store_backward, entering_backward, active_backward)
        sigma_forward = place_rows(sigma_forward, sigmas_forward, active_forward)
        sigma_backward = place_rows(sigma_backward, sigmas_backward, active_backward)
        log_terms = place_rows(log_terms, running, active_forward)
        return (
            next_forward,
            next_backward,
            running,
            store_forward,
            store_backward,
            sigma_forward,
            sigma_backward,
            log_terms,
        )

    initial = (
        jnp.zeros((targets, width), jnp.float32),
        jnp.zeros((targets, width), jnp.float32),
        jnp.zeros((targets,), jnp.float32),
        jnp.zeros((targets, width), jnp.float32),
        jnp.zeros((targets, width), jnp.float32),
        jnp.zeros((targets, markers + 1), jnp.float32),
        jnp.zeros((targets, markers), jnp.float32),
        jnp.zeros((targets,), jnp.float32),
    )
    final_state = lax.fori_loop(0, chain_size + bundles - 1, moment_step, initial)
    store_forward, store_backward, sigma_forward, sigma_backward, log_terms = final_state[3:]
    whole_log = lax.psum(log_terms, "group")
    log_likelihood = whole_log / (markers * chain_size)

    def posterior(pieces):
        entering_ahead, entering_behind, geno_col, sigmas_ahead, sigmas_behind = pieces
        retain, inject, weight = forward_terms(panel_alleles, geno_col, recomb_rates)
        unused_f, forward_states = advance(entering_ahead, retain, inject, sigmas_ahead, True)
        forward_rows = forward_states / sigmas_ahead[1:, None]
        retain, inject, weight = backward_terms(panel_alleles, geno_col, recomb_rates)
        unused_b, backward_states = advance(entering_behind, retain, inject, sigmas_behind, True)
        scaled_back = backward_states[:-1] / sigmas_behind[:-1, None]
        backward_rows = jnp.concatenate([entering_behind[None], scaled_back], axis=0)[::-1]
        product = forward_rows * backward_rows
        numerator = jnp.sum(jnp.where(panel_alleles == 1, product, 0.0), axis=1)
        return (numerator, jnp.sum(product, axis=1))

    numerator, denominator = lax.map(
        posterior, (store_forward, store_backward, genotypes, sigma_forward, sigma_backward)
    )
    numerator, denominator = lax.psum((numerator, denominator), "batch")
    return (numerator / denominator, log_likelihood)


ROWS, LANES = 8, 128
HALF = LANES // 2
GROUPS = 4
SHARES = (9, 7)
STEP = 2 * LANES
MISSING = 2
SCALE = math.sqrt(MISMATCH * (1.0 - MISMATCH))
HALF_STEP = 0.5 * math.log((1.0 - MISMATCH) / MISMATCH)
VMEM = pl.BlockSpec(memory_space=pltpu.VMEM)
F32, BF16 = jnp.float32, jnp.bfloat16


def iota(shape, axis):
    return lax.broadcasted_iota(jnp.int32, shape, axis)


MARKERS = ROWS * GROUPS
SUBSET = 5 * ROWS
TALL = 2 * SUBSET
TRIANGLE, SQUARE = 0, 1
SETS = [
    [(TRIANGLE, 0, 0), (TRIANGLE, 0, 1), (TRIANGLE, 0, 3)]
    + [(TRIANGLE, 1, a) for a in (0, 1, 2, 7)]
    + [(SQUARE, 1, j) for j in (0, 1)],
    [(TRIANGLE, 0, 2), (TRIANGLE, 0, 7), (TRIANGLE, 1, 3)] + [(SQUARE, 1, j) for j in range(2, ROWS)],
]
TILES = SETS[0] + SETS[1]
TUCKED = [(1, 1), (1, 2), (1, 3), (2, 2), (2, 3), (3, 3)]
FIRST_TUCKED = 3
SPARE = 2


def paired_with(shape, a):
    return ROWS - 2 - a if shape == TRIANGLE and a < 3 else -1


def pack_kernel(widths, geno_ref, rate_ref, panel_ref, *refs):
    outs, (misc_ref, genos, rates_in, sems) = refs[:-4], refs[-4:]
    place = lax.axis_index("group")
    chunk = panel_ref.shape[1] // GROUPS
    copies = []
    for n, ref in enumerate(outs):
        d, p = n % GROUPS, n // GROUPS
        part = widths[p]
        start = pl.multiple_of((place ^ d) * chunk + sum(widths[:p]), LANES)
        copies.append(
            pltpu.make_async_copy(panel_ref.at[:, pl.ds(start, part)], ref.at[:, pl.ds(0, part)], sems.at[n])
        )
    small = [
        pltpu.make_async_copy(geno_ref, genos, sems.at[len(outs)]),
        pltpu.make_async_copy(rate_ref, rates_in, sems.at[len(outs) + 1]),
    ]
    for copy in small + copies:
        copy.start()
    for copy in small:
        copy.wait()
    row, lane = iota((ROWS, LANES), 0), iota((ROWS, LANES), 1)
    tile = jnp.zeros((ROWS, LANES), jnp.int32)
    misc = jnp.zeros((ROWS, LANES), F32)
    for i in range(ROWS):
        tile = jnp.where(row == i, jnp.where(lane < HALF, genos[0, i], genos[1, i]), tile)
        misc = jnp.where(lane == i, rates_in[i], misc)
        for h in range(2):
            known = jnp.where(genos[h, i] == MISSING, 0.0, 1.0)
            misc = jnp.where(lane == 2 * ROWS * (h + 1) + i, known, misc)
    for ref in outs[:GROUPS]:
        ref[:, widths[0] :] = tile
    misc_ref[...] = jnp.where((row == GROUPS + place) | (row == GROUPS - 1 - place), misc, 0.0)
    for copy in copies:
        copy.wait()


def window_kernel(step, has_misc, *refs):
    pieces, geno_refs = refs[:GROUPS], refs[GROUPS : 2 * GROUPS]
    misc_ref, t_ref, panel, genos, wide, left = refs[2 * GROUPS :]
    place = lax.axis_index("group")
    columns = panel.shape[1]
    for d in range(GROUPS):
        rows = pl.ds(pl.multiple_of((place ^ d) * ROWS, ROWS), ROWS)
        panel[rows, :] = pieces[d][...]
        genos[rows, :] = geno_refs[d][...]

    r, j = iota((4 * MARKERS, 2 * MARKERS), 0), iota((4 * MARKERS, 2 * MARKERS), 1)
    same = r // (2 * MARKERS) == j // MARKERS
    prefix, marker = (r // MARKERS) % 2 == 0, r % MARKERS
    at = j % MARKERS
    sums = jnp.where(prefix, jnp.where(at <= marker, 1.0, 0.0), jnp.where(at < marker, -1.0, 0.0))
    sums = jnp.where(same, sums, 0.0).astype(BF16)

    for start in range(0, columns, step):
        here = slice(start, start + step)
        signs = []
        for h in range(2):
            for b in range(GROUPS):
                rows = slice(b * ROWS, (b + 1) * ROWS)
                seen = genos[rows, h * HALF : h * HALF + 1]
                agrees = jnp.where(panel[rows, here] == seen, 1.0, -1.0)
                signs.append(jnp.where(seen == MISSING, 0.0, agrees))
        signs = jnp.concatenate(signs, axis=0).astype(BF16)
        power = jnp.dot(sums, signs, preferred_element_type=F32)
        value = jnp.exp(power * HALF_STEP)
        upper = value.astype(BF16).astype(F32)
        lower = value - upper
        blocks = {}
        for h in range(2):
            for kind in range(2):
                for b in range(GROUPS):
                    at = h * 2 * MARKERS + kind * MARKERS + b * ROWS
                    both = jnp.concatenate([upper[at : at + ROWS], lower[at : at + ROWS]], axis=0).astype(BF16)
                    blocks[kind, h, b] = both
                    wide[kind, (h * GROUPS + b) * 2 * ROWS : (h * GROUPS + b + 1) * 2 * ROWS, here] = both
        row = iota((ROWS, step), 0)
        for half in range(2):
            for slot, (shape, block, j) in enumerate(TILES):
                paired = paired_with(shape, j)
                outer = 0 if half == 0 else GROUPS - 1
                own = abs(outer - block)
                near = own if shape == TRIANGLE else outer
                first = row <= j if half == 0 else row >= ROWS - 1 - j

                def carries(j):
                    t = own * ROWS + (j if half == 0 else ROWS - 1 - j)
                    return jnp.broadcast_to(panel[t : t + 1, here], (ROWS, step)).astype(F32)

                mask = carries(j) if paired < 0 else jnp.where(first, carries(j), carries(paired))
                mask = jnp.concatenate([mask, mask], axis=0).astype(BF16)
                for h in range(2):
                    base = blocks[1 - half, h, near]
                    if paired >= 0:
                        at = h * 2 * MARKERS + (1 - half) * MARKERS + near * ROWS
                        shift = j + 1 if half == 0 else ROWS - 1 - j
                        both = [x[at : at + ROWS] for x in (upper, lower)]
                        both = [jnp.where(first, x, pltpu.roll(x, shift, 0)) for x in both]
                        base = jnp.concatenate(both, axis=0).astype(BF16)
                    at = (slot * 2 + h) * 2 * ROWS
                    left[half, at : at + 2 * ROWS, here] = base * mask

    def product(a, b):
        return lax.dot_general(a, b, (((1,), (1,)), ((), ())), preferred_element_type=F32)

    lane = iota((ROWS, LANES), 1)
    first = lane % (2 * ROWS) < ROWS

    def rows_of(acc, slot):
        return acc[slot * 2 * ROWS : slot * 2 * ROWS + ROWS] + acc[slot * 2 * ROWS + ROWS : (slot + 1) * 2 * ROWS]

    def fold(a, b):
        return jnp.where(first, a + pltpu.roll(a, LANES - ROWS, 1), b + pltpu.roll(b, ROWS, 1))

    def both_targets(acc, slots):
        return jnp.where(lane < HALF, rows_of(acc, slots[0]), rows_of(acc, slots[1]))

    def unfold(tile, column, to_column, odd):
        shift = 2 * ROWS * (to_column - column) + ROWS * odd
        tile = tile + pltpu.roll(tile, LANES - ROWS, 1)
        return tile if shift == 0 else pltpu.roll(tile, shift % LANES, 1)

    row = iota((ROWS, LANES), 0)
    misc = misc_ref[...] if has_misc else jnp.zeros((ROWS, LANES), F32)
    sums_e = product(wide[1], wide[0])
    plain = [both_targets(sums_e, [b, GROUPS + b]) for b in range(GROUPS)]
    column = (lane % HALF) // (2 * ROWS)
    for half in range(2):
        outer = 0 if half == 0 else GROUPS - 1
        sums_t = product(left[half], wide[half])
        tucked = {}
        for n, (b, to) in enumerate(TUCKED):
            slot = FIRST_TUCKED + n
            moved = unfold(plain[b], to, outer, slot % 2)
            here = (column == outer) & (first if slot % 2 == 0 else jnp.logical_not(first))
            tucked.setdefault(slot // 2, []).append((here, moved))
        for subset in range(2):
            base = subset * len(SETS[0])
            tiles = [both_targets(sums_t, [2 * n, 2 * n + 1]) for n in range(base, base + len(SETS[subset]))] + [plain[0]]
            for q in range(SUBSET // ROWS):
                value = fold(tiles[2 * q], tiles[2 * q + 1])
                for here, moved in tucked.get(q, []):
                    value = jnp.where(here, moved, value)
                if q == SPARE // 2:
                    spare = row >= GROUPS if half == 0 else row < GROUPS
                    value = jnp.where(spare & first, misc, value)
                at = subset * SUBSET + q * ROWS
                t_ref[half, at : at + ROWS, :] = value


def solve_kernel(panel_size, copies, sum_ref, ends_ref):
    low = lax.axis_index("group") < GROUPS // 2
    row, lane = iota((ROWS, LANES), 0), iota((ROWS, LANES), 1)
    target = lane // HALF
    folded = (lane % (2 * ROWS)) // ROWS
    column_of = (lane % HALF) // (2 * ROWS)
    misc = sum_ref[SPARE // 2 * ROWS : (SPARE // 2 + 1) * ROWS, :]

    def spread(tile, at):
        return jnp.broadcast_to(tile[:, at : at + 1], (ROWS, LANES))

    def drawn(slot, to, odd):
        tile = sum_ref[slot // 2 * ROWS : (slot // 2 + 1) * ROWS, :]
        shifts = [2 * ROWS * (to - outer) + ROWS * (odd - slot % 2) for outer in (0, GROUPS - 1)]
        return jnp.where(low, *(pltpu.roll(tile, shift % LANES, 1) if shift else tile for shift in shifts))

    last = sum_ref[SUBSET - ROWS :, :]
    pair = [jnp.where(folded == 0, pltpu.roll(last, LANES - ROWS, 1), 0.0), jnp.zeros((ROWS, LANES), F32)]
    for n, (b, to) in enumerate(TUCKED):
        here = (column_of == to) & (folded == b % 2)
        pair[b // 2] = jnp.where(here, drawn(FIRST_TUCKED + n, to, b % 2), pair[b // 2])
    square = jnp.concatenate(pair + [misc, jnp.zeros((LANES - 3 * ROWS, LANES), F32)], axis=0)
    turned = jnp.transpose(square)

    listed = turned[:ROWS] * (1.0 / copies)
    spare = GROUPS * ROWS // 2
    rates = [jnp.where(low, spread(listed, spare + GROUPS + b), spread(listed, spare + GROUPS - 1 - b)) for b in range(GROUPS)]
    odds = [rate / (1.0 - rate) for rate in rates]
    inverse = 1.0 / panel_size
    ahead = []
    for b in range(GROUPS):
        following = odds[b + 1][0:1, :] if b + 1 < GROUPS else jnp.ones((1, LANES), F32)
        ahead.append(jnp.concatenate([odds[b][1:, :], following], axis=0) * inverse)
    behind = [odd * inverse for odd in odds]

    trail_tiles = []
    for q in range(GROUPS // 2):
        factor = jnp.where(folded == 0, behind[2 * q], behind[2 * q + 1])
        trail_tiles.append(pair[q] * factor)

    def turned_tile(h, b, f):
        at = h * HALF + b * 2 * ROWS + f * ROWS
        return turned[at : at + ROWS] * ahead[b]

    lead_tiles = {(h, b, f): turned_tile(h, b, f) for h in range(2) for b in range(GROUPS) for f in range(2)}

    def lead_column(t, b):
        s, at = t // ROWS, (t // ROWS // 2) * ROWS + t % ROWS
        return jnp.where(target == 0, spread(lead_tiles[0, b, s % 2], at), spread(lead_tiles[1, b, s % 2], at))

    def trail_column(t, b):
        at = 2 * ROWS * (t // ROWS) + t % ROWS + ROWS * (b % 2)
        tile = trail_tiles[b // 2]
        return jnp.where(target == 0, spread(tile, at), spread(tile, HALF + at))

    zero = jnp.zeros((ROWS, LANES), F32)
    lead, trail, starts, ends = [zero] * GROUPS, [zero] * GROUPS, [zero] * GROUPS, [zero] * GROUPS
    v = jnp.ones((ROWS, LANES), F32)
    z = jnp.ones((ROWS, LANES), F32)
    for t in range(MARKERS):
        u = MARKERS - 1 - t
        bt, bu = t // ROWS, u // ROWS
        starts[bt] = jnp.where(row == t % ROWS, v, starts[bt])
        ends[bu] = jnp.where(row == u % ROWS, z, ends[bu])
        for b in range(bt, GROUPS):
            lead[b] = lead[b] + v * lead_column(t, b)
        for b in range(bu + 1):
            trail[b] = trail[b] + z * trail_column(u, b)
        v = jnp.broadcast_to(lead[bt][t % ROWS : t % ROWS + 1, :], (ROWS, LANES))
        z = jnp.broadcast_to(trail[bu][u % ROWS : u % ROWS + 1, :], (ROWS, LANES))
    for b in range(GROUPS):
        ends_ref[b * ROWS : (b + 1) * ROWS, :] = starts[b]
        ends_ref[MARKERS + b * ROWS : MARKERS + (b + 1) * ROWS, :] = ends[b]

    stay = [jnp.log(1.0 - rate) for rate in rates]
    stay[0] = jnp.where(row == 0, 0.0, stay[0])
    stay = jnp.sum(sum(stay), axis=0, keepdims=True)
    marked = jnp.where(low, row, ROWS - 1 - row) >= GROUPS
    logs = []
    for h in range(2):
        cell = marked & (lane >= 2 * ROWS * (h + 1)) & (lane < 2 * ROWS * (h + 1) + ROWS)
        seen = jnp.sum(jnp.where(cell, misc, 0.0), axis=0, keepdims=True)
        seen = jnp.sum(seen, axis=1, keepdims=True) * (1.0 / copies)
        whole = jnp.log(v[0:1, h * HALF : h * HALF + 1]) + stay[:, 0:1] + seen * math.log(SCALE)
        logs.append(whole * (1.0 / MARKERS))
    ends_ref[2 * MARKERS :, :] = jnp.where(row == 0, inverse / v, jnp.where(target == 0, *logs))


def contract_kernel(weight_ref, t_ref, dose_ref, log_ref):
    place = lax.axis_index("group")
    low = place < GROUPS // 2
    inward = (place == 1) | (place == GROUPS - 2)
    row, lane = iota((ROWS, LANES), 0), iota((ROWS, LANES), 1)
    folded = (lane % (2 * ROWS)) // ROWS
    side = jnp.where(low, 1, -1)
    turn = jnp.where(low, 0, ROWS - 1)
    order = turn + side * row

    def weights(is_start, block):
        at = jnp.where(is_start, 0, MARKERS) + block * ROWS
        return weight_ref[pl.ds(pl.multiple_of(at, ROWS), ROWS), :]

    picked = weights(jnp.logical_not(low), GROUPS - 1)
    column = (lane % HALF) // (2 * ROWS)
    for b in range(GROUPS - 1):
        picked = jnp.where(column == b, weights(jnp.logical_not(low), b), picked)
    picked = jnp.where(row == lane % ROWS, picked, 0.0)
    across = jnp.sum(picked, axis=0, keepdims=True) * weight_ref[2 * MARKERS : 2 * MARKERS + 1, :]
    far_end = ROWS * column + lane % ROWS

    def reaches(j):
        t = place * ROWS + turn + side * j
        return (far_end - t) * side >= 0

    near = weights(low, place)
    outermost = weights(low, jnp.where(low, 0, GROUPS - 1))
    inner = jnp.where(inward, 1.0, 0.0)
    total = jnp.zeros((ROWS, LANES), F32)

    def select(pair):
        return pair[0] if pair[0] is pair[1] else jnp.where(folded == 0, *pair)

    for subset in range(2):
        slots = SETS[subset] + [None]
        for q in range(SUBSET // ROWS):
            firsts, seconds, shared, moved = [], [], [], []
            for entry in slots[2 * q : 2 * q + 2]:
                if entry is None:
                    firsts.append(-1)
                    seconds.append(-1)
                    shared.append(near)
                    moved.append(near)
                    continue
                shape, block, j = entry
                paired = paired_with(shape, j)
                used = inner if block else 1.0 - inner
                weight = (near if shape == TRIANGLE else outermost) * used
                firsts.append(j)
                seconds.append(paired)
                shared.append(weight)
                if paired < 0:
                    moved.append(weight)
                else:
                    moved.append(jnp.where(low, pltpu.roll(weight, j + 1, 0), pltpu.roll(weight, ROWS - 1 - j, 0)))
            is_square = [entry is not None and entry[0] == SQUARE for entry in slots[2 * q : 2 * q + 2]]
            ends = [ROWS - 1 if square else j for square, j in zip(is_square, firsts)]
            a, second, end = (jnp.where(folded == 0, *pair) for pair in (firsts, seconds, ends))
            own = order <= end
            marker = jnp.where(own, a, second)
            weight = jnp.where(own, select(shared), select(moved)) * across
            at = subset * SUBSET + q * ROWS
            terms = jnp.where((marker >= 0) & reaches(marker), t_ref[at : at + ROWS, :] * weight, 0.0)
            one = jnp.sum(jnp.where(own, terms, 0.0), axis=0, keepdims=True)
            total = total + jnp.where(row == a, one, 0.0)
            if max(seconds) >= 0:
                other = jnp.sum(jnp.where(own, 0.0, terms), axis=0, keepdims=True)
                total = total + jnp.where(row == second, other, 0.0)
    doses = []
    for h in range(2):
        dose = jnp.sum(jnp.where(lane // HALF == h, total, 0.0), axis=1, keepdims=True)
        doses.append(jnp.sum(jnp.where(order == lane, dose, 0.0), axis=0, keepdims=True))
    dose_ref[...] = jnp.concatenate(doses, axis=0)[:, :ROWS]
    logs = weight_ref[2 * MARKERS + 1 : 2 * MARKERS + 2, :]
    log_ref[...] = jnp.concatenate([logs[:, :1], logs[:, HALF : HALF + 1]], axis=1)


def exchange(x, axis, by):
    peers = lax.axis_size(axis)
    return lax.ppermute(x, axis, [(i, i ^ by) for i in range(peers)])


def exchange_flat(x, by):
    peers = lax.axis_size("group") * lax.axis_size("batch")
    return lax.ppermute(x, ("group", "batch"), [(i, i ^ by) for i in range(peers)])


def is_odd(bits):
    odd = bits
    for shift in (16, 8, 4, 2, 1):
        odd = odd ^ (odd >> shift)
    return odd & 1


def on_device_windows(panel_alleles, recomb_rates, genotypes):
    width = panel_alleles.shape[1]
    copies = lax.axis_size("batch")
    chunk = width // GROUPS
    place = lax.axis_index("group")
    widths = [chunk * share // sum(SHARES) for share in SHARES]
    shapes = [
        jax.ShapeDtypeStruct((ROWS, part + (LANES if p == 0 else 0)), jnp.int32)
        for p, part in enumerate(widths)
        for d in range(GROUPS)
    ]
    *cuts, misc = pl.pallas_call(
        functools.partial(pack_kernel, widths),
        out_shape=shapes + [jax.ShapeDtypeStruct((ROWS, LANES), F32)],
        in_specs=[pl.BlockSpec(memory_space=pltpu.HBM)] * 3,
        out_specs=[VMEM] * (len(shapes) + 1),
        scratch_shapes=[
            pltpu.SMEM(genotypes.shape, jnp.int32),
            pltpu.SMEM(recomb_rates.shape, F32),
            pltpu.SemaphoreType.DMA((len(shapes) + 2,)),
        ],
        compiler_params=pltpu.CompilerParams(vmem_limit_bytes=4 * 1024 * 1024),
        name="pack",
    )(*(pltpu.with_memory_space_constraint(x, pltpu.HBM) for x in (genotypes, recomb_rates, panel_alleles)))
    arrived = None
    for p in range(len(widths)):
        part = cuts[p * GROUPS : (p + 1) * GROUPS]
        if arrived is not None:
            part[1:], arrived = lax.optimization_barrier((part[1:], arrived))
            cuts[(p - 1) * GROUPS + 1] = arrived
        part = [cut if d == 0 else exchange(cut, "group", d) for d, cut in enumerate(part)]
        cuts[p * GROUPS : (p + 1) * GROUPS] = part
        arrived = part[1]
    tags = [cut[:, widths[0] :] for cut in cuts[:GROUPS]]
    sums = []
    for p, part in enumerate(widths):
        pieces = [cut[:, :part] for cut in cuts[p * GROUPS : (p + 1) * GROUPS]]
        sums.append(
            pl.pallas_call(
                functools.partial(window_kernel, STEP, p == 0),
                out_shape=jax.ShapeDtypeStruct((2, TALL, LANES), F32),
                in_specs=[VMEM] * (2 * GROUPS + 1),
                out_specs=VMEM,
                scratch_shapes=[
                    pltpu.VMEM((MARKERS, part), jnp.int32),
                    pltpu.VMEM((MARKERS, LANES), jnp.int32),
                    pltpu.VMEM((2, 4 * MARKERS, part), BF16),
                    pltpu.VMEM((2, len(TILES) * 4 * ROWS, part), BF16),
                ],
                compiler_params=pltpu.CompilerParams(vmem_limit_bytes=40 * 1024 * 1024),
                cost_estimate=pl.CostEstimate(flops=part * 900000, bytes_accessed=0, transcendentals=0),
                name="windows",
            )(*pieces, *tags, misc)
        )
    sums = sum(sums)
    sums = sums.reshape(2, 2, SUBSET, LANES)
    half = place // (GROUPS // 2)
    carried = is_odd(place ^ lax.axis_index("batch"))

    def pick(array, index, axis):
        return lax.dynamic_index_in_dim(array, index, axis, False)

    both = pick(sums, carried, 1) + exchange(pick(sums, 1 - carried, 1), "group", 1)
    core = copies
    kept = pick(both, half, 0) + exchange_flat(pick(both, 1 - half, 0), 2 * core + core)
    bits = [1 << n for n in range(copies.bit_length() - 1)]
    for by in bits[1:] + bits[:1]:
        kept = kept + exchange_flat(kept, by + core)
    theirs = exchange(kept, "group", 1)
    weights = pl.pallas_call(
        functools.partial(solve_kernel, float(width * copies), float(copies)),
        out_shape=jax.ShapeDtypeStruct((2 * MARKERS + ROWS, LANES), F32),
        in_specs=[VMEM],
        out_specs=VMEM,
        compiler_params=pltpu.CompilerParams(vmem_limit_bytes=4 * 1024 * 1024),
        cost_estimate=pl.CostEstimate(flops=1000000, bytes_accessed=0, transcendentals=0),
        name="solve",
    )(kept)
    whole = jnp.where(carried == 0, jnp.concatenate([kept, theirs], axis=0), jnp.concatenate([theirs, kept], axis=0))
    dosage, logs = pl.pallas_call(
        contract_kernel,
        out_shape=[jax.ShapeDtypeStruct((2, ROWS), F32), jax.ShapeDtypeStruct((1, 2), F32)],
        in_specs=[VMEM] * 2,
        out_specs=[VMEM] * 2,
        compiler_params=pltpu.CompilerParams(vmem_limit_bytes=4 * 1024 * 1024),
        name="contract",
    )(weights, whole)
    return dosage, logs.reshape(2)


def fits_windows(panel_alleles, genotypes, groups, copies):
    markers, width = panel_alleles.shape
    return (
        groups == GROUPS
        and copies & (copies - 1) == 0
        and markers == ROWS
        and genotypes.shape[0] == 2
        and width % (GROUPS * sum(SHARES) * STEP) == 0
    )


def on_device(panel_alleles, recomb_rates, genotypes):
    groups, copies = lax.axis_size("group"), lax.axis_size("batch")
    if fits_windows(panel_alleles, genotypes, groups, copies):
        return on_device_windows(panel_alleles, recomb_rates, genotypes)
    return on_device_chain(panel_alleles, recomb_rates, genotypes)


def solution(mesh):
    placed = (P("group", "batch"), P("group"), P(None, "group"))
    return jax.shard_map(
        on_device, mesh=mesh, in_specs=placed, out_specs=(P(None, "group"), P()), check_vma=False
    )
```

```python
import functools
import math

import jax
import jax.numpy as jnp
from jax import lax
from jax.experimental import pallas as pl
from jax.experimental.pallas import tpu as pltpu
from jax.sharding import PartitionSpec as P

MISMATCH = 0.05
HIGHEST = lax.Precision.HIGHEST


def haplotypes(panel_rows):
    return panel_rows.shape[1] * lax.axis_size("batch")


def from_behind(x, axis, by):
    peers = lax.axis_size(axis)
    pairs = [(i, i + by) for i in range(peers) if 0 <= i + by < peers]
    return lax.ppermute(x, axis, pairs)


def emission(panel_rows, geno_col):
    observed = geno_col[:, None]
    agrees = jnp.where(panel_rows == observed, 1.0 - MISMATCH, MISMATCH)
    return jnp.where(observed == 2, 1.0, agrees).astype(jnp.float32)


def forward_terms(panel_rows, geno_col, switches):
    emitted = emission(panel_rows, geno_col)
    retain = emitted * (1.0 - switches)[:, None]
    inject = emitted * (switches / haplotypes(panel_rows))[:, None]
    return (retain, inject, None)


def backward_terms(panel_rows, geno_col, switches):
    emitted = emission(panel_rows, geno_col)[::-1]
    flipped = switches[::-1]
    retain = emitted * (1.0 - flipped)[:, None]
    inject = jnp.broadcast_to((flipped / haplotypes(panel_rows))[:, None], emitted.shape)
    return (retain, inject, emitted)


def partial_sums(entering, retain, inject, weight, extent):
    logs = jnp.cumsum(jnp.log(retain), axis=0)
    shifted = jnp.concatenate([jnp.zeros_like(entering)[None], logs[: extent - 1]], axis=0)
    before = jnp.exp(shifted)
    left_side = before if weight is None else weight * before
    leading = jnp.einsum("jk,k->j", left_side, entering, precision=HIGHEST)
    anchor = shifted[0]
    right_side = inject * jnp.exp(anchor[None] - logs)
    nearby = jnp.exp(jnp.minimum(shifted - anchor[None], 0.0))
    nearby = nearby if weight is None else weight * nearby
    columns = [jnp.einsum("jk,tk->jt", nearby, right_side, precision=HIGHEST)]
    coupling = jnp.concatenate(columns, axis=1)
    return (leading, coupling)


def solve_sums(leading, coupling):
    columns = coupling.shape[1]

    def settle(marker, sigmas):
        below = jnp.arange(columns) < marker
        update = leading[marker] + jnp.sum(
            jnp.where(below, coupling[marker] * sigmas[:columns], 0.0)
        )
        return sigmas.at[marker].set(update)

    return lax.fori_loop(0, leading.shape[0], settle, jnp.zeros_like(leading))


def advance(entering, retain, inject, sigmas, keep_states):

    def advance_single(current, pieces):
        current = pieces[0] * current + pieces[1] * pieces[2]
        return (current, current if keep_states else None)

    return lax.scan(advance_single, entering, (retain, inject, sigmas[: retain.shape[0]]))


def place_rows(store, block, active):
    return jnp.where(active, block, store)


def on_device_chain(panel_alleles, recomb_rates, genotypes):
    chain_size = lax.axis_size("group")
    position = lax.axis_index("group")
    markers, width = panel_alleles.shape
    targets = genotypes.shape[0]
    bundles = targets // targets
    uniform = jnp.full((targets, width), 1.0 / haplotypes(panel_alleles), jnp.float32)
    first_row = position == 0
    last_row = position == chain_size - 1

    def local_sums(active, arrivals, geno_rows, maker, extent):

        def local_compute():

            def local_single(pieces):
                retain, inject, weight = maker(panel_alleles, pieces[1], recomb_rates)
                return partial_sums(pieces[0], retain, inject, weight, extent)

            return lax.map(local_single, (arrivals, geno_rows))

        def local_skipped():
            return (
                jnp.zeros((targets, extent), jnp.float32),
                jnp.zeros((targets, extent, markers), jnp.float32),
            )

        return lax.cond(active, local_compute, local_skipped)

    def outgoing(active, arrivals, geno_rows, sigmas, maker, scale_row):

        def outgoing_compute():

            def outgoing_single(pieces):
                retain, inject, weight = maker(panel_alleles, pieces[1], recomb_rates)
                ending, unused = advance(pieces[0], retain, inject, pieces[2], False)
                return ending / pieces[2][scale_row]

            return lax.map(outgoing_single, (arrivals, geno_rows, sigmas))

        def outgoing_skipped():
            return jnp.zeros((targets, width), jnp.float32)

        return lax.cond(active, outgoing_compute, outgoing_skipped)

    def moment_step(moment, carried_state):
        (
            sent_forward,
            sent_backward,
            sent_running,
            store_forward,
            store_backward,
            sigma_forward,
            sigma_backward,
            log_terms,
        ) = carried_state
        got_forward = from_behind(sent_forward, "group", 1)
        got_backward = from_behind(sent_backward, "group", -1)
        entering_forward = jnp.where(first_row, uniform, got_forward)
        entering_backward = jnp.where(last_row, uniform, got_backward)
        index_forward = moment - position
        index_backward = moment - (chain_size - 1 - position)
        active_forward = (index_forward >= 0) & (index_forward < bundles)
        active_backward = (index_backward >= 0) & (index_backward < bundles)
        lead_forward, couple_forward = local_sums(
            active_forward, entering_forward, genotypes, forward_terms, markers + 1
        )
        lead_backward, couple_backward = local_sums(
            active_backward, entering_backward, genotypes, backward_terms, markers
        )
        lead_forward, couple_forward, lead_backward, couple_backward = lax.psum(
            (lead_forward, couple_forward, lead_backward, couple_backward), "batch"
        )
        sigmas_forward = jax.vmap(solve_sums)(lead_forward, couple_forward)
        sigmas_backward = jax.vmap(solve_sums)(lead_backward, couple_backward)
        next_forward = outgoing(
            active_forward, entering_forward, genotypes, sigmas_forward, forward_terms, markers
        )
        next_backward = outgoing(
            active_backward,
            entering_backward,
            genotypes,
            sigmas_backward,
            backward_terms,
            markers - 1,
        )
        guarded = jnp.where(active_forward, sigmas_forward[:, markers], 1.0)
        running = jnp.log(guarded)
        store_forward = place_rows(store_forward, entering_forward, active_forward)
        store_backward = place_rows(store_backward, entering_backward, active_backward)
        sigma_forward = place_rows(sigma_forward, sigmas_forward, active_forward)
        sigma_backward = place_rows(sigma_backward, sigmas_backward, active_backward)
        log_terms = place_rows(log_terms, running, active_forward)
        return (
            next_forward,
            next_backward,
            running,
            store_forward,
            store_backward,
            sigma_forward,
            sigma_backward,
            log_terms,
        )

    initial = (
        jnp.zeros((targets, width), jnp.float32),
        jnp.zeros((targets, width), jnp.float32),
        jnp.zeros((targets,), jnp.float32),
        jnp.zeros((targets, width), jnp.float32),
        jnp.zeros((targets, width), jnp.float32),
        jnp.zeros((targets, markers + 1), jnp.float32),
        jnp.zeros((targets, markers), jnp.float32),
        jnp.zeros((targets,), jnp.float32),
    )
    final_state = lax.fori_loop(0, chain_size + bundles - 1, moment_step, initial)
    store_forward, store_backward, sigma_forward, sigma_backward, log_terms = final_state[3:]
    whole_log = lax.psum(log_terms, "group")
    log_likelihood = whole_log / (markers * chain_size)

    def posterior(pieces):
        entering_ahead, entering_behind, geno_col, sigmas_ahead, sigmas_behind = pieces
        retain, inject, weight = forward_terms(panel_alleles, geno_col, recomb_rates)
        unused_f, forward_states = advance(entering_ahead, retain, inject, sigmas_ahead, True)
        forward_rows = forward_states / sigmas_ahead[1:, None]
        retain, inject, weight = backward_terms(panel_alleles, geno_col, recomb_rates)
        unused_b, backward_states = advance(entering_behind, retain, inject, sigmas_behind, True)
        scaled_back = backward_states[:-1] / sigmas_behind[:-1, None]
        backward_rows = jnp.concatenate([entering_behind[None], scaled_back], axis=0)[::-1]
        product = forward_rows * backward_rows
        numerator = jnp.sum(jnp.where(panel_alleles == 1, product, 0.0), axis=1)
        return (numerator, jnp.sum(product, axis=1))

    numerator, denominator = lax.map(
        posterior, (store_forward, store_backward, genotypes, sigma_forward, sigma_backward)
    )
    numerator, denominator = lax.psum((numerator, denominator), "batch")
    return (numerator / denominator, log_likelihood)


ROWS, LANES = 8, 128
HALF = LANES // 2
GROUPS = 4
SHARES = (9, 7)
STEP = 2 * LANES
MISSING = 2
SCALE = math.sqrt(MISMATCH * (1.0 - MISMATCH))
HALF_STEP = 0.5 * math.log((1.0 - MISMATCH) / MISMATCH)
VMEM = pl.BlockSpec(memory_space=pltpu.VMEM)
F32, BF16 = jnp.float32, jnp.bfloat16


def iota(shape, axis):
    return lax.broadcasted_iota(jnp.int32, shape, axis)


MARKERS = ROWS * GROUPS
SUBSET = 5 * ROWS
TALL = 2 * SUBSET
TRIANGLE, SQUARE = 0, 1
SETS = [
    [(TRIANGLE, 0, 0), (TRIANGLE, 0, 1), (TRIANGLE, 0, 3)]
    + [(TRIANGLE, 1, a) for a in (0, 1, 2, 7)]
    + [(SQUARE, 1, j) for j in (0, 1)],
    [(TRIANGLE, 0, 2), (TRIANGLE, 0, 7), (TRIANGLE, 1, 3)] + [(SQUARE, 1, j) for j in range(2, ROWS)],
]
TILES = SETS[0] + SETS[1]
TUCKED = [(1, 1), (1, 2), (1, 3), (2, 2), (2, 3), (3, 3)]
FIRST_TUCKED = 3
SPARE = 2


def paired_with(shape, a):
    return ROWS - 2 - a if shape == TRIANGLE and a < 3 else -1


def pack_kernel(widths, geno_ref, rate_ref, panel_ref, *refs):
    outs, (misc_ref, genos, rates_in, sems) = refs[:-4], refs[-4:]
    place = lax.axis_index("group")
    chunk = panel_ref.shape[1] // GROUPS
    copies = []
    for n, ref in enumerate(outs):
        d, p = n % GROUPS, n // GROUPS
        part = widths[p]
        start = pl.multiple_of((place ^ d) * chunk + sum(widths[:p]), LANES)
        copies.append(
            pltpu.make_async_copy(panel_ref.at[:, pl.ds(start, part)], ref.at[:, pl.ds(0, part)], sems.at[n])
        )
    small = [
        pltpu.make_async_copy(geno_ref, genos, sems.at[len(outs)]),
        pltpu.make_async_copy(rate_ref, rates_in, sems.at[len(outs) + 1]),
    ]
    for copy in small + copies:
        copy.start()
    for copy in small:
        copy.wait()
    row, lane = iota((ROWS, LANES), 0), iota((ROWS, LANES), 1)
    tile = jnp.zeros((ROWS, LANES), jnp.int32)
    misc = jnp.zeros((ROWS, LANES), F32)
    for i in range(ROWS):
        tile = jnp.where(row == i, jnp.where(lane < HALF, genos[0, i], genos[1, i]), tile)
        misc = jnp.where(lane == i, rates_in[i], misc)
        for h in range(2):
            known = jnp.where(genos[h, i] == MISSING, 0.0, 1.0)
            misc = jnp.where(lane == 2 * ROWS * (h + 1) + i, known, misc)
    for ref in outs[:GROUPS]:
        ref[:, widths[0] :] = tile
    misc_ref[...] = jnp.where((row == GROUPS + place) | (row == GROUPS - 1 - place), misc, 0.0)
    for copy in copies:
        copy.wait()


def window_kernel(step, has_misc, *refs):
    pieces, geno_refs = refs[:GROUPS], refs[GROUPS : 2 * GROUPS]
    misc_ref, t_ref, panel, genos, wide, left = refs[2 * GROUPS :]
    place = lax.axis_index("group")
    columns = panel.shape[1]
    for d in range(GROUPS):
        rows = pl.ds(pl.multiple_of((place ^ d) * ROWS, ROWS), ROWS)
        panel[rows, :] = pieces[d][...]
        genos[rows, :] = geno_refs[d][...]

    r, j = iota((4 * MARKERS, 2 * MARKERS), 0), iota((4 * MARKERS, 2 * MARKERS), 1)
    same = r // (2 * MARKERS) == j // MARKERS
    prefix, marker = (r // MARKERS) % 2 == 0, r % MARKERS
    at = j % MARKERS
    sums = jnp.where(prefix, jnp.where(at <= marker, 1.0, 0.0), jnp.where(at < marker, -1.0, 0.0))
    sums = jnp.where(same, sums, 0.0).astype(BF16)

    for start in range(0, columns, step):
        here = slice(start, start + step)
        signs = []
        for h in range(2):
            for b in range(GROUPS):
                rows = slice(b * ROWS, (b + 1) * ROWS)
                seen = genos[rows, h * HALF : h * HALF + 1]
                agrees = jnp.where(panel[rows, here] == seen, 1.0, -1.0)
                signs.append(jnp.where(seen == MISSING, 0.0, agrees))
        signs = jnp.concatenate(signs, axis=0).astype(BF16)
        power = jnp.dot(sums, signs, preferred_element_type=F32)
        value = jnp.exp(power * HALF_STEP)
        upper = value.astype(BF16).astype(F32)
        lower = value - upper
        blocks = {}
        for h in range(2):
            for kind in range(2):
                for b in range(GROUPS):
                    at = h * 2 * MARKERS + kind * MARKERS + b * ROWS
                    both = jnp.concatenate([upper[at : at + ROWS], lower[at : at + ROWS]], axis=0).astype(BF16)
                    blocks[kind, h, b] = both
                    wide[kind, (h * GROUPS + b) * 2 * ROWS : (h * GROUPS + b + 1) * 2 * ROWS, here] = both
        row = iota((ROWS, step), 0)
        for half in range(2):
            for slot, (shape, block, j) in enumerate(TILES):
                paired = paired_with(shape, j)
                outer = 0 if half == 0 else GROUPS - 1
                own = abs(outer - block)
                near = own if shape == TRIANGLE else outer
                first = row <= j if half == 0 else row >= ROWS - 1 - j

                def carries(j):
                    t = own * ROWS + (j if half == 0 else ROWS - 1 - j)
                    return jnp.broadcast_to(panel[t : t + 1, here], (ROWS, step)).astype(F32)

                mask = carries(j) if paired < 0 else jnp.where(first, carries(j), carries(paired))
                mask = jnp.concatenate([mask, mask], axis=0).astype(BF16)
                for h in range(2):
                    base = blocks[1 - half, h, near]
                    if paired >= 0:
                        at = h * 2 * MARKERS + (1 - half) * MARKERS + near * ROWS
                        shift = j + 1 if half == 0 else ROWS - 1 - j
                        both = [x[at : at + ROWS] for x in (upper, lower)]
                        both = [jnp.where(first, x, pltpu.roll(x, shift, 0)) for x in both]
                        base = jnp.concatenate(both, axis=0).astype(BF16)
                    at = (slot * 2 + h) * 2 * ROWS
                    left[half, at : at + 2 * ROWS, here] = base * mask

    def product(a, b):
        return lax.dot_general(a, b, (((1,), (1,)), ((), ())), preferred_element_type=F32)

    lane = iota((ROWS, LANES), 1)
    first = lane % (2 * ROWS) < ROWS

    def rows_of(acc, slot):
        return acc[slot * 2 * ROWS : slot * 2 * ROWS + ROWS] + acc[slot * 2 * ROWS + ROWS : (slot + 1) * 2 * ROWS]

    def fold(a, b):
        return jnp.where(first, a + pltpu.roll(a, LANES - ROWS, 1), b + pltpu.roll(b, ROWS, 1))

    def both_targets(acc, slots):
        return jnp.where(lane < HALF, rows_of(acc, slots[0]), rows_of(acc, slots[1]))

    def unfold(tile, column, to_column, odd):
        shift = 2 * ROWS * (to_column - column) + ROWS * odd
        tile = tile + pltpu.roll(tile, LANES - ROWS, 1)
        return tile if shift == 0 else pltpu.roll(tile, shift % LANES, 1)

    row = iota((ROWS, LANES), 0)
    misc = misc_ref[...] if has_misc else jnp.zeros((ROWS, LANES), F32)
    sums_e = product(wide[1], wide[0])
    plain = [both_targets(sums_e, [b, GROUPS + b]) for b in range(GROUPS)]
    column = (lane % HALF) // (2 * ROWS)
    for half in range(2):
        outer = 0 if half == 0 else GROUPS - 1
        sums_t = product(left[half], wide[half])
        tucked = {}
        for n, (b, to) in enumerate(TUCKED):
            slot = FIRST_TUCKED + n
            moved = unfold(plain[b], to, outer, slot % 2)
            here = (column == outer) & (first if slot % 2 == 0 else jnp.logical_not(first))
            tucked.setdefault(slot // 2, []).append((here, moved))
        for subset in range(2):
            base = subset * len(SETS[0])
            tiles = [both_targets(sums_t, [2 * n, 2 * n + 1]) for n in range(base, base + len(SETS[subset]))] + [plain[0]]
            for q in range(SUBSET // ROWS):
                value = fold(tiles[2 * q], tiles[2 * q + 1])
                for here, moved in tucked.get(q, []):
                    value = jnp.where(here, moved, value)
                if q == SPARE // 2:
                    spare = row >= GROUPS if half == 0 else row < GROUPS
                    value = jnp.where(spare & first, misc, value)
                at = subset * SUBSET + q * ROWS
                t_ref[half, at : at + ROWS, :] = value


def solve_kernel(panel_size, copies, sum_ref, ends_ref):
    low = lax.axis_index("group") < GROUPS // 2
    row, lane = iota((ROWS, LANES), 0), iota((ROWS, LANES), 1)
    target = lane // HALF
    folded = (lane % (2 * ROWS)) // ROWS
    column_of = (lane % HALF) // (2 * ROWS)
    misc = sum_ref[SPARE // 2 * ROWS : (SPARE // 2 + 1) * ROWS, :]

    def spread(tile, at):
        return jnp.broadcast_to(tile[:, at : at + 1], (ROWS, LANES))

    def drawn(slot, to, odd):
        tile = sum_ref[slot // 2 * ROWS : (slot // 2 + 1) * ROWS, :]
        shifts = [2 * ROWS * (to - outer) + ROWS * (odd - slot % 2) for outer in (0, GROUPS - 1)]
        return jnp.where(low, *(pltpu.roll(tile, shift % LANES, 1) if shift else tile for shift in shifts))

    last = sum_ref[SUBSET - ROWS :, :]
    pair = [jnp.where(folded == 0, pltpu.roll(last, LANES - ROWS, 1), 0.0), jnp.zeros((ROWS, LANES), F32)]
    for n, (b, to) in enumerate(TUCKED):
        here = (column_of == to) & (folded == b % 2)
        pair[b // 2] = jnp.where(here, drawn(FIRST_TUCKED + n, to, b % 2), pair[b // 2])
    square = jnp.concatenate(pair + [misc, jnp.zeros((LANES - 3 * ROWS, LANES), F32)], axis=0)
    turned = jnp.transpose(square)

    listed = turned[:ROWS] * (1.0 / copies)
    spare = GROUPS * ROWS // 2
    rates = [jnp.where(low, spread(listed, spare + GROUPS + b), spread(listed, spare + GROUPS - 1 - b)) for b in range(GROUPS)]
    odds = [rate / (1.0 - rate) for rate in rates]
    inverse = 1.0 / panel_size
    ahead = []
    for b in range(GROUPS):
        following = odds[b + 1][0:1, :] if b + 1 < GROUPS else jnp.ones((1, LANES), F32)
        ahead.append(jnp.concatenate([odds[b][1:, :], following], axis=0) * inverse)
    behind = [odd * inverse for odd in odds]

    trail_tiles = []
    for q in range(GROUPS // 2):
        factor = jnp.where(folded == 0, behind[2 * q], behind[2 * q + 1])
        trail_tiles.append(pair[q] * factor)

    def turned_tile(h, b, f):
        at = h * HALF + b * 2 * ROWS + f * ROWS
        return turned[at : at + ROWS] * ahead[b]

    lead_tiles = {(h, b, f): turned_tile(h, b, f) for h in range(2) for b in range(GROUPS) for f in range(2)}

    def lead_column(t, b):
        s, at = t // ROWS, (t // ROWS // 2) * ROWS + t % ROWS
        return jnp.where(target == 0, spread(lead_tiles[0, b, s % 2], at), spread(lead_tiles[1, b, s % 2], at))

    def trail_column(t, b):
        at = 2 * ROWS * (t // ROWS) + t % ROWS + ROWS * (b % 2)
        tile = trail_tiles[b // 2]
        return jnp.where(target == 0, spread(tile, at), spread(tile, HALF + at))

    zero = jnp.zeros((ROWS, LANES), F32)
    lead, trail, starts, ends = [zero] * GROUPS, [zero] * GROUPS, [zero] * GROUPS, [zero] * GROUPS
    v = jnp.ones((ROWS, LANES), F32)
    z = jnp.ones((ROWS, LANES), F32)
    for t in range(MARKERS):
        u = MARKERS - 1 - t
        bt, bu = t // ROWS, u // ROWS
        starts[bt] = jnp.where(row == t % ROWS, v, starts[bt])
        ends[bu] = jnp.where(row == u % ROWS, z, ends[bu])
        for b in range(bt, GROUPS):
            lead[b] = lead[b] + v * lead_column(t, b)
        for b in range(bu + 1):
            trail[b] = trail[b] + z * trail_column(u, b)
        v = jnp.broadcast_to(lead[bt][t % ROWS : t % ROWS + 1, :], (ROWS, LANES))
        z = jnp.broadcast_to(trail[bu][u % ROWS : u % ROWS + 1, :], (ROWS, LANES))
    for b in range(GROUPS):
        ends_ref[b * ROWS : (b + 1) * ROWS, :] = starts[b]
        ends_ref[MARKERS + b * ROWS : MARKERS + (b + 1) * ROWS, :] = ends[b]

    stay = [jnp.log(1.0 - rate) for rate in rates]
    stay[0] = jnp.where(row == 0, 0.0, stay[0])
    stay = jnp.sum(sum(stay), axis=0, keepdims=True)
    marked = jnp.where(low, row, ROWS - 1 - row) >= GROUPS
    logs = []
    for h in range(2):
        cell = marked & (lane >= 2 * ROWS * (h + 1)) & (lane < 2 * ROWS * (h + 1) + ROWS)
        seen = jnp.sum(jnp.where(cell, misc, 0.0), axis=0, keepdims=True)
        seen = jnp.sum(seen, axis=1, keepdims=True) * (1.0 / copies)
        whole = jnp.log(v[0:1, h * HALF : h * HALF + 1]) + stay[:, 0:1] + seen * math.log(SCALE)
        logs.append(whole * (1.0 / MARKERS))
    ends_ref[2 * MARKERS :, :] = jnp.where(row == 0, inverse / v, jnp.where(target == 0, *logs))


def contract_kernel(weight_ref, t_ref, dose_ref, log_ref):
    place = lax.axis_index("group")
    low = place < GROUPS // 2
    inward = (place == 1) | (place == GROUPS - 2)
    row, lane = iota((ROWS, LANES), 0), iota((ROWS, LANES), 1)
    folded = (lane % (2 * ROWS)) // ROWS
    side = jnp.where(low, 1, -1)
    turn = jnp.where(low, 0, ROWS - 1)
    order = turn + side * row

    def weights(is_start, block):
        at = jnp.where(is_start, 0, MARKERS) + block * ROWS
        return weight_ref[pl.ds(pl.multiple_of(at, ROWS), ROWS), :]

    picked = weights(jnp.logical_not(low), GROUPS - 1)
    column = (lane % HALF) // (2 * ROWS)
    for b in range(GROUPS - 1):
        picked = jnp.where(column == b, weights(jnp.logical_not(low), b), picked)
    picked = jnp.where(row == lane % ROWS, picked, 0.0)
    across = jnp.sum(picked, axis=0, keepdims=True) * weight_ref[2 * MARKERS : 2 * MARKERS + 1, :]
    far_end = ROWS * column + lane % ROWS

    def reaches(j):
        t = place * ROWS + turn + side * j
        return (far_end - t) * side >= 0

    near = weights(low, place)
    outermost = weights(low, jnp.where(low, 0, GROUPS - 1))
    inner = jnp.where(inward, 1.0, 0.0)
    total = jnp.zeros((ROWS, LANES), F32)

    def select(pair):
        return pair[0] if pair[0] is pair[1] else jnp.where(folded == 0, *pair)

    for subset in range(2):
        slots = SETS[subset] + [None]
        for q in range(SUBSET // ROWS):
            firsts, seconds, shared, moved = [], [], [], []
            for entry in slots[2 * q : 2 * q + 2]:
                if entry is None:
                    firsts.append(-1)
                    seconds.append(-1)
                    shared.append(near)
                    moved.append(near)
                    continue
                shape, block, j = entry
                paired = paired_with(shape, j)
                used = inner if block else 1.0 - inner
                weight = (near if shape == TRIANGLE else outermost) * used
                firsts.append(j)
                seconds.append(paired)
                shared.append(weight)
                if paired < 0:
                    moved.append(weight)
                else:
                    moved.append(jnp.where(low, pltpu.roll(weight, j + 1, 0), pltpu.roll(weight, ROWS - 1 - j, 0)))
            is_square = [entry is not None and entry[0] == SQUARE for entry in slots[2 * q : 2 * q + 2]]
            ends = [ROWS - 1 if square else j for square, j in zip(is_square, firsts)]
            a, second, end = (jnp.where(folded == 0, *pair) for pair in (firsts, seconds, ends))
            own = order <= end
            marker = jnp.where(own, a, second)
            weight = jnp.where(own, select(shared), select(moved)) * across
            at = subset * SUBSET + q * ROWS
            terms = jnp.where((marker >= 0) & reaches(marker), t_ref[at : at + ROWS, :] * weight, 0.0)
            one = jnp.sum(jnp.where(own, terms, 0.0), axis=0, keepdims=True)
            total = total + jnp.where(row == a, one, 0.0)
            if max(seconds) >= 0:
                other = jnp.sum(jnp.where(own, 0.0, terms), axis=0, keepdims=True)
                total = total + jnp.where(row == second, other, 0.0)
    doses = []
    for h in range(2):
        dose = jnp.sum(jnp.where(lane // HALF == h, total, 0.0), axis=1, keepdims=True)
        doses.append(jnp.sum(jnp.where(order == lane, dose, 0.0), axis=0, keepdims=True))
    dose_ref[...] = jnp.concatenate(doses, axis=0)[:, :ROWS]
    logs = weight_ref[2 * MARKERS + 1 : 2 * MARKERS + 2, :]
    log_ref[...] = jnp.concatenate([logs[:, :1], logs[:, HALF : HALF + 1]], axis=1)


def exchange(x, axis, by):
    peers = lax.axis_size(axis)
    return lax.ppermute(x, axis, [(i, i ^ by) for i in range(peers)])


def exchange_flat(x, by):
    peers = lax.axis_size("group") * lax.axis_size("batch")
    return lax.ppermute(x, ("group", "batch"), [(i, i ^ by) for i in range(peers)])


def is_odd(bits):
    odd = bits
    for shift in (16, 8, 4, 2, 1):
        odd = odd ^ (odd >> shift)
    return odd & 1


def on_device_windows(panel_alleles, recomb_rates, genotypes):
    width = panel_alleles.shape[1]
    copies = lax.axis_size("batch")
    chunk = width // GROUPS
    place = lax.axis_index("group")
    widths = [chunk * share // sum(SHARES) for share in SHARES]
    shapes = [
        jax.ShapeDtypeStruct((ROWS, part + (LANES if p == 0 else 0)), jnp.int32)
        for p, part in enumerate(widths)
        for d in range(GROUPS)
    ]
    *cuts, misc = pl.pallas_call(
        functools.partial(pack_kernel, widths),
        out_shape=shapes + [jax.ShapeDtypeStruct((ROWS, LANES), F32)],
        in_specs=[pl.BlockSpec(memory_space=pltpu.HBM)] * 3,
        out_specs=[VMEM] * (len(shapes) + 1),
        scratch_shapes=[
            pltpu.SMEM(genotypes.shape, jnp.int32),
            pltpu.SMEM(recomb_rates.shape, F32),
            pltpu.SemaphoreType.DMA((len(shapes) + 2,)),
        ],
        compiler_params=pltpu.CompilerParams(vmem_limit_bytes=4 * 1024 * 1024),
        name="pack",
    )(*(pltpu.with_memory_space_constraint(x, pltpu.HBM) for x in (genotypes, recomb_rates, panel_alleles)))
    arrived = None
    for p in range(len(widths)):
        part = cuts[p * GROUPS : (p + 1) * GROUPS]
        if arrived is not None:
            part[1:], arrived = lax.optimization_barrier((part[1:], arrived))
            cuts[(p - 1) * GROUPS + 1] = arrived
        part = [cut if d == 0 else exchange(cut, "group", d) for d, cut in enumerate(part)]
        cuts[p * GROUPS : (p + 1) * GROUPS] = part
        arrived = part[1]
    tags = [cut[:, widths[0] :] for cut in cuts[:GROUPS]]
    sums = []
    for p, part in enumerate(widths):
        pieces = [cut[:, :part] for cut in cuts[p * GROUPS : (p + 1) * GROUPS]]
        sums.append(
            pl.pallas_call(
                functools.partial(window_kernel, part, p == 0),
                out_shape=jax.ShapeDtypeStruct((2, TALL, LANES), F32),
                in_specs=[VMEM] * (2 * GROUPS + 1),
                out_specs=VMEM,
                scratch_shapes=[
                    pltpu.VMEM((MARKERS, part), jnp.int32),
                    pltpu.VMEM((MARKERS, LANES), jnp.int32),
                    pltpu.VMEM((2, 4 * MARKERS, part), BF16),
                    pltpu.VMEM((2, len(TILES) * 4 * ROWS, part), BF16),
                ],
                compiler_params=pltpu.CompilerParams(vmem_limit_bytes=40 * 1024 * 1024),
                cost_estimate=pl.CostEstimate(flops=part * 900000, bytes_accessed=0, transcendentals=0),
                name="windows",
            )(*pieces, *tags, misc)
        )
    sums = sum(sums)
    sums = sums.reshape(2, 2, SUBSET, LANES)
    half = place // (GROUPS // 2)
    carried = is_odd(place ^ lax.axis_index("batch"))

    def pick(array, index, axis):
        return lax.dynamic_index_in_dim(array, index, axis, False)

    both = pick(sums, carried, 1) + exchange(pick(sums, 1 - carried, 1), "group", 1)
    core = copies
    kept = pick(both, half, 0) + exchange_flat(pick(both, 1 - half, 0), 2 * core + core)
    by = 1
    while by < copies:
        kept = kept + exchange_flat(kept, by + core)
        by *= 2
    theirs = exchange(kept, "group", 1)
    weights = pl.pallas_call(
        functools.partial(solve_kernel, float(width * copies), float(copies)),
        out_shape=jax.ShapeDtypeStruct((2 * MARKERS + ROWS, LANES), F32),
        in_specs=[VMEM],
        out_specs=VMEM,
        compiler_params=pltpu.CompilerParams(vmem_limit_bytes=4 * 1024 * 1024),
        cost_estimate=pl.CostEstimate(flops=1000000, bytes_accessed=0, transcendentals=0),
        name="solve",
    )(kept)
    whole = jnp.where(carried == 0, jnp.concatenate([kept, theirs], axis=0), jnp.concatenate([theirs, kept], axis=0))
    dosage, logs = pl.pallas_call(
        contract_kernel,
        out_shape=[jax.ShapeDtypeStruct((2, ROWS), F32), jax.ShapeDtypeStruct((1, 2), F32)],
        in_specs=[VMEM] * 2,
        out_specs=[VMEM] * 2,
        compiler_params=pltpu.CompilerParams(vmem_limit_bytes=4 * 1024 * 1024),
        name="contract",
    )(weights, whole)
    return dosage, logs.reshape(2)


def fits_windows(panel_alleles, genotypes, groups, copies):
    markers, width = panel_alleles.shape
    return (
        groups == GROUPS
        and copies & (copies - 1) == 0
        and markers == ROWS
        and genotypes.shape[0] == 2
        and width % (GROUPS * sum(SHARES) * STEP) == 0
    )


def on_device(panel_alleles, recomb_rates, genotypes):
    groups, copies = lax.axis_size("group"), lax.axis_size("batch")
    if fits_windows(panel_alleles, genotypes, groups, copies):
        return on_device_windows(panel_alleles, recomb_rates, genotypes)
    return on_device_chain(panel_alleles, recomb_rates, genotypes)


def solution(mesh):
    placed = (P("group", "batch"), P("group"), P(None, "group"))
    return jax.shard_map(
        on_device, mesh=mesh, in_specs=placed, out_specs=(P(None, "group"), P()), check_vma=False
    )
```
